32 devices in a mesh: energy: 16 (over z, x, core), slab: 2 (over y).
Axes of the slice: x: 2, y: 2, z: 4, core: 2. Of those that a mesh axis runs over, the one named last changes fastest.
Arguments:
- green_blocks: bfloat16 [2, 12, 12, 256, 128], P(None, None, None, 'energy', 'slab'), may hold values from -6 to 6
- couplings: bfloat16 [12, 12, 2, 1024], P(None, None, 'slab', 'energy'), may hold values from -1.75 to 1.75
- band_weights: float32 [9, 2, 1024], P(None, 'slab', 'energy'), may hold values from 0.02 to 0.2
- neighbours: int32 [2, 1024], P('slab', 'energy'), may hold values from 0 to 127, as said below
- shifts: int32 [2, 1024], P('slab', 'energy'), may hold values from -32 to 32
Outputs:
- self_energy: bfloat16 [2, 12, 12, 256, 128], P(None, None, None, 'energy', 'slab')
The draws below stay inside these ranges and needn't reach their ends.
Inputs may be any that keep to these rules, and one draw needn't show every extreme that they name: `neighbours`: the partner of each coupling of atom a lies within 4 atoms of a; partners of one atom may repeat.
All inputs are finite; a program needn't handle non-finite values.
Results may differ from the reference program's by a relative error of at most 0.0057.
Values may be sent and summed in bfloat16 or wider, within the bound.
A program may use at most 128 MiB of HBM per device.

```python
import math
import jax
import jax.numpy as jnp
from jax import lax

ORB = 12
ENERGIES = 256
NBR = 16
BAND = 9
SHIFT = 32
HALO = 4
SLABS = 2
ATOMS = 128
PAIRS_SLAB = 1024


def draw_neighbours(key, part):
    pair_index = jnp.arange(SLABS * PAIRS_SLAB, dtype=jnp.int32)
    atom_index = pair_index // NBR
    slot_index = pair_index % NBR
    offset = jax.random.randint(key, (SLABS * PAIRS_SLAB,), -HALO, HALO + 1, dtype=jnp.int32)
    offset = jnp.where(slot_index == 0, 0, jnp.where(slot_index == 1, -HALO, jnp.where(slot_index == 2, HALO, offset)))
    partner = atom_index + offset
    partner = jnp.where(partner < 0, -partner, partner)
    partner = jnp.where(partner > ATOMS - 1, 2 * (ATOMS - 1) - partner, partner)
    return partner.astype(jnp.int32).reshape(SLABS, PAIRS_SLAB)


def with_ends(values, key, low, high):
    longest = values.shape.index(max(values.shape))
    spots = []
    for shift in (0, 1):
        where = [jax.random.randint(jax.random.fold_in(key, axis), (), 0, length) for axis, length in enumerate(values.shape)]
        where[longest] = (where[longest] + shift) % values.shape[longest]
        spots.append(tuple(where))
    return values.at[spots[0]].set(low).at[spots[1]].set(high)


def steps_of(stream_key, extent, shards, low, largest):
    factor_of = 1.0
    for axis_at, shards_of in shards:
        steps = jax.random.uniform(jax.random.fold_in(jax.random.fold_in(stream_key, 6), axis_at), (shards_of,), jnp.float32, low / len(shards), largest / len(shards))
        factor_of = factor_of * jnp.repeat(jnp.exp(steps), extent[axis_at] // shards_of).reshape((-1,) + (1,) * (len(extent) - 1 - axis_at))
    return factor_of


def gaussian(key, dims, scale, bound, shards=(), kind=jnp.bfloat16):
    array = scale * jax.random.normal(key, dims, jnp.float32)
    if shards:
        array = array * steps_of(key, dims, shards, -0.22, 0.18)
    return jnp.clip(array, -bound, bound).astype(kind)


def setup_inputs(seed: int = 0) -> dict:
    keys = jax.random.split(jax.random.key(seed), 6)
    green_blocks = gaussian(keys[0], (2, ORB, ORB, ENERGIES, ATOMS), 1.0, 6.0, ((3, 16), (4, 2)))
    couplings = gaussian(keys[1], (ORB, ORB, SLABS, PAIRS_SLAB), ORB ** -0.5, 1.75, ((2, 2), (3, 16)))
    band_weights = jnp.clip(jnp.exp(math.log(0.2) - 2.3025851 * jax.random.uniform(keys[2], (BAND, SLABS, PAIRS_SLAB), jnp.float32) ** steps_of(keys[2], (BAND, SLABS, PAIRS_SLAB), ((1, 2), (2, 16)), -0.2, 0.2)), 0.02, 0.2)
    neighbours = draw_neighbours(jax.random.fold_in(keys[5], 71), 0)
    shifts = with_ends(jax.random.randint(keys[4], (SLABS, PAIRS_SLAB), 0 - SHIFT, SHIFT + 1), jax.random.fold_in(keys[4], 1), 0 - SHIFT, SHIFT).astype(jnp.int32)
    return dict(green_blocks=green_blocks, couplings=couplings, band_weights=band_weights, neighbours=neighbours, shifts=shifts)


def reference(green_blocks, couplings, band_weights, neighbours, shifts):
    atom_major_in = jnp.transpose(green_blocks, (0, 1, 2, 4, 3))
    atom_count = atom_major_in.shape[3]
    energy_count = atom_major_in.shape[4]
    pad_width = SHIFT + BAND // 2
    padded = jnp.pad(atom_major_in, ((0, 0), (0, 0), (0, 0), (0, 0), (pad_width, pad_width)))
    partner_rows = neighbours.reshape(atom_count, NBR).astype(jnp.int32)
    starts = (shifts.reshape(atom_count, NBR) + pad_width - BAND // 2).astype(jnp.int32)
    band_w = band_weights.reshape(BAND, atom_count, NBR).transpose(1, 2, 0)
    coupling = couplings.reshape(ORB, ORB, atom_count, NBR).transpose(2, 0, 1, 3)
    anchor = jnp.zeros((), jnp.int32)

    def window_of(row, start):
        piece = lax.dynamic_slice(padded, (anchor, anchor, anchor, row, start), (2, ORB, ORB, 1, energy_count + BAND - 1))
        return piece[:, :, :, 0, :]

    def one_atom(per_atom):
        rows_here, starts_here, weight_here, matrix = per_atom
        windows = jax.vmap(window_of, out_axes=3)(rows_here, starts_here)
        summed = jnp.zeros((2, ORB, ORB, NBR, energy_count), jnp.float32)
        for offset in range(BAND):
            summed = summed + weight_here[:, offset][:, None] * windows[..., offset:offset + energy_count].astype(jnp.float32)
        banded = summed.astype(jnp.bfloat16)
        matrix_f = matrix.astype(jnp.float32)
        left_product = jnp.einsum('pqk,cqrkE->cprkE', matrix_f, banded.astype(jnp.float32)).astype(jnp.bfloat16)
        result = jnp.einsum('cprkE,srk->cpsE', left_product.astype(jnp.float32), matrix_f)
        return result.astype(jnp.bfloat16)

    stacked = lax.map(one_atom, (partner_rows, starts, band_w, coupling), batch_size=8)
    return jnp.transpose(stacked, (1, 2, 3, 4, 0))
```

```python
import functools

import jax
import jax.numpy as jnp
from jax import lax
from jax.experimental import pallas as pl
from jax.experimental.pallas import tpu as pltpu
from jax.sharding import PartitionSpec as P

ORB = 12
NBR = 16
BAND = 9
SHIFT = 32
HALO = 4
BLOCK = 2 * ORB * ORB
PAIR = ORB * ORB
REACH = SHIFT + BAND // 2
SPAN = 64
WINDOW = 128

MESH = pl.DeviceIdType.MESH
NT = (((1,), (1,)), ((), ()))


def order(groups, per_dev):
    count = groups * per_dev
    row = lax.broadcasted_iota(jnp.int32, (count, count), 0)
    atom = lax.broadcasted_iota(jnp.int32, (count, count), 1)
    return (atom == (row % groups) * per_dev + row // groups).astype(jnp.bfloat16)


def eye(count):
    row = lax.broadcasted_iota(jnp.int32, (count, count), 0)
    column = lax.broadcasted_iota(jnp.int32, (count, count), 1)
    return (row == column).astype(jnp.bfloat16)


def partner_of(i, step):
    out, bit = 0, 1
    while bit <= step:
        out = out + bit * lax.rem(lax.div(i, bit) + step // bit, 2)
        bit *= 2
    return lax.div(i, bit) * bit + out if step else i


def pack_kernel(groups, per_dev, x_ref, sent, wide, packed):
    local_e = sent.shape[1]
    tiles = wide.shape[0]
    count = x_ref.shape[1]
    lanes = min(count, 128)
    if lanes < 128:
        wide[...] = jnp.zeros_like(wide)
    for j in range(tiles):
        wide[j, :x_ref.shape[0], :lanes] = x_ref[:, j * 128:j * 128 + lanes].astype(jnp.float32)
    pick = order(groups, per_dev)
    for e in range(local_e):
        rows = jnp.concatenate([wide[j, pl.ds(e, BLOCK, stride=local_e), :] for j in range(tiles)], axis=1)
        rows = rows[:, :count].astype(jnp.bfloat16)
        turned = lax.dot_general(pick, rows, NT, preferred_element_type=jnp.float32)
        flat = jnp.concatenate([turned[i * groups:(i + 1) * groups] for i in range(per_dev)], axis=1)
        for j in range(packed.shape[0]):
            packed[j, pl.ds(e, groups, stride=local_e), :] = flat[:, j * 128:(j + 1) * 128]
    for g in range(groups):
        for j in range(packed.shape[0]):
            sent[g, :, j * 128:(j + 1) * 128] = packed[j, g * local_e:(g + 1) * local_e, :].astype(jnp.bfloat16)


def gather_kernel(inner, layers, side, sent, mats_in, weights_in, ints_in, landed, mats, weights, ints,
                  main_send, main_recv, relay_send, relay_recv, table_send, table_recv):
    me, slab = lax.axis_index("energy"), lax.axis_index("slab")
    slabs = lax.axis_size("slab")
    layer, i = lax.div(me, inner), lax.rem(me, inner)
    chunks = sent.shape[0]
    mine = chunks // inner
    slots = mine + 2
    barrier = pltpu.get_barrier_semaphore()
    first, last = i == 0, i == inner - 1
    below, above = layer > 0, layer < layers - 1
    slab_below, slab_above = slab > 0, slab < slabs - 1
    owner, spot = lax.div(me, layers), lax.rem(me, layers)

    def hail(device, row):
        pl.semaphore_signal(barrier, inc=1, device_id=(device, row), device_id_type=MESH)

    for step in range(1, inner):
        hail(layer * inner + partner_of(i, step), slab)

    @pl.when(first & slab_below)
    def _():
        for j in range(inner):
            hail(layer * inner + j, slab - 1)

    @pl.when(last & slab_above)
    def _():
        for j in range(inner):
            hail(layer * inner + j, slab + 1)

    @pl.when(below)
    def _():
        hail(me - inner, slab)

    @pl.when(above)
    def _():
        hail(me + inner, slab)

    for j in range(layers):
        @pl.when(i * layers + j != me)
        def _():
            hail(i * layers + j, slab)

    one = lambda flag: jnp.where(flag, 1, 0)
    pl.semaphore_wait(
        barrier, inner - 1 + one(slab_above) + one(slab_below) + one(above) + one(below) + layers - one(owner == i))

    piece = side + i

    def block(kind, to):
        if kind == 0:
            return sent.at[pl.ds(to * mine, mine)], landed.at[pl.ds(1, mine), piece], slab
        if kind == 1:
            return (sent.at[lax.rem(to * mine - 1 + chunks, chunks)], landed.at[0, piece],
                    slab + one(to == 0))
        return (sent.at[lax.rem(to * mine + mine, chunks)], landed.at[slots - 1, piece],
                slab - one(to == inner - 1))

    def outgoing(kind, step):
        to = partner_of(i, step)
        src, dst, row = block(kind, to)
        return pltpu.make_async_remote_copy(
            src_ref=src, dst_ref=dst, send_sem=main_send.at[kind, step], recv_sem=main_recv.at[kind, step],
            device_id=(layer * inner + to, row), device_id_type=MESH)

    def incoming(kind, step):
        source = partner_of(i, step)
        at = side + source
        dst = (landed.at[pl.ds(1, mine), at], landed.at[0, at], landed.at[slots - 1, at])[kind]
        src = sent.at[pl.ds(0, mine)] if kind == 0 else sent.at[0]
        return pltpu.make_async_remote_copy(
            src_ref=src, dst_ref=dst, send_sem=main_send.at[kind, step], recv_sem=main_recv.at[kind, step],
            device_id=(layer * inner + source, slab), device_id_type=MESH)

    def leaves(kind, step):
        to = partner_of(i, step)
        if kind == 0:
            return None
        if kind == 1:
            return (to > 0) | slab_above
        return (to < inner - 1) | slab_below

    def arrives(kind):
        if kind == 0:
            return None
        if kind == 1:
            return (i > 0) | slab_below
        return (i < inner - 1) | slab_above

    def guarded(flag, act):
        if flag is None:
            act()
        else:
            pl.when(flag)(act)

    for step in range(1, inner):
        for kind in range(3):
            guarded(leaves(kind, step), lambda: outgoing(kind, step).start())

    @pl.when(first & slab_above)
    def _():
        outgoing(1, 0).start()

    @pl.when(last & slab_below)
    def _():
        outgoing(2, 0).start()

    landed[pl.ds(1, mine), piece] = sent[pl.ds(i * mine, mine)]

    @pl.when(i > 0)
    def _():
        landed[0, piece] = sent[lax.rem(i * mine - 1 + chunks, chunks)]

    @pl.when(i < inner - 1)
    def _():
        landed[slots - 1, piece] = sent[lax.rem(i * mine + mine, chunks)]

    @pl.when(first & jnp.logical_not(slab_below))
    def _():
        landed[0, side:side + inner] = jnp.zeros((inner,) + landed.shape[2:], landed.dtype)

    @pl.when(last & jnp.logical_not(slab_above))
    def _():
        landed[slots - 1, side:side + inner] = jnp.zeros((inner,) + landed.shape[2:], landed.dtype)

    tables = ((mats_in, mats), (weights_in, weights), (ints_in, ints))

    def table(number, j, to):
        src, dst = tables[number]
        return pltpu.make_async_remote_copy(
            src_ref=src, dst_ref=dst.at[j], send_sem=table_send.at[number, 0], recv_sem=table_recv.at[number, 0],
            device_id=(to, slab), device_id_type=MESH)

    for j in range(layers):
        to = j * inner + owner

        @pl.when(to != me)
        def _():
            for number in range(3):
                src, dst = tables[number]
                pltpu.make_async_remote_copy(
                    src_ref=src, dst_ref=dst.at[spot], send_sem=table_send.at[number, j],
                    recv_sem=table_recv.at[number, spot], device_id=(to, slab), device_id_type=MESH).start()

    @pl.when(owner == i)
    def _():
        for src, dst in tables:
            dst[spot] = src[...]

    def relay(way, source):
        at = source - (inner - side) if way == 0 else source
        into = at if way == 0 else side + inner + source
        return pltpu.make_async_remote_copy(
            src_ref=landed.at[:, side + source], dst_ref=landed.at[:, into],
            send_sem=relay_send.at[way, at], recv_sem=relay_recv.at[way, at],
            device_id=(me + inner if way == 0 else me - inner, slab), device_id_type=MESH)

    for step in range(inner):
        source = partner_of(i, step)
        for kind in range(3):
            if step:
                guarded(arrives(kind), lambda: incoming(kind, step).wait_recv())
        if step == 0:
            pl.when(first & slab_below)(lambda: incoming(1, 0).wait_recv())
            pl.when(last & slab_above)(lambda: incoming(2, 0).wait_recv())
        pl.when(above & (source >= inner - side))(lambda: relay(0, source).start())
        pl.when(below & (source < side))(lambda: relay(1, source).start())

    def zero(start):
        landed[:, start:start + side] = jnp.zeros((slots, side) + landed.shape[2:], landed.dtype)

    pl.when(jnp.logical_not(below))(lambda: zero(0))
    pl.when(jnp.logical_not(above))(lambda: zero(side + inner))

    def relayed(way, at):
        into = at if way == 0 else side + inner + at
        return pltpu.make_async_remote_copy(
            src_ref=landed.at[:, into], dst_ref=landed.at[:, into],
            send_sem=relay_send.at[way, at], recv_sem=relay_recv.at[way, at],
            device_id=(me - inner if way == 0 else me + inner, slab), device_id_type=MESH)

    for at in range(side):
        pl.when(below)(lambda: relayed(0, at).wait_recv())
        pl.when(above)(lambda: relayed(1, at).wait_recv())

    for j in range(layers):
        @pl.when(i * layers + j != me)
        def _():
            for number in range(3):
                src, dst = tables[number]
                pltpu.make_async_remote_copy(
                    src_ref=src, dst_ref=dst.at[j], send_sem=table_send.at[number, j],
                    recv_sem=table_recv.at[number, j], device_id=(me, slab), device_id_type=MESH).wait_recv()

        @pl.when(j * inner + owner != me)
        def _():
            for number in range(3):
                src, dst = tables[number]
                pltpu.make_async_remote_copy(
                    src_ref=src, dst_ref=dst.at[j], send_sem=table_send.at[number, j],
                    recv_sem=table_recv.at[number, j], device_id=(me, slab), device_id_type=MESH).wait_send()

    for step in range(1, inner):
        for kind in range(3):
            guarded(leaves(kind, step), lambda: outgoing(kind, step).wait_send())
    pl.when(first & slab_above)(lambda: outgoing(1, 0).wait_send())
    pl.when(last & slab_below)(lambda: outgoing(2, 0).wait_send())
    for at in range(side):
        pl.when(above)(lambda: relayed(0, at).wait_send())
        pl.when(below)(lambda: relayed(1, at).wait_send())


def back_kernel(inner, out_ref, landed, send_sem, recv_sem):
    me, slab = lax.axis_index("energy"), lax.axis_index("slab")
    layer, i = lax.div(me, inner), lax.rem(me, inner)
    mine = out_ref.shape[1]
    barrier = pltpu.get_barrier_semaphore()
    for step in range(1, inner):
        pl.semaphore_signal(
            barrier, inc=1, device_id=(layer * inner + partner_of(i, step), slab), device_id_type=MESH)
    pl.semaphore_wait(barrier, inner - 1)

    def copy(step, at):
        to = partner_of(i, step)
        return pltpu.make_async_remote_copy(
            src_ref=out_ref.at[to], dst_ref=landed.at[pl.ds(at * mine, mine)],
            send_sem=send_sem.at[step], recv_sem=recv_sem.at[step],
            device_id=(layer * inner + to, slab), device_id_type=MESH)

    for step in range(1, inner):
        copy(step, i).start()
    landed[pl.ds(i * mine, mine)] = out_ref[i]
    for step in range(1, inner):
        copy(step, partner_of(i, step)).wait_recv()
        copy(step, i).wait_send()


def unpack_kernel(groups, per_dev, landed, out_ref, wide, tall):
    local_e = landed.shape[1]
    lanes = min(out_ref.shape[1], 128)
    for g in range(groups):
        for j in range(wide.shape[0]):
            wide[j, g * local_e:(g + 1) * local_e, :] = landed[g, :, j * 128:(j + 1) * 128].astype(jnp.float32)
    pick = order(groups, per_dev)
    for e in range(local_e):
        rows = jnp.concatenate(
            [wide[j, pl.ds(e, groups, stride=local_e), :] for j in range(wide.shape[0])], axis=1)
        stack = jnp.concatenate([rows[:, i * BLOCK:(i + 1) * BLOCK] for i in range(per_dev)], axis=0)
        turned = jnp.dot(stack.T.astype(jnp.bfloat16), pick, preferred_element_type=jnp.float32)
        if lanes < 128:
            turned = jnp.concatenate([turned, jnp.zeros((BLOCK, 128 - lanes), jnp.float32)], axis=1)
        for j in range(tall.shape[0]):
            tall[j, pl.ds(e, BLOCK, stride=local_e), :] = turned[:, j * 128:(j + 1) * 128]
    for j in range(tall.shape[0]):
        out_ref[:, j * 128:j * 128 + lanes] = tall[j, :out_ref.shape[0], :lanes].astype(jnp.bfloat16)


def scatter_kernel(side, ints_ref, landed, weight_ref, matrix_ref, out_ref,
                   green, spread_q, spread_r, both, bands, stage):
    slots, pieces, local_e, width = landed.shape
    inner = pieces - 2 * side
    mine = slots - 2
    rows_e = pieces * local_e
    late = rows_e - WINDOW
    slab_atoms = inner * mine * HALO
    first_atom = (lax.axis_index("slab") * slab_atoms
                  + lax.rem(lax.axis_index("energy"), inner) * mine * HALO - HALO)
    unit = eye(128)

    def turn(slot, carry):
        if local_e % 16:
            for piece in range(pieces):
                stage[piece * local_e:(piece + 1) * local_e, :] = landed[slot, piece].astype(jnp.float32)
            tall = stage[...].astype(jnp.bfloat16)
        else:
            tall = landed[slot].reshape(rows_e, width)
        two = jnp.concatenate([tall[:WINDOW], tall[late:]], axis=0)
        turned = jnp.concatenate([
            lax.dot_general(unit, two[:, j * 128:(j + 1) * 128], NT, preferred_element_type=jnp.float32).astype(
                jnp.bfloat16) for j in range(width // 128)], axis=0)
        for atom in range(HALO):
            for c in range(2):
                start = (2 * atom + c) * PAIR
                for window in range(2):
                    green[window, slot * HALO + atom, :, c * WINDOW:(c + 1) * WINDOW] = (
                        turned[start:start + PAIR, window * WINDOW:(window + 1) * WINDOW])
        return carry

    lax.fori_loop(0, slots, turn, 0)

    wide = NBR * PAIR
    lane = lax.broadcasted_iota(jnp.int32, (8, wide), 1)
    key_q = (lane // ORB)[:1]
    key_r = (lane // PAIR * ORB + lane % ORB)[:1]
    row = lax.broadcasted_iota(jnp.int32, (NBR * ORB, wide), 0)
    count = matrix_ref.shape[0] * matrix_ref.shape[1]
    matrices = matrix_ref[...].reshape(count, matrix_ref.shape[2])[:, :NBR * ORB]
    spread_q[...] = jnp.dot(matrices, (row == key_q).astype(jnp.bfloat16), preferred_element_type=jnp.float32)
    spread_r[...] = jnp.dot(matrices, (row == key_r).astype(jnp.bfloat16), preferred_element_type=jnp.float32)

    sub = lax.broadcasted_iota(jnp.int32, (8, WINDOW), 0)
    left_half = lax.broadcasted_iota(jnp.int32, (WINDOW, WINDOW), 1) < SPAN
    low_rows = lax.broadcasted_iota(jnp.int32, (8, wide), 0) < 4

    def chunk(m, carry):
        parts = []
        for a in range(HALO):
            atom = m * HALO + a
            for k in range(NBR):
                index = a * NBR + k
                shift = ints_ref[m, 1, index]
                later = jnp.where(shift >= 0, 1, 0)
                base = shift + side * local_e - BAND // 2 - later * late
                weight = weight_ref[m, pl.ds(index, 1), :]
                tile = pltpu.roll(jnp.broadcast_to(weight, (8, WINDOW)), WINDOW - BAND + 1 - base, 1)
                for step in (1, 2, 4):
                    tile = jnp.where((sub & step) != 0, pltpu.roll(tile, step, 1), tile)
                tiles = [tile] + [pltpu.roll(tile, 8 * b, 1) for b in range(1, WINDOW // 8)]
                band = jnp.concatenate(tiles, axis=0)
                turned_band = jnp.concatenate(tiles[SPAN // 8:] + tiles[:SPAN // 8], axis=0)
                toeplitz = jnp.concatenate([
                    jnp.where(left_half, band, 0.0).astype(jnp.bfloat16),
                    jnp.where(left_half, 0.0, turned_band).astype(jnp.bfloat16)], axis=0)
                partner = jnp.clip(ints_ref[m, 0, index] - first_atom, 0, slots * HALO - 1)
                banded = jnp.dot(green[later, partner], toeplitz, preferred_element_type=jnp.float32)
                bands[a % 2, k * PAIR:(k + 1) * PAIR, :] = banded.astype(jnp.bfloat16)
            right = spread_r[pl.ds(pl.multiple_of(atom * 16, 16), 16), :]
            rights = (right[:8], jnp.concatenate([right[8:12], right[:4]], axis=0), right[4:12])
            for four in range(ORB // 4):
                rows = []
                for h in range(2):
                    p = four * 4 + h * 2
                    q0 = spread_q[pl.ds(atom * 16 + p, 1), :]
                    q1 = spread_q[pl.ds(atom * 16 + p + 1, 1), :]
                    rows += [q0 * rights[0], jnp.where(low_rows, q0, q1) * rights[1], q1 * rights[2]]
                both[a % 2, four * 48:(four + 1) * 48, :] = jnp.concatenate(rows, axis=0).astype(jnp.bfloat16)
            total = jnp.dot(both[a % 2], bands[a % 2], preferred_element_type=jnp.float32)
            turned = lax.dot_general(unit, total.astype(jnp.bfloat16), NT, preferred_element_type=jnp.float32)
            parts += [turned[:SPAN], turned[SPAN:]]
        whole = jnp.concatenate(parts, axis=1)
        for d in range(inner):
            out_ref[d, m] = whole[d * local_e:(d + 1) * local_e].astype(jnp.bfloat16)
        return carry

    lax.fori_loop(0, mine, chunk, 0)


def on_device(green_blocks, couplings, band_weights, neighbours, shifts):
    groups = lax.axis_size("energy")
    local_e, slab_count = green_blocks.shape[3:]
    per_dev = slab_count // groups
    width = per_dev * BLOCK
    pairs = per_dev * NBR
    inner = SPAN // local_e
    layers = groups // inner
    side = pl.cdiv(REACH, local_e)
    pieces = inner + 2 * side
    mine = groups // inner
    slots = mine + 2
    assert per_dev == HALO and side <= inner and pieces * local_e >= WINDOW
    vmem = pl.BlockSpec(memory_space=pltpu.VMEM)
    smem = pl.BlockSpec(memory_space=pltpu.SMEM)
    blocks = jax.ShapeDtypeStruct((groups, local_e, width), jnp.bfloat16)
    wide = pltpu.VMEM((pl.cdiv(slab_count, 128), BLOCK * local_e, 128), jnp.float32)
    packed = pltpu.VMEM((width // 128, local_e * groups, 128), jnp.float32)
    room = pltpu.CompilerParams(vmem_limit_bytes=32 * 1024 * 1024)

    matrix = couplings.reshape(ORB, ORB, per_dev, NBR).transpose(2, 0, 3, 1).reshape(per_dev, ORB, NBR * ORB)
    matrix = jnp.pad(matrix, ((0, 0), (0, 16 - ORB), (0, 256 - NBR * ORB))).reshape(per_dev * 16, 256)
    weight = jnp.pad(band_weights.reshape(BAND, pairs)[::-1].T, ((0, 0), (0, WINDOW - BAND)))
    ints = jnp.pad(jnp.concatenate([neighbours, shifts], axis=0), ((0, 6), (0, 128 - pairs)))

    sent = pl.pallas_call(
        functools.partial(pack_kernel, groups, per_dev),
        out_shape=blocks, in_specs=[vmem], out_specs=vmem,
        scratch_shapes=[wide, packed], compiler_params=room,
    )(green_blocks.reshape(BLOCK * local_e, slab_count))

    landed, mats, weights, numbers = pl.pallas_call(
        functools.partial(gather_kernel, inner, layers, side),
        out_shape=(
            jax.ShapeDtypeStruct((slots, pieces, local_e, width), jnp.bfloat16),
            jax.ShapeDtypeStruct((layers,) + matrix.shape, jnp.bfloat16),
            jax.ShapeDtypeStruct((layers,) + weight.shape, jnp.float32),
            jax.ShapeDtypeStruct((layers,) + ints.shape, jnp.int32),
        ),
        in_specs=[vmem] * 4, out_specs=(vmem,) * 4,
        scratch_shapes=[
            pltpu.SemaphoreType.DMA((3, inner)), pltpu.SemaphoreType.DMA((3, inner)),
            pltpu.SemaphoreType.DMA((2, side)), pltpu.SemaphoreType.DMA((2, side)),
            pltpu.SemaphoreType.DMA((3, layers)), pltpu.SemaphoreType.DMA((3, layers)),
        ],
        compiler_params=pltpu.CompilerParams(
            collective_id=0, has_side_effects=True, vmem_limit_bytes=32 * 1024 * 1024),
    )(sent, matrix, weight, ints)

    out = pl.pallas_call(
        functools.partial(scatter_kernel, side),
        out_shape=jax.ShapeDtypeStruct((inner, mine, local_e, width), jnp.bfloat16),
        in_specs=[smem, vmem, vmem, vmem],
        out_specs=vmem,
        scratch_shapes=[
            pltpu.VMEM((2, slots * HALO, PAIR, 2 * WINDOW), jnp.bfloat16),
            pltpu.VMEM((mine * HALO * 16, NBR * PAIR), jnp.float32),
            pltpu.VMEM((mine * HALO * 16, NBR * PAIR), jnp.float32),
            pltpu.VMEM((2, PAIR, NBR * PAIR), jnp.bfloat16),
            pltpu.VMEM((2, NBR * PAIR, WINDOW), jnp.bfloat16),
            pltpu.VMEM((pieces * local_e, width), jnp.float32),
        ],
        compiler_params=pltpu.CompilerParams(vmem_limit_bytes=40 * 1024 * 1024),
    )(numbers, landed, weights, mats)

    back = pl.pallas_call(
        functools.partial(back_kernel, inner),
        out_shape=blocks, in_specs=[vmem], out_specs=vmem,
        scratch_shapes=[pltpu.SemaphoreType.DMA((inner,)), pltpu.SemaphoreType.DMA((inner,))],
        compiler_params=pltpu.CompilerParams(
            collective_id=1, has_side_effects=True, vmem_limit_bytes=32 * 1024 * 1024),
    )(out)
    result = pl.pallas_call(
        functools.partial(unpack_kernel, groups, per_dev),
        out_shape=jax.ShapeDtypeStruct((BLOCK * local_e, slab_count), jnp.bfloat16),
        in_specs=[vmem], out_specs=vmem,
        scratch_shapes=[packed, wide], compiler_params=room,
    )(back)
    return result.reshape(2, ORB, ORB, local_e, slab_count)


def solution(mesh):
    return jax.shard_map(
        on_device,
        mesh=mesh,
        in_specs=(
            P(None, None, None, "energy", "slab"),
            P(None, None, "slab", "energy"),
            P(None, "slab", "energy"),
            P("slab", "energy"),
            P("slab", "energy"),
        ),
        out_specs=P(None, None, None, "energy", "slab"),
        check_vma=False,
    )
```

```python
import functools

import jax
import jax.numpy as jnp
from jax import lax
from jax.experimental import pallas as pl
from jax.experimental.pallas import tpu as pltpu
from jax.sharding import PartitionSpec as P

ORB = 12
NBR = 16
BAND = 9
SHIFT = 32
HALO = 4
BLOCK = 2 * ORB * ORB
PAIR = ORB * ORB
REACH = SHIFT + BAND // 2
SPAN = 64
WINDOW = 128

MESH = pl.DeviceIdType.MESH
NT = (((1,), (1,)), ((), ()))


def order(groups, per_dev):
    count = groups * per_dev
    row = lax.broadcasted_iota(jnp.int32, (count, count), 0)
    atom = lax.broadcasted_iota(jnp.int32, (count, count), 1)
    return (atom == (row % groups) * per_dev + row // groups).astype(jnp.bfloat16)


def eye(count):
    row = lax.broadcasted_iota(jnp.int32, (count, count), 0)
    column = lax.broadcasted_iota(jnp.int32, (count, count), 1)
    return (row == column).astype(jnp.bfloat16)


def partner_of(i, step):
    out, bit = 0, 1
    while bit <= step:
        out = out + bit * lax.rem(lax.div(i, bit) + step // bit, 2)
        bit *= 2
    return lax.div(i, bit) * bit + out if step else i


def pack_kernel(groups, per_dev, x_ref, sent, wide, packed):
    local_e = sent.shape[1]
    tiles = wide.shape[0]
    count = x_ref.shape[1]
    lanes = min(count, 128)
    if lanes < 128:
        wide[...] = jnp.zeros_like(wide)
    for j in range(tiles):
        wide[j, :x_ref.shape[0], :lanes] = x_ref[:, j * 128:j * 128 + lanes].astype(jnp.float32)
    pick = order(groups, per_dev)
    for e in range(local_e):
        rows = jnp.concatenate([wide[j, pl.ds(e, BLOCK, stride=local_e), :] for j in range(tiles)], axis=1)
        rows = rows[:, :count].astype(jnp.bfloat16)
        turned = lax.dot_general(pick, rows, NT, preferred_element_type=jnp.float32)
        flat = jnp.concatenate([turned[i * groups:(i + 1) * groups] for i in range(per_dev)], axis=1)
        for j in range(packed.shape[0]):
            packed[j, pl.ds(e, groups, stride=local_e), :] = flat[:, j * 128:(j + 1) * 128]
    for g in range(groups):
        for j in range(packed.shape[0]):
            sent[g, :, j * 128:(j + 1) * 128] = packed[j, g * local_e:(g + 1) * local_e, :].astype(jnp.bfloat16)


def gather_kernel(inner, layers, side, sent, mats_in, weights_in, ints_in, landed, mats, weights, ints,
                  main_send, main_recv, relay_send, relay_recv, table_send, table_recv):
    me, slab = lax.axis_index("energy"), lax.axis_index("slab")
    slabs = lax.axis_size("slab")
    layer, i = lax.div(me, inner), lax.rem(me, inner)
    chunks = sent.shape[0]
    mine = chunks // inner
    slots = mine + 2
    barrier = pltpu.get_barrier_semaphore()
    first, last = i == 0, i == inner - 1
    below, above = layer > 0, layer < layers - 1
    slab_below, slab_above = slab > 0, slab < slabs - 1
    owner, spot = lax.div(me, layers), lax.rem(me, layers)

    def hail(device, row):
        pl.semaphore_signal(barrier, inc=1, device_id=(device, row), device_id_type=MESH)

    for step in range(1, inner):
        hail(layer * inner + partner_of(i, step), slab)

    @pl.when(first & slab_below)
    def _():
        for j in range(inner):
            hail(layer * inner + j, slab - 1)

    @pl.when(last & slab_above)
    def _():
        for j in range(inner):
            hail(layer * inner + j, slab + 1)

    @pl.when(below)
    def _():
        hail(me - inner, slab)

    @pl.when(above)
    def _():
        hail(me + inner, slab)

    for j in range(layers):
        @pl.when(i * layers + j != me)
        def _():
            hail(i * layers + j, slab)

    one = lambda flag: jnp.where(flag, 1, 0)
    pl.semaphore_wait(
        barrier, inner - 1 + one(slab_above) + one(slab_below) + one(above) + one(below) + layers - one(owner == i))

    piece = side + i

    def block(kind, to):
        if kind == 0:
            return sent.at[pl.ds(to * mine, mine)], landed.at[pl.ds(1, mine), piece], slab
        if kind == 1:
            return (sent.at[lax.rem(to * mine - 1 + chunks, chunks)], landed.at[0, piece],
                    slab + one(to == 0))
        return (sent.at[lax.rem(to * mine + mine, chunks)], landed.at[slots - 1, piece],
                slab - one(to == inner - 1))

    def outgoing(kind, step):
        to = partner_of(i, step)
        src, dst, row = block(kind, to)
        return pltpu.make_async_remote_copy(
            src_ref=src, dst_ref=dst, send_sem=main_send.at[kind, step], recv_sem=main_recv.at[kind, step],
            device_id=(layer * inner + to, row), device_id_type=MESH)

    def incoming(kind, step):
        source = partner_of(i, step)
        at = side + source
        dst = (landed.at[pl.ds(1, mine), at], landed.at[0, at], landed.at[slots - 1, at])[kind]
        src = sent.at[pl.ds(0, mine)] if kind == 0 else sent.at[0]
        return pltpu.make_async_remote_copy(
            src_ref=src, dst_ref=dst, send_sem=main_send.at[kind, step], recv_sem=main_recv.at[kind, step],
            device_id=(layer * inner + source, slab), device_id_type=MESH)

    def leaves(kind, step):
        to = partner_of(i, step)
        if kind == 0:
            return None
        if kind == 1:
            return (to > 0) | slab_above
        return (to < inner - 1) | slab_below

    def arrives(kind):
        if kind == 0:
            return None
        if kind == 1:
            return (i > 0) | slab_below
        return (i < inner - 1) | slab_above

    def guarded(flag, act):
        if flag is None:
            act()
        else:
            pl.when(flag)(act)

    for step in range(1, inner):
        for kind in range(3):
            guarded(leaves(kind, step), lambda: outgoing(kind, step).start())

    @pl.when(first & slab_above)
    def _():
        outgoing(1, 0).start()

    @pl.when(last & slab_below)
    def _():
        outgoing(2, 0).start()

    landed[pl.ds(1, mine), piece] = sent[pl.ds(i * mine, mine)]

    @pl.when(i > 0)
    def _():
        landed[0, piece] = sent[lax.rem(i * mine - 1 + chunks, chunks)]

    @pl.when(i < inner - 1)
    def _():
        landed[slots - 1, piece] = sent[lax.rem(i * mine + mine, chunks)]

    @pl.when(first & jnp.logical_not(slab_below))
    def _():
        landed[0, side:side + inner] = jnp.zeros((inner,) + landed.shape[2:], landed.dtype)

    @pl.when(last & jnp.logical_not(slab_above))
    def _():
        landed[slots - 1, side:side + inner] = jnp.zeros((inner,) + landed.shape[2:], landed.dtype)

    tables = ((mats_in, mats), (weights_in, weights), (ints_in, ints))

    def table(number, j, to):
        src, dst = tables[number]
        return pltpu.make_async_remote_copy(
            src_ref=src, dst_ref=dst.at[j], send_sem=table_send.at[number, 0], recv_sem=table_recv.at[number, 0],
            device_id=(to, slab), device_id_type=MESH)

    for j in range(layers):
        to = j * inner + owner

        @pl.when(to != me)
        def _():
            for number in range(3):
                src, dst = tables[number]
                pltpu.make_async_remote_copy(
                    src_ref=src, dst_ref=dst.at[spot], send_sem=table_send.at[number, j],
                    recv_sem=table_recv.at[number, spot], device_id=(to, slab), device_id_type=MESH).start()

    @pl.when(owner == i)
    def _():
        for src, dst in tables:
            dst[spot] = src[...]

    def relay(way, source):
        at = source - (inner - side) if way == 0 else source
        into = at if way == 0 else side + inner + source
        return pltpu.make_async_remote_copy(
            src_ref=landed.at[:, side + source], dst_ref=landed.at[:, into],
            send_sem=relay_send.at[way, at], recv_sem=relay_recv.at[way, at],
            device_id=(me + inner if way == 0 else me - inner, slab), device_id_type=MESH)

    for step in range(inner):
        source = partner_of(i, step)
        for kind in range(3):
            if step:
                guarded(arrives(kind), lambda: incoming(kind, step).wait_recv())
        if step == 0:
            pl.when(first & slab_below)(lambda: incoming(1, 0).wait_recv())
            pl.when(last & slab_above)(lambda: incoming(2, 0).wait_recv())
        pl.when(above & (source >= inner - side))(lambda: relay(0, source).start())
        pl.when(below & (source < side))(lambda: relay(1, source).start())

    def zero(start):
        landed[:, start:start + side] = jnp.zeros((slots, side) + landed.shape[2:], landed.dtype)

    pl.when(jnp.logical_not(below))(lambda: zero(0))
    pl.when(jnp.logical_not(above))(lambda: zero(side + inner))

    def relayed(way, at):
        into = at if way == 0 else side + inner + at
        return pltpu.make_async_remote_copy(
            src_ref=landed.at[:, into], dst_ref=landed.at[:, into],
            send_sem=relay_send.at[way, at], recv_sem=relay_recv.at[way, at],
            device_id=(me - inner if way == 0 else me + inner, slab), device_id_type=MESH)

    for at in range(side):
        pl.when(below)(lambda: relayed(0, at).wait_recv())
        pl.when(above)(lambda: relayed(1, at).wait_recv())

    for j in range(layers):
        @pl.when(i * layers + j != me)
        def _():
            for number in range(3):
                src, dst = tables[number]
                pltpu.make_async_remote_copy(
                    src_ref=src, dst_ref=dst.at[j], send_sem=table_send.at[number, j],
                    recv_sem=table_recv.at[number, j], device_id=(me, slab), device_id_type=MESH).wait_recv()

        @pl.when(j * inner + owner != me)
        def _():
            for number in range(3):
                src, dst = tables[number]
                pltpu.make_async_remote_copy(
                    src_ref=src, dst_ref=dst.at[j], send_sem=table_send.at[number, j],
                    recv_sem=table_recv.at[number, j], device_id=(me, slab), device_id_type=MESH).wait_send()

    for step in range(1, inner):
        for kind in range(3):
            guarded(leaves(kind, step), lambda: outgoing(kind, step).wait_send())
    pl.when(first & slab_above)(lambda: outgoing(1, 0).wait_send())
    pl.when(last & slab_below)(lambda: outgoing(2, 0).wait_send())
    for at in range(side):
        pl.when(above)(lambda: relayed(0, at).wait_send())
        pl.when(below)(lambda: relayed(1, at).wait_send())


def unpack_kernel(groups, per_dev, landed, out_ref, wide, tall):
    local_e = landed.shape[1]
    lanes = min(out_ref.shape[1], 128)
    for g in range(groups):
        for j in range(wide.shape[0]):
            wide[j, g * local_e:(g + 1) * local_e, :] = landed[g, :, j * 128:(j + 1) * 128].astype(jnp.float32)
    pick = order(groups, per_dev)
    for e in range(local_e):
        rows = jnp.concatenate(
            [wide[j, pl.ds(e, groups, stride=local_e), :] for j in range(wide.shape[0])], axis=1)
        stack = jnp.concatenate([rows[:, i * BLOCK:(i + 1) * BLOCK] for i in range(per_dev)], axis=0)
        turned = jnp.dot(stack.T.astype(jnp.bfloat16), pick, preferred_element_type=jnp.float32)
        if lanes < 128:
            turned = jnp.concatenate([turned, jnp.zeros((BLOCK, 128 - lanes), jnp.float32)], axis=1)
        for j in range(tall.shape[0]):
            tall[j, pl.ds(e, BLOCK, stride=local_e), :] = turned[:, j * 128:(j + 1) * 128]
    for j in range(tall.shape[0]):
        out_ref[:, j * 128:j * 128 + lanes] = tall[j, :out_ref.shape[0], :lanes].astype(jnp.bfloat16)


def scatter_kernel(side, ints_ref, landed, weight_ref, matrix_ref, back_ref,
                   out_ref, green, spread_q, spread_r, both, bands, stage, send_sem, recv_sem):
    slots, pieces, local_e, width = landed.shape
    inner = pieces - 2 * side
    mine = slots - 2
    rows_e = pieces * local_e
    late = rows_e - WINDOW
    slab_atoms = inner * mine * HALO
    first_atom = (lax.axis_index("slab") * slab_atoms
                  + lax.rem(lax.axis_index("energy"), inner) * mine * HALO - HALO)
    unit = eye(128)
    me, slab = lax.axis_index("energy"), lax.axis_index("slab")
    base_of_layer, i = lax.div(me, inner) * inner, lax.rem(me, inner)
    barrier = pltpu.get_barrier_semaphore()
    for step in range(1, inner):
        pl.semaphore_signal(
            barrier, inc=1, device_id=(base_of_layer + partner_of(i, step), slab), device_id_type=MESH)
    pl.semaphore_wait(barrier, inner - 1)

    def share(step, m, owner):
        to = partner_of(i, step)
        return pltpu.make_async_remote_copy(
            src_ref=out_ref.at[to, m], dst_ref=back_ref.at[owner * mine + m],
            send_sem=send_sem.at[step, m], recv_sem=recv_sem.at[step, m],
            device_id=(base_of_layer + to, slab), device_id_type=MESH)

    def turn(slot, carry):
        if local_e % 16:
            for piece in range(pieces):
                stage[piece * local_e:(piece + 1) * local_e, :] = landed[slot, piece].astype(jnp.float32)
            tall = stage[...].astype(jnp.bfloat16)
        else:
            tall = landed[slot].reshape(rows_e, width)
        two = jnp.concatenate([tall[:WINDOW], tall[late:]], axis=0)
        turned = jnp.concatenate([
            lax.dot_general(unit, two[:, j * 128:(j + 1) * 128], NT, preferred_element_type=jnp.float32).astype(
                jnp.bfloat16) for j in range(width // 128)], axis=0)
        for atom in range(HALO):
            for c in range(2):
                start = (2 * atom + c) * PAIR
                for window in range(2):
                    green[window, slot * HALO + atom, :, c * WINDOW:(c + 1) * WINDOW] = (
                        turned[start:start + PAIR, window * WINDOW:(window + 1) * WINDOW])
        return carry

    lax.fori_loop(0, slots, turn, 0)

    wide = NBR * PAIR
    lane = lax.broadcasted_iota(jnp.int32, (8, wide), 1)
    key_q = (lane // ORB)[:1]
    key_r = (lane // PAIR * ORB + lane % ORB)[:1]
    row = lax.broadcasted_iota(jnp.int32, (NBR * ORB, wide), 0)
    count = matrix_ref.shape[0] * matrix_ref.shape[1]
    matrices = matrix_ref[...].reshape(count, matrix_ref.shape[2])[:, :NBR * ORB]
    spread_q[...] = jnp.dot(matrices, (row == key_q).astype(jnp.bfloat16), preferred_element_type=jnp.float32)
    spread_r[...] = jnp.dot(matrices, (row == key_r).astype(jnp.bfloat16), preferred_element_type=jnp.float32)

    sub = lax.broadcasted_iota(jnp.int32, (8, WINDOW), 0)
    left_half = lax.broadcasted_iota(jnp.int32, (WINDOW, WINDOW), 1) < SPAN
    low_rows = lax.broadcasted_iota(jnp.int32, (8, wide), 0) < 4

    def chunk(m, carry):
        parts = []
        for a in range(HALO):
            atom = m * HALO + a
            for k in range(NBR):
                index = a * NBR + k
                shift = ints_ref[m, 1, index]
                later = jnp.where(shift >= 0, 1, 0)
                base = shift + side * local_e - BAND // 2 - later * late
                weight = weight_ref[m, pl.ds(index, 1), :]
                tile = pltpu.roll(jnp.broadcast_to(weight, (8, WINDOW)), WINDOW - BAND + 1 - base, 1)
                for step in (1, 2, 4):
                    tile = jnp.where((sub & step) != 0, pltpu.roll(tile, step, 1), tile)
                tiles = [tile] + [pltpu.roll(tile, 8 * b, 1) for b in range(1, WINDOW // 8)]
                band = jnp.concatenate(tiles, axis=0)
                turned_band = jnp.concatenate(tiles[SPAN // 8:] + tiles[:SPAN // 8], axis=0)
                toeplitz = jnp.concatenate([
                    jnp.where(left_half, band, 0.0).astype(jnp.bfloat16),
                    jnp.where(left_half, 0.0, turned_band).astype(jnp.bfloat16)], axis=0)
                partner = jnp.clip(ints_ref[m, 0, index] - first_atom, 0, slots * HALO - 1)
                banded = jnp.dot(green[later, partner], toeplitz, preferred_element_type=jnp.float32)
                bands[a % 2, k * PAIR:(k + 1) * PAIR, :] = banded.astype(jnp.bfloat16)
            right = spread_r[pl.ds(pl.multiple_of(atom * 16, 16), 16), :]
            rights = (right[:8], jnp.concatenate([right[8:12], right[:4]], axis=0), right[4:12])
            for four in range(ORB // 4):
                rows = []
                for h in range(2):
                    p = four * 4 + h * 2
                    q0 = spread_q[pl.ds(atom * 16 + p, 1), :]
                    q1 = spread_q[pl.ds(atom * 16 + p + 1, 1), :]
                    rows += [q0 * rights[0], jnp.where(low_rows, q0, q1) * rights[1], q1 * rights[2]]
                both[a % 2, four * 48:(four + 1) * 48, :] = jnp.concatenate(rows, axis=0).astype(jnp.bfloat16)
            total = jnp.dot(both[a % 2], bands[a % 2], preferred_element_type=jnp.float32)
            turned = lax.dot_general(unit, total.astype(jnp.bfloat16), NT, preferred_element_type=jnp.float32)
            parts += [turned[:SPAN], turned[SPAN:]]
        whole = jnp.concatenate(parts, axis=1)
        for d in range(inner):
            out_ref[d, m] = whole[d * local_e:(d + 1) * local_e].astype(jnp.bfloat16)
        for step in range(1, inner):
            share(step, m, i).start()
        back_ref[i * mine + m] = out_ref[i, m]
        return carry

    lax.fori_loop(0, mine, chunk, 0)

    def finish(m, carry):
        for step in range(1, inner):
            share(step, m, partner_of(i, step)).wait_recv()
            share(step, m, i).wait_send()
        return carry

    lax.fori_loop(0, mine, finish, 0)


def on_device(green_blocks, couplings, band_weights, neighbours, shifts):
    groups = lax.axis_size("energy")
    local_e, slab_count = green_blocks.shape[3:]
    per_dev = slab_count // groups
    width = per_dev * BLOCK
    pairs = per_dev * NBR
    inner = SPAN // local_e
    layers = groups // inner
    side = pl.cdiv(REACH, local_e)
    pieces = inner + 2 * side
    mine = groups // inner
    slots = mine + 2
    assert per_dev == HALO and side <= inner and pieces * local_e >= WINDOW
    vmem = pl.BlockSpec(memory_space=pltpu.VMEM)
    smem = pl.BlockSpec(memory_space=pltpu.SMEM)
    blocks = jax.ShapeDtypeStruct((groups, local_e, width), jnp.bfloat16)
    wide = pltpu.VMEM((pl.cdiv(slab_count, 128), BLOCK * local_e, 128), jnp.float32)
    packed = pltpu.VMEM((width // 128, local_e * groups, 128), jnp.float32)
    room = pltpu.CompilerParams(vmem_limit_bytes=32 * 1024 * 1024)

    matrix = couplings.reshape(ORB, ORB, per_dev, NBR).transpose(2, 0, 3, 1).reshape(per_dev, ORB, NBR * ORB)
    matrix = jnp.pad(matrix, ((0, 0), (0, 16 - ORB), (0, 256 - NBR * ORB))).reshape(per_dev * 16, 256)
    weight = jnp.pad(band_weights.reshape(BAND, pairs)[::-1].T, ((0, 0), (0, WINDOW - BAND)))
    ints = jnp.pad(jnp.concatenate([neighbours, shifts], axis=0), ((0, 6), (0, 128 - pairs)))

    sent = pl.pallas_call(
        functools.partial(pack_kernel, groups, per_dev),
        out_shape=blocks, in_specs=[vmem], out_specs=vmem,
        scratch_shapes=[wide, packed], compiler_params=room,
    )(green_blocks.reshape(BLOCK * local_e, slab_count))

    landed, mats, weights, numbers = pl.pallas_call(
        functools.partial(gather_kernel, inner, layers, side),
        out_shape=(
            jax.ShapeDtypeStruct((slots, pieces, local_e, width), jnp.bfloat16),
            jax.ShapeDtypeStruct((layers,) + matrix.shape, jnp.bfloat16),
            jax.ShapeDtypeStruct((layers,) + weight.shape, jnp.float32),
            jax.ShapeDtypeStruct((layers,) + ints.shape, jnp.int32),
        ),
        in_specs=[vmem] * 4, out_specs=(vmem,) * 4,
        scratch_shapes=[
            pltpu.SemaphoreType.DMA((3, inner)), pltpu.SemaphoreType.DMA((3, inner)),
            pltpu.SemaphoreType.DMA((2, side)), pltpu.SemaphoreType.DMA((2, side)),
            pltpu.SemaphoreType.DMA((3, layers)), pltpu.SemaphoreType.DMA((3, layers)),
        ],
        compiler_params=pltpu.CompilerParams(
            collective_id=0, has_side_effects=True, vmem_limit_bytes=32 * 1024 * 1024),
    )(sent, matrix, weight, ints)

    back = pl.pallas_call(
        functools.partial(scatter_kernel, side),
        out_shape=blocks,
        in_specs=[smem, vmem, vmem, vmem],
        out_specs=vmem,
        scratch_shapes=[
            pltpu.VMEM((inner, mine, local_e, width), jnp.bfloat16),
            pltpu.VMEM((2, slots * HALO, PAIR, 2 * WINDOW), jnp.bfloat16),
            pltpu.VMEM((mine * HALO * 16, NBR * PAIR), jnp.float32),
            pltpu.VMEM((mine * HALO * 16, NBR * PAIR), jnp.float32),
            pltpu.VMEM((2, PAIR, NBR * PAIR), jnp.bfloat16),
            pltpu.VMEM((2, NBR * PAIR, WINDOW), jnp.bfloat16),
            pltpu.VMEM((pieces * local_e, width), jnp.float32),
            pltpu.SemaphoreType.DMA((inner, mine)), pltpu.SemaphoreType.DMA((inner, mine)),
        ],
        compiler_params=pltpu.CompilerParams(
            collective_id=1, has_side_effects=True, vmem_limit_bytes=40 * 1024 * 1024),
    )(numbers, landed, weights, mats)
    result = pl.pallas_call(
        functools.partial(unpack_kernel, groups, per_dev),
        out_shape=jax.ShapeDtypeStruct((BLOCK * local_e, slab_count), jnp.bfloat16),
        in_specs=[vmem], out_specs=vmem,
        scratch_shapes=[packed, wide], compiler_params=room,
    )(back)
    return result.reshape(2, ORB, ORB, local_e, slab_count)


def solution(mesh):
    return jax.shard_map(
        on_device,
        mesh=mesh,
        in_specs=(
            P(None, None, None, "energy", "slab"),
            P(None, None, "slab", "energy"),
            P(None, "slab", "energy"),
            P("slab", "energy"),
            P("slab", "energy"),
        ),
        out_specs=P(None, None, None, "energy", "slab"),
        check_vma=False,
    )
```

```python
import functools

import jax
import jax.numpy as jnp
from jax import lax
from jax.experimental import pallas as pl
from jax.experimental.pallas import tpu as pltpu
from jax.sharding import PartitionSpec as P

ORB = 12
NBR = 16
BAND = 9
SHIFT = 32
HALO = 4
BLOCK = 2 * ORB * ORB
PAIR = ORB * ORB
REACH = SHIFT + BAND // 2
SPAN = 64
WINDOW = 128

MESH = pl.DeviceIdType.MESH
NT = (((1,), (1,)), ((), ()))


def order(groups, per_dev):
    count = groups * per_dev
    row = lax.broadcasted_iota(jnp.int32, (count, count), 0)
    atom = lax.broadcasted_iota(jnp.int32, (count, count), 1)
    return (atom == (row % groups) * per_dev + row // groups).astype(jnp.bfloat16)


def eye(count):
    row = lax.broadcasted_iota(jnp.int32, (count, count), 0)
    column = lax.broadcasted_iota(jnp.int32, (count, count), 1)
    return (row == column).astype(jnp.bfloat16)


def partner_of(i, step):
    out, bit = 0, 1
    while bit <= step:
        out = out + bit * lax.rem(lax.div(i, bit) + step // bit, 2)
        bit *= 2
    return lax.div(i, bit) * bit + out if step else i


def pack_kernel(groups, per_dev, x_ref, sent, wide, packed):
    local_e = sent.shape[1]
    tiles = wide.shape[0]
    count = x_ref.shape[1]
    lanes = min(count, 128)
    if lanes < 128:
        wide[...] = jnp.zeros_like(wide)
    for j in range(tiles):
        wide[j, :x_ref.shape[0], :lanes] = x_ref[:, j * 128:j * 128 + lanes].astype(jnp.float32)
    pick = order(groups, per_dev)
    for e in range(local_e):
        rows = jnp.concatenate([wide[j, pl.ds(e, BLOCK, stride=local_e), :] for j in range(tiles)], axis=1)
        rows = rows[:, :count].astype(jnp.bfloat16)
        turned = lax.dot_general(pick, rows, NT, preferred_element_type=jnp.float32)
        flat = jnp.concatenate([turned[i * groups:(i + 1) * groups] for i in range(per_dev)], axis=1)
        for j in range(packed.shape[0]):
            packed[j, pl.ds(e, groups, stride=local_e), :] = flat[:, j * 128:(j + 1) * 128]
    for g in range(groups):
        for j in range(packed.shape[0]):
            sent[g, :, j * 128:(j + 1) * 128] = packed[j, g * local_e:(g + 1) * local_e, :].astype(jnp.bfloat16)


def unpack_kernel(groups, per_dev, landed, out_ref, wide, tall):
    local_e = landed.shape[1]
    lanes = min(out_ref.shape[1], 128)
    for g in range(groups):
        for j in range(wide.shape[0]):
            wide[j, g * local_e:(g + 1) * local_e, :] = landed[g, :, j * 128:(j + 1) * 128].astype(jnp.float32)
    pick = order(groups, per_dev)
    for e in range(local_e):
        rows = jnp.concatenate(
            [wide[j, pl.ds(e, groups, stride=local_e), :] for j in range(wide.shape[0])], axis=1)
        stack = jnp.concatenate([rows[:, i * BLOCK:(i + 1) * BLOCK] for i in range(per_dev)], axis=0)
        turned = jnp.dot(stack.T.astype(jnp.bfloat16), pick, preferred_element_type=jnp.float32)
        if lanes < 128:
            turned = jnp.concatenate([turned, jnp.zeros((BLOCK, 128 - lanes), jnp.float32)], axis=1)
        for j in range(tall.shape[0]):
            tall[j, pl.ds(e, BLOCK, stride=local_e), :] = turned[:, j * 128:(j + 1) * 128]
    for j in range(tall.shape[0]):
        out_ref[:, j * 128:j * 128 + lanes] = tall[j, :out_ref.shape[0], :lanes].astype(jnp.bfloat16)


def wire_kernel(inner, layers, side, sent, mats_in, weights_in, ints_in, back_ref,
                landed, mats, weights, ints, numbers, out_ref, green, spread_q, spread_r, both, toeplitz, bands, stage,
                slot_send, slot_recv, relay_send, relay_recv, table_send, table_recv, back_send, back_recv, local_sem):
    slots, pieces, local_e, width = landed.shape
    mine = slots - 2
    chunks = sent.shape[0]
    rows_e = pieces * local_e
    late = rows_e - WINDOW
    me, slab = lax.axis_index("energy"), lax.axis_index("slab")
    slabs = lax.axis_size("slab")
    layer, i = lax.div(me, inner), lax.rem(me, inner)
    first_of_layer = layer * inner
    first_atom = slab * (chunks * HALO) + i * (mine * HALO) - HALO
    first, last = i == 0, i == inner - 1
    below, above = layer > 0, layer < layers - 1
    slab_below, slab_above = slab > 0, slab < slabs - 1
    owner, spot = lax.div(me, layers), lax.rem(me, layers)
    barrier = pltpu.get_barrier_semaphore()
    one = lambda flag: jnp.where(flag, 1, 0)

    def hail(device, row):
        pl.semaphore_signal(barrier, inc=1, device_id=(device, row), device_id_type=MESH)

    for step in range(1, inner):
        hail(first_of_layer + partner_of(i, step), slab)

    @pl.when(first & slab_below)
    def _():
        for j in range(inner):
            hail(first_of_layer + j, slab - 1)

    @pl.when(last & slab_above)
    def _():
        for j in range(inner):
            hail(first_of_layer + j, slab + 1)

    pl.when(below)(lambda: hail(me - inner, slab))
    pl.when(above)(lambda: hail(me + inner, slab))
    for j in range(layers):
        pl.when(i * layers + j != me)(lambda: hail(i * layers + j, slab))
    pl.semaphore_wait(
        barrier, inner - 1 + one(slab_above) + one(slab_below) + one(above) + one(below) + layers - one(owner == i))

    tables = ((mats_in, mats), (weights_in, weights), (ints_in, ints))

    def table(number, j, at, to):
        src, dst = tables[number]
        return pltpu.make_async_remote_copy(
            src_ref=src, dst_ref=dst.at[at], send_sem=table_send.at[number, j], recv_sem=table_recv.at[number, at],
            device_id=(to, slab), device_id_type=MESH)

    for j in range(layers):
        to = j * inner + owner

        @pl.when(to != me)
        def _():
            for number in range(3):
                table(number, j, spot, to).start()

    def outgoing(slot, step):
        to = partner_of(i, step)
        row = slab + one((slot == 0) & (to == 0)) - one((slot == slots - 1) & (to == inner - 1))
        return pltpu.make_async_remote_copy(
            src_ref=sent.at[lax.rem(to * mine + slot - 1 + chunks, chunks)], dst_ref=landed.at[slot, side + i],
            send_sem=slot_send.at[slot, step], recv_sem=slot_recv.at[slot, step],
            device_id=(first_of_layer + to, row), device_id_type=MESH)

    def incoming(slot, step):
        source = partner_of(i, step)
        return pltpu.make_async_remote_copy(
            src_ref=sent.at[0], dst_ref=landed.at[slot, side + source],
            send_sem=slot_send.at[slot, step], recv_sem=slot_recv.at[slot, step],
            device_id=(first_of_layer + source, slab), device_id_type=MESH)

    def leaves(slot, step):
        to = partner_of(i, step)
        real = ((slot > 0) | (to > 0) | slab_above) & ((slot < slots - 1) | (to < inner - 1) | slab_below)
        if step:
            return real
        return real & (((slot == 0) & first) | ((slot == slots - 1) & last))

    def comes(slot, step):
        real = ((slot > 0) | (i > 0) | slab_below) & ((slot < slots - 1) | (i < inner - 1) | slab_above)
        if step:
            return real
        return real & (((slot == 0) & first) | ((slot == slots - 1) & last))

    def send_slot(slot, carry):
        for step in range(inner):
            pl.when(leaves(slot, step))(lambda: outgoing(slot, step).start())
        return carry

    lax.fori_loop(0, slots, send_slot, 0)

    landed[pl.ds(1, mine), side + i] = sent[pl.ds(i * mine, mine)]

    @pl.when(i > 0)
    def _():
        landed[0, side + i] = sent[lax.rem(i * mine - 1 + chunks, chunks)]

    @pl.when(i < inner - 1)
    def _():
        landed[slots - 1, side + i] = sent[lax.rem(i * mine + mine, chunks)]

    @pl.when(first & jnp.logical_not(slab_below))
    def _():
        landed[0, side:side + inner] = jnp.zeros((inner, local_e, width), landed.dtype)

    @pl.when(last & jnp.logical_not(slab_above))
    def _():
        landed[slots - 1, side:side + inner] = jnp.zeros((inner, local_e, width), landed.dtype)

    def zero(start):
        landed[:, start:start + side] = jnp.zeros((slots, side, local_e, width), landed.dtype)

    pl.when(jnp.logical_not(below))(lambda: zero(0))
    pl.when(jnp.logical_not(above))(lambda: zero(side + inner))

    @pl.when(owner == i)
    def _():
        for src, dst in tables:
            dst[spot] = src[...]

    for j in range(layers):
        @pl.when(i * layers + j != me)
        def _():
            for number in range(3):
                table(number, j, j, me).wait_recv()
    to_scalars = pltpu.make_async_copy(ints, numbers, local_sem)
    to_scalars.start()

    wide = NBR * PAIR
    lane = lax.broadcasted_iota(jnp.int32, (8, wide), 1)
    key_q = (lane // ORB)[:1]
    key_r = (lane // PAIR * ORB + lane % ORB)[:1]
    row = lax.broadcasted_iota(jnp.int32, (NBR * ORB, wide), 0)
    count = mats.shape[0] * mats.shape[1]
    matrices = mats[...].reshape(count, mats.shape[2])[:, :NBR * ORB]
    spread_q[...] = jnp.dot(matrices, (row == key_q).astype(jnp.bfloat16), preferred_element_type=jnp.float32)
    spread_r[...] = jnp.dot(matrices, (row == key_r).astype(jnp.bfloat16), preferred_element_type=jnp.float32)
    to_scalars.wait()

    def relay(way, slot):
        start, into = (inner, 0) if way == 0 else (side, side + inner)
        return pltpu.make_async_remote_copy(
            src_ref=landed.at[slot, start:start + side], dst_ref=landed.at[slot, into:into + side],
            send_sem=relay_send.at[way, slot], recv_sem=relay_recv.at[way, slot],
            device_id=(me + inner if way == 0 else me - inner, slab), device_id_type=MESH)

    def relayed(way, slot):
        into = 0 if way == 0 else side + inner
        return pltpu.make_async_remote_copy(
            src_ref=landed.at[slot, into:into + side], dst_ref=landed.at[slot, into:into + side],
            send_sem=relay_send.at[way, slot], recv_sem=relay_recv.at[way, slot],
            device_id=(me - inner if way == 0 else me + inner, slab), device_id_type=MESH)

    sub = lax.broadcasted_iota(jnp.int32, (8, WINDOW), 0)
    left_half = lax.broadcasted_iota(jnp.int32, (WINDOW, WINDOW), 1) < SPAN
    low_rows = lax.broadcasted_iota(jnp.int32, (8, wide), 0) < 4
    pair_of_atoms = 2

    def window_of(m, index):
        shift = numbers[m, 1, index]
        return shift, jnp.where(shift >= 0, 1, 0)

    def prepare(h, carry):
        m = lax.div(h, HALO // pair_of_atoms)
        for a in range(pair_of_atoms):
            atom = h * pair_of_atoms + a
            for k in range(NBR):
                index = lax.rem(atom, HALO) * NBR + k
                shift, later = window_of(m, index)
                base = shift + side * local_e - BAND // 2 - later * late
                weight = weights[m, pl.ds(index, 1), :]
                tile = pltpu.roll(jnp.broadcast_to(weight, (8, WINDOW)), WINDOW - BAND + 1 - base, 1)
                for step in (1, 2, 4):
                    tile = jnp.where((sub & step) != 0, pltpu.roll(tile, step, 1), tile)
                tiles = [tile] + [pltpu.roll(tile, 8 * b, 1) for b in range(1, WINDOW // 8)]
                band = jnp.concatenate(tiles, axis=0)
                turned_band = jnp.concatenate(tiles[SPAN // 8:] + tiles[:SPAN // 8], axis=0)
                toeplitz[atom * NBR + k, :WINDOW] = jnp.where(left_half, band, 0.0).astype(jnp.bfloat16)
                toeplitz[atom * NBR + k, WINDOW:] = jnp.where(left_half, 0.0, turned_band).astype(jnp.bfloat16)
            right = spread_r[pl.ds(pl.multiple_of(atom * 16, 16), 16), :]
            rights = (right[:8], jnp.concatenate([right[8:12], right[:4]], axis=0), right[4:12])
            for four in range(ORB // 4):
                rows = []
                for half in range(2):
                    p = four * 4 + half * 2
                    q0 = spread_q[pl.ds(atom * 16 + p, 1), :]
                    q1 = spread_q[pl.ds(atom * 16 + p + 1, 1), :]
                    rows += [q0 * rights[0], jnp.where(low_rows, q0, q1) * rights[1], q1 * rights[2]]
                both[atom, four * 48:(four + 1) * 48, :] = jnp.concatenate(rows, axis=0).astype(jnp.bfloat16)

        @pl.when(h < slots)
        def _():
            for step in range(inner):
                pl.when(comes(h, step))(lambda: incoming(h, step).wait_recv())
            pl.when(above)(lambda: relay(0, h).start())
            pl.when(below)(lambda: relay(1, h).start())
        return carry

    steps = mine * HALO // pair_of_atoms
    assert steps >= slots
    lax.fori_loop(0, steps, prepare, 0)

    unit = eye(128)

    def turn(slot, carry):
        pl.when(below)(lambda: relayed(0, slot).wait_recv())
        pl.when(above)(lambda: relayed(1, slot).wait_recv())
        if local_e % 16:
            for piece in range(pieces):
                stage[piece * local_e:(piece + 1) * local_e, :] = landed[slot, piece].astype(jnp.float32)
            tall = stage[...].astype(jnp.bfloat16)
        else:
            tall = landed[slot].reshape(rows_e, width)
        two = jnp.concatenate([tall[:WINDOW], tall[late:]], axis=0)
        turned = jnp.concatenate([
            lax.dot_general(unit, two[:, j * 128:(j + 1) * 128], NT, preferred_element_type=jnp.float32).astype(
                jnp.bfloat16) for j in range(width // 128)], axis=0)
        for atom in range(HALO):
            for c in range(2):
                start = (2 * atom + c) * PAIR
                for window in range(2):
                    green[window, slot * HALO + atom, :, c * WINDOW:(c + 1) * WINDOW] = (
                        turned[start:start + PAIR, window * WINDOW:(window + 1) * WINDOW])
        return carry

    lax.fori_loop(0, 2, turn, 0)

    def share(step, m, at):
        to = partner_of(i, step)
        return pltpu.make_async_remote_copy(
            src_ref=out_ref.at[to, m], dst_ref=back_ref.at[at * mine + m],
            send_sem=back_send.at[step, m], recv_sem=back_recv.at[step, m],
            device_id=(first_of_layer + to, slab), device_id_type=MESH)

    def chunk(m, carry):
        turn(m + 2, 0)
        for a in range(HALO):
            for k in range(NBR):
                index = a * NBR + k
                later = window_of(m, index)[1]
                partner = jnp.clip(numbers[m, 0, index] - first_atom, 0, slots * HALO - 1)
                banded = jnp.dot(
                    green[later, partner], toeplitz[m * HALO * NBR + index], preferred_element_type=jnp.float32)
                bands[a, k * PAIR:(k + 1) * PAIR, :] = banded.astype(jnp.bfloat16)
        parts = []
        for a in range(HALO):
            total = jnp.dot(both[m * HALO + a], bands[a], preferred_element_type=jnp.float32)
            turned = lax.dot_general(unit, total.astype(jnp.bfloat16), NT, preferred_element_type=jnp.float32)
            parts += [turned[:SPAN], turned[SPAN:]]
        whole = jnp.concatenate(parts, axis=1)
        for d in range(inner):
            out_ref[d, m] = whole[d * local_e:(d + 1) * local_e].astype(jnp.bfloat16)
        for step in range(1, inner):
            share(step, m, i).start()
        back_ref[i * mine + m] = out_ref[i, m]
        return carry

    lax.fori_loop(0, mine, chunk, 0)

    for j in range(layers):
        @pl.when(j * inner + owner != me)
        def _():
            for number in range(3):
                table(number, j, j, me).wait_send()

    def sent_slot(slot, carry):
        for step in range(inner):
            pl.when(leaves(slot, step))(lambda: outgoing(slot, step).wait_send())
        pl.when(above)(lambda: relay(0, slot).wait_send())
        pl.when(below)(lambda: relay(1, slot).wait_send())
        return carry

    lax.fori_loop(0, slots, sent_slot, 0)

    def finish(m, carry):
        for step in range(1, inner):
            share(step, m, partner_of(i, step)).wait_recv()
            share(step, m, i).wait_send()
        return carry

    lax.fori_loop(0, mine, finish, 0)


def on_device(green_blocks, couplings, band_weights, neighbours, shifts):
    groups = lax.axis_size("energy")
    local_e, slab_count = green_blocks.shape[3:]
    per_dev = slab_count // groups
    width = per_dev * BLOCK
    pairs = per_dev * NBR
    inner = SPAN // local_e
    layers = groups // inner
    side = pl.cdiv(REACH, local_e)
    pieces = inner + 2 * side
    mine = groups // inner
    slots = mine + 2
    assert per_dev == HALO and side <= inner and pieces * local_e >= WINDOW
    vmem = pl.BlockSpec(memory_space=pltpu.VMEM)
    smem = pl.BlockSpec(memory_space=pltpu.SMEM)
    blocks = jax.ShapeDtypeStruct((groups, local_e, width), jnp.bfloat16)
    wide = pltpu.VMEM((pl.cdiv(slab_count, 128), BLOCK * local_e, 128), jnp.float32)
    packed = pltpu.VMEM((width // 128, local_e * groups, 128), jnp.float32)
    room = pltpu.CompilerParams(vmem_limit_bytes=32 * 1024 * 1024)

    matrix = couplings.reshape(ORB, ORB, per_dev, NBR).transpose(2, 0, 3, 1).reshape(per_dev, ORB, NBR * ORB)
    matrix = jnp.pad(matrix, ((0, 0), (0, 16 - ORB), (0, 256 - NBR * ORB))).reshape(per_dev * 16, 256)
    weight = jnp.pad(band_weights.reshape(BAND, pairs)[::-1].T, ((0, 0), (0, WINDOW - BAND)))
    ints = jnp.pad(jnp.concatenate([neighbours, shifts], axis=0), ((0, 6), (0, 128 - pairs)))

    sent = pl.pallas_call(
        functools.partial(pack_kernel, groups, per_dev),
        out_shape=blocks, in_specs=[vmem], out_specs=vmem,
        scratch_shapes=[wide, packed], compiler_params=room,
    )(green_blocks.reshape(BLOCK * local_e, slab_count))

    back = pl.pallas_call(
        functools.partial(wire_kernel, inner, layers, side),
        out_shape=blocks,
        in_specs=[vmem] * 4,
        out_specs=vmem,
        scratch_shapes=[
            pltpu.VMEM((slots, pieces, local_e, width), jnp.bfloat16),
            pltpu.VMEM((layers,) + matrix.shape, jnp.bfloat16),
            pltpu.VMEM((layers,) + weight.shape, jnp.float32),
            pltpu.VMEM((layers,) + ints.shape, jnp.int32),
            pltpu.SMEM((layers,) + ints.shape, jnp.int32),
            pltpu.VMEM((inner, mine, local_e, width), jnp.bfloat16),
            pltpu.VMEM((2, slots * HALO, PAIR, 2 * WINDOW), jnp.bfloat16),
            pltpu.VMEM((mine * HALO * 16, NBR * PAIR), jnp.float32),
            pltpu.VMEM((mine * HALO * 16, NBR * PAIR), jnp.float32),
            pltpu.VMEM((mine * HALO, PAIR, NBR * PAIR), jnp.bfloat16),
            pltpu.VMEM((mine * HALO * NBR, 2 * WINDOW, WINDOW), jnp.bfloat16),
            pltpu.VMEM((HALO, NBR * PAIR, WINDOW), jnp.bfloat16),
            pltpu.VMEM((pieces * local_e, width), jnp.float32),
            pltpu.SemaphoreType.DMA((slots, inner)), pltpu.SemaphoreType.DMA((slots, inner)),
            pltpu.SemaphoreType.DMA((2, slots)), pltpu.SemaphoreType.DMA((2, slots)),
            pltpu.SemaphoreType.DMA((3, layers)), pltpu.SemaphoreType.DMA((3, layers)),
            pltpu.SemaphoreType.DMA((inner, mine)), pltpu.SemaphoreType.DMA((inner, mine)),
            pltpu.SemaphoreType.DMA,
        ],
        compiler_params=pltpu.CompilerParams(
            collective_id=0, has_side_effects=True, vmem_limit_bytes=56 * 1024 * 1024),
    )(sent, matrix, weight, ints)
    result = pl.pallas_call(
        functools.partial(unpack_kernel, groups, per_dev),
        out_shape=jax.ShapeDtypeStruct((BLOCK * local_e, slab_count), jnp.bfloat16),
        in_specs=[vmem], out_specs=vmem,
        scratch_shapes=[packed, wide], compiler_params=room,
    )(back)
    return result.reshape(2, ORB, ORB, local_e, slab_count)


def solution(mesh):
    return jax.shard_map(
        on_device,
        mesh=mesh,
        in_specs=(
            P(None, None, None, "energy", "slab"),
            P(None, None, "slab", "energy"),
            P(None, "slab", "energy"),
            P("slab", "energy"),
            P("slab", "energy"),
        ),
        out_specs=P(None, None, None, "energy", "slab"),
        check_vma=False,
    )
```

```python
import functools

import jax
import jax.numpy as jnp
from jax import lax
from jax.experimental import pallas as pl
from jax.experimental.pallas import tpu as pltpu
from jax.sharding import PartitionSpec as P

ORB = 12
NBR = 16
BAND = 9
SHIFT = 32
HALO = 4
BLOCK = 2 * ORB * ORB
PAIR = ORB * ORB
REACH = SHIFT + BAND // 2
SPAN = 64
WINDOW = 128

MESH = pl.DeviceIdType.MESH
NT = (((1,), (1,)), ((), ()))


def order(groups, per_dev):
    count = groups * per_dev
    row = lax.broadcasted_iota(jnp.int32, (count, count), 0)
    atom = lax.broadcasted_iota(jnp.int32, (count, count), 1)
    return (atom == (row % groups) * per_dev + row // groups).astype(jnp.bfloat16)


def eye(count):
    row = lax.broadcasted_iota(jnp.int32, (count, count), 0)
    column = lax.broadcasted_iota(jnp.int32, (count, count), 1)
    return (row == column).astype(jnp.bfloat16)


def partner_of(i, step):
    out, bit = 0, 1
    while bit <= step:
        out = out + bit * lax.rem(lax.div(i, bit) + step // bit, 2)
        bit *= 2
    return lax.div(i, bit) * bit + out if step else i


def pack_kernel(groups, per_dev, x_ref, sent, wide, packed):
    local_e = sent.shape[1]
    tiles = wide.shape[0]
    count = x_ref.shape[1]
    lanes = min(count, 128)
    if lanes < 128:
        wide[...] = jnp.zeros_like(wide)
    for j in range(tiles):
        wide[j, :x_ref.shape[0], :lanes] = x_ref[:, j * 128:j * 128 + lanes].astype(jnp.float32)
    pick = order(groups, per_dev)
    for e in range(local_e):
        rows = jnp.concatenate([wide[j, pl.ds(e, BLOCK, stride=local_e), :] for j in range(tiles)], axis=1)
        rows = rows[:, :count].astype(jnp.bfloat16)
        turned = lax.dot_general(pick, rows, NT, preferred_element_type=jnp.float32)
        flat = jnp.concatenate([turned[i * groups:(i + 1) * groups] for i in range(per_dev)], axis=1)
        for j in range(packed.shape[0]):
            packed[j, pl.ds(e, groups, stride=local_e), :] = flat[:, j * 128:(j + 1) * 128]
    for g in range(groups):
        for j in range(packed.shape[0]):
            sent[g, :, j * 128:(j + 1) * 128] = packed[j, g * local_e:(g + 1) * local_e, :].astype(jnp.bfloat16)


def unpack_kernel(groups, per_dev, landed, out_ref, wide, tall):
    local_e = landed.shape[1]
    lanes = min(out_ref.shape[1], 128)
    for g in range(groups):
        for j in range(wide.shape[0]):
            wide[j, g * local_e:(g + 1) * local_e, :] = landed[g, :, j * 128:(j + 1) * 128].astype(jnp.float32)
    pick = order(groups, per_dev)
    for e in range(local_e):
        rows = jnp.concatenate(
            [wide[j, pl.ds(e, groups, stride=local_e), :] for j in range(wide.shape[0])], axis=1)
        stack = jnp.concatenate([rows[:, i * BLOCK:(i + 1) * BLOCK] for i in range(per_dev)], axis=0)
        turned = jnp.dot(stack.T.astype(jnp.bfloat16), pick, preferred_element_type=jnp.float32)
        if lanes < 128:
            turned = jnp.concatenate([turned, jnp.zeros((BLOCK, 128 - lanes), jnp.float32)], axis=1)
        for j in range(tall.shape[0]):
            tall[j, pl.ds(e, BLOCK, stride=local_e), :] = turned[:, j * 128:(j + 1) * 128]
    for j in range(tall.shape[0]):
        out_ref[:, j * 128:j * 128 + lanes] = tall[j, :out_ref.shape[0], :lanes].astype(jnp.bfloat16)


def wire_kernel(inner, layers, side, sent, mats_in, weights_in, ints_in, back_ref,
                landed, mats, weights, ints, numbers, out_ref, green, spread_q, spread_r, both, toeplitz, bands, stage,
                slot_send, slot_recv, relay_send, relay_recv, table_send, table_recv, back_send, back_recv, local_sem):
    slots, pieces, local_e, width = landed.shape
    mine = slots - 2
    chunks = sent.shape[0]
    rows_e = pieces * local_e
    late = rows_e - WINDOW
    me, slab = lax.axis_index("energy"), lax.axis_index("slab")
    slabs = lax.axis_size("slab")
    layer, i = lax.div(me, inner), lax.rem(me, inner)
    first_of_layer = layer * inner
    first_atom = slab * (chunks * HALO) + i * (mine * HALO) - HALO
    first, last = i == 0, i == inner - 1
    below, above = layer > 0, layer < layers - 1
    slab_below, slab_above = slab > 0, slab < slabs - 1
    owner, spot = lax.div(me, layers), lax.rem(me, layers)
    barrier = pltpu.get_barrier_semaphore()
    one = lambda flag: jnp.where(flag, 1, 0)

    def hail(device, row):
        pl.semaphore_signal(barrier, inc=1, device_id=(device, row), device_id_type=MESH)

    for step in range(1, inner):
        hail(first_of_layer + partner_of(i, step), slab)

    @pl.when(first & slab_below)
    def _():
        for j in range(inner):
            hail(first_of_layer + j, slab - 1)

    @pl.when(last & slab_above)
    def _():
        for j in range(inner):
            hail(first_of_layer + j, slab + 1)

    pl.when(below)(lambda: hail(me - inner, slab))
    pl.when(above)(lambda: hail(me + inner, slab))
    for j in range(layers):
        pl.when(i * layers + j != me)(lambda: hail(i * layers + j, slab))
    pl.semaphore_wait(
        barrier, inner - 1 + one(slab_above) + one(slab_below) + one(above) + one(below) + layers - one(owner == i))

    tables = ((mats_in, mats), (weights_in, weights), (ints_in, ints))

    def table(number, j, at, to):
        src, dst = tables[number]
        return pltpu.make_async_remote_copy(
            src_ref=src, dst_ref=dst.at[at], send_sem=table_send.at[number, j], recv_sem=table_recv.at[number, at],
            device_id=(to, slab), device_id_type=MESH)

    for j in range(layers):
        to = j * inner + owner

        @pl.when(to != me)
        def _():
            for number in range(3):
                table(number, j, spot, to).start()

    def outgoing(slot, step):
        to = partner_of(i, step)
        row = slab + one((slot == 0) & (to == 0)) - one((slot == slots - 1) & (to == inner - 1))
        return pltpu.make_async_remote_copy(
            src_ref=sent.at[lax.rem(to * mine + slot - 1 + chunks, chunks)], dst_ref=landed.at[slot, side + i],
            send_sem=slot_send.at[slot, step], recv_sem=slot_recv.at[slot, step],
            device_id=(first_of_layer + to, row), device_id_type=MESH)

    def incoming(slot, step):
        source = partner_of(i, step)
        return pltpu.make_async_remote_copy(
            src_ref=sent.at[0], dst_ref=landed.at[slot, side + source],
            send_sem=slot_send.at[slot, step], recv_sem=slot_recv.at[slot, step],
            device_id=(first_of_layer + source, slab), device_id_type=MESH)

    def leaves(slot, step):
        to = partner_of(i, step)
        real = ((slot > 0) | (to > 0) | slab_above) & ((slot < slots - 1) | (to < inner - 1) | slab_below)
        if step:
            return real
        return real & (((slot == 0) & first) | ((slot == slots - 1) & last))

    def comes(slot, step):
        real = ((slot > 0) | (i > 0) | slab_below) & ((slot < slots - 1) | (i < inner - 1) | slab_above)
        if step:
            return real
        return real & (((slot == 0) & first) | ((slot == slots - 1) & last))

    def send_slot(slot, carry):
        for step in range(inner):
            pl.when(leaves(slot, step))(lambda: outgoing(slot, step).start())
        return carry

    lax.fori_loop(0, slots, send_slot, 0)

    landed[pl.ds(1, mine), side + i] = sent[pl.ds(i * mine, mine)]

    @pl.when(i > 0)
    def _():
        landed[0, side + i] = sent[lax.rem(i * mine - 1 + chunks, chunks)]

    @pl.when(i < inner - 1)
    def _():
        landed[slots - 1, side + i] = sent[lax.rem(i * mine + mine, chunks)]

    @pl.when(first & jnp.logical_not(slab_below))
    def _():
        landed[0, side:side + inner] = jnp.zeros((inner, local_e, width), landed.dtype)

    @pl.when(last & jnp.logical_not(slab_above))
    def _():
        landed[slots - 1, side:side + inner] = jnp.zeros((inner, local_e, width), landed.dtype)

    def clear(start):
        landed[:, start:start + side] = jnp.zeros((slots, side, local_e, width), landed.dtype)

    pl.when(jnp.logical_not(below))(lambda: clear(0))
    pl.when(jnp.logical_not(above))(lambda: clear(side + inner))

    @pl.when(owner == i)
    def _():
        for src, dst in tables:
            dst[spot] = src[...]

    for j in range(layers):
        @pl.when(i * layers + j != me)
        def _():
            for number in range(3):
                table(number, j, j, me).wait_recv()
    to_scalars = pltpu.make_async_copy(ints, numbers, local_sem)
    to_scalars.start()

    wide = NBR * PAIR
    lane = lax.broadcasted_iota(jnp.int32, (8, wide), 1)
    key_q = (lane // ORB)[:1]
    key_r = (lane // PAIR * ORB + lane % ORB)[:1]
    row = lax.broadcasted_iota(jnp.int32, (NBR * ORB, wide), 0)
    count = mats.shape[0] * mats.shape[1]
    matrices = mats[...].reshape(count, mats.shape[2])[:, :NBR * ORB]
    spread_q[...] = jnp.dot(matrices, (row == key_q).astype(jnp.bfloat16), preferred_element_type=jnp.float32)
    spread_r[...] = jnp.dot(matrices, (row == key_r).astype(jnp.bfloat16), preferred_element_type=jnp.float32)
    to_scalars.wait()

    def relay(way, slot):
        start, into = (inner, 0) if way == 0 else (side, side + inner)
        return pltpu.make_async_remote_copy(
            src_ref=landed.at[slot, start:start + side], dst_ref=landed.at[slot, into:into + side],
            send_sem=relay_send.at[way, slot], recv_sem=relay_recv.at[way, slot],
            device_id=(me + inner if way == 0 else me - inner, slab), device_id_type=MESH)

    def relayed(way, slot):
        into = 0 if way == 0 else side + inner
        return pltpu.make_async_remote_copy(
            src_ref=landed.at[slot, into:into + side], dst_ref=landed.at[slot, into:into + side],
            send_sem=relay_send.at[way, slot], recv_sem=relay_recv.at[way, slot],
            device_id=(me - inner if way == 0 else me + inner, slab), device_id_type=MESH)

    sub = lax.broadcasted_iota(jnp.int32, (8, WINDOW), 0)
    left_half = lax.broadcasted_iota(jnp.int32, (WINDOW, WINDOW), 1) < SPAN
    low_rows = lax.broadcasted_iota(jnp.int32, (8, wide), 0) < 4
    pair_of_atoms = 2
    zero = jnp.zeros((16, WINDOW), jnp.bfloat16)

    def window_of(m, index):
        shift = numbers[m, 1, index]
        return shift, jnp.where(shift >= 0, 1, 0)

    def prepare(h, carry):
        m = lax.div(h, HALO // pair_of_atoms)
        for a in range(pair_of_atoms):
            atom = h * pair_of_atoms + a
            tiles = []
            for k in range(NBR):
                index = lax.rem(atom, HALO) * NBR + k
                shift, later = window_of(m, index)
                base = shift + side * local_e - BAND // 2 - later * late
                weight = weights[m, pl.ds(index, 1), :]
                tiles.append(pltpu.roll(jnp.broadcast_to(weight, (8, WINDOW)), WINDOW - BAND + 1 - base, 1))
            for step in (1, 2, 4):
                tiles = [jnp.where((sub & step) != 0, pltpu.roll(tile, step, 1), tile) for tile in tiles]
            tiles = [jnp.concatenate([tile, pltpu.roll(tile, 8, 1)], axis=0).astype(jnp.bfloat16) for tile in tiles]
            for b in range(WINDOW // 16):
                for k in range(NBR):
                    tile = pltpu.roll(tiles[k], 16 * b, 1) if b else tiles[k]
                    toeplitz[atom * NBR + k, 16 * b:16 * b + 16] = jnp.where(left_half[:16], tile, zero)
                    low = WINDOW + (16 * b - SPAN) % WINDOW
                    toeplitz[atom * NBR + k, low:low + 16] = jnp.where(left_half[:16], zero, tile)
            right = spread_r[pl.ds(pl.multiple_of(atom * 16, 16), 16), :]
            rights = (right[:8], jnp.concatenate([right[8:12], right[:4]], axis=0), right[4:12])
            for four in range(ORB // 4):
                rows = []
                for half in range(2):
                    p = four * 4 + half * 2
                    q0 = spread_q[pl.ds(atom * 16 + p, 1), :]
                    q1 = spread_q[pl.ds(atom * 16 + p + 1, 1), :]
                    rows += [q0 * rights[0], jnp.where(low_rows, q0, q1) * rights[1], q1 * rights[2]]
                both[atom, four * 48:(four + 1) * 48, :] = jnp.concatenate(rows, axis=0).astype(jnp.bfloat16)

        @pl.when(h < slots)
        def _():
            for step in range(inner):
                pl.when(comes(h, step))(lambda: incoming(h, step).wait_recv())
            pl.when(above)(lambda: relay(0, h).start())
            pl.when(below)(lambda: relay(1, h).start())
        return carry

    steps = mine * HALO // pair_of_atoms
    assert steps >= slots
    lax.fori_loop(0, steps, prepare, 0)

    unit = eye(128)

    def turn(slot, carry):
        pl.when(below)(lambda: relayed(0, slot).wait_recv())
        pl.when(above)(lambda: relayed(1, slot).wait_recv())
        if local_e % 16:
            for piece in range(pieces):
                stage[piece * local_e:(piece + 1) * local_e, :] = landed[slot, piece].astype(jnp.float32)
            tall = stage[...].astype(jnp.bfloat16)
        else:
            tall = landed[slot].reshape(rows_e, width)
        two = jnp.concatenate([tall[:WINDOW], tall[late:]], axis=0)
        turned = jnp.concatenate([
            lax.dot_general(unit, two[:, j * 128:(j + 1) * 128], NT, preferred_element_type=jnp.float32).astype(
                jnp.bfloat16) for j in range(width // 128)], axis=0)
        for atom in range(HALO):
            for c in range(2):
                start = (2 * atom + c) * PAIR
                for window in range(2):
                    green[window, slot * HALO + atom, :, c * WINDOW:(c + 1) * WINDOW] = (
                        turned[start:start + PAIR, window * WINDOW:(window + 1) * WINDOW])
        return carry

    lax.fori_loop(0, 2, turn, 0)

    def share(step, m, at):
        to = partner_of(i, step)
        return pltpu.make_async_remote_copy(
            src_ref=out_ref.at[to, m], dst_ref=back_ref.at[at * mine + m],
            send_sem=back_send.at[step, m], recv_sem=back_recv.at[step, m],
            device_id=(first_of_layer + to, slab), device_id_type=MESH)

    def chunk(m, carry):
        turn(m + 2, 0)
        for a in range(HALO):
            for k in range(NBR):
                index = a * NBR + k
                later = window_of(m, index)[1]
                partner = jnp.clip(numbers[m, 0, index] - first_atom, 0, slots * HALO - 1)
                banded = jnp.dot(
                    green[later, partner], toeplitz[m * HALO * NBR + index], preferred_element_type=jnp.float32)
                bands[a, k * PAIR:(k + 1) * PAIR, :] = banded.astype(jnp.bfloat16)
        parts = []
        for a in range(HALO):
            total = jnp.dot(both[m * HALO + a], bands[a], preferred_element_type=jnp.float32)
            turned = lax.dot_general(unit, total.astype(jnp.bfloat16), NT, preferred_element_type=jnp.float32)
            parts += [turned[:SPAN], turned[SPAN:]]
        whole = jnp.concatenate(parts, axis=1)
        for d in range(inner):
            out_ref[d, m] = whole[d * local_e:(d + 1) * local_e].astype(jnp.bfloat16)
        for step in range(1, inner):
            share(step, m, i).start()
        back_ref[i * mine + m] = out_ref[i, m]
        return carry

    lax.fori_loop(0, mine, chunk, 0)

    for j in range(layers):
        @pl.when(j * inner + owner != me)
        def _():
            for number in range(3):
                table(number, j, j, me).wait_send()

    def sent_slot(slot, carry):
        for step in range(inner):
            pl.when(leaves(slot, step))(lambda: outgoing(slot, step).wait_send())
        pl.when(above)(lambda: relay(0, slot).wait_send())
        pl.when(below)(lambda: relay(1, slot).wait_send())
        return carry

    lax.fori_loop(0, slots, sent_slot, 0)

    def finish(m, carry):
        for step in range(1, inner):
            share(step, m, partner_of(i, step)).wait_recv()
            share(step, m, i).wait_send()
        return carry

    lax.fori_loop(0, mine, finish, 0)


def on_device(green_blocks, couplings, band_weights, neighbours, shifts):
    groups = lax.axis_size("energy")
    local_e, slab_count = green_blocks.shape[3:]
    per_dev = slab_count // groups
    width = per_dev * BLOCK
    pairs = per_dev * NBR
    inner = SPAN // local_e
    layers = groups // inner
    side = pl.cdiv(REACH, local_e)
    pieces = inner + 2 * side
    mine = groups // inner
    slots = mine + 2
    assert per_dev == HALO and side <= inner and pieces * local_e >= WINDOW
    vmem = pl.BlockSpec(memory_space=pltpu.VMEM)
    smem = pl.BlockSpec(memory_space=pltpu.SMEM)
    blocks = jax.ShapeDtypeStruct((groups, local_e, width), jnp.bfloat16)
    wide = pltpu.VMEM((pl.cdiv(slab_count, 128), BLOCK * local_e, 128), jnp.float32)
    packed = pltpu.VMEM((width // 128, local_e * groups, 128), jnp.float32)
    room = pltpu.CompilerParams(vmem_limit_bytes=32 * 1024 * 1024)

    matrix = couplings.reshape(ORB, ORB, per_dev, NBR).transpose(2, 0, 3, 1).reshape(per_dev, ORB, NBR * ORB)
    matrix = jnp.pad(matrix, ((0, 0), (0, 16 - ORB), (0, 256 - NBR * ORB))).reshape(per_dev * 16, 256)
    weight = jnp.pad(band_weights.reshape(BAND, pairs)[::-1].T, ((0, 0), (0, WINDOW - BAND)))
    ints = jnp.pad(jnp.concatenate([neighbours, shifts], axis=0), ((0, 6), (0, 128 - pairs)))

    sent = pl.pallas_call(
        functools.partial(pack_kernel, groups, per_dev),
        out_shape=blocks, in_specs=[vmem], out_specs=vmem,
        scratch_shapes=[wide, packed], compiler_params=room,
    )(green_blocks.reshape(BLOCK * local_e, slab_count))

    back = pl.pallas_call(
        functools.partial(wire_kernel, inner, layers, side),
        out_shape=blocks,
        in_specs=[vmem] * 4,
        out_specs=vmem,
        scratch_shapes=[
            pltpu.VMEM((slots, pieces, local_e, width), jnp.bfloat16),
            pltpu.VMEM((layers,) + matrix.shape, jnp.bfloat16),
            pltpu.VMEM((layers,) + weight.shape, jnp.float32),
            pltpu.VMEM((layers,) + ints.shape, jnp.int32),
            pltpu.SMEM((layers,) + ints.shape, jnp.int32),
            pltpu.VMEM((inner, mine, local_e, width), jnp.bfloat16),
            pltpu.VMEM((2, slots * HALO, PAIR, 2 * WINDOW), jnp.bfloat16),
            pltpu.VMEM((mine * HALO * 16, NBR * PAIR), jnp.float32),
            pltpu.VMEM((mine * HALO * 16, NBR * PAIR), jnp.float32),
            pltpu.VMEM((mine * HALO, PAIR, NBR * PAIR), jnp.bfloat16),
            pltpu.VMEM((mine * HALO * NBR, 2 * WINDOW, WINDOW), jnp.bfloat16),
            pltpu.VMEM((HALO, NBR * PAIR, WINDOW), jnp.bfloat16),
            pltpu.VMEM((pieces * local_e, width), jnp.float32),
            pltpu.SemaphoreType.DMA((slots, inner)), pltpu.SemaphoreType.DMA((slots, inner)),
            pltpu.SemaphoreType.DMA((2, slots)), pltpu.SemaphoreType.DMA((2, slots)),
            pltpu.SemaphoreType.DMA((3, layers)), pltpu.SemaphoreType.DMA((3, layers)),
            pltpu.SemaphoreType.DMA((inner, mine)), pltpu.SemaphoreType.DMA((inner, mine)),
            pltpu.SemaphoreType.DMA,
        ],
        compiler_params=pltpu.CompilerParams(
            collective_id=0, has_side_effects=True, vmem_limit_bytes=56 * 1024 * 1024),
    )(sent, matrix, weight, ints)
    result = pl.pallas_call(
        functools.partial(unpack_kernel, groups, per_dev),
        out_shape=jax.ShapeDtypeStruct((BLOCK * local_e, slab_count), jnp.bfloat16),
        in_specs=[vmem], out_specs=vmem,
        scratch_shapes=[packed, wide], compiler_params=room,
    )(back)
    return result.reshape(2, ORB, ORB, local_e, slab_count)


def solution(mesh):
    return jax.shard_map(
        on_device,
        mesh=mesh,
        in_specs=(
            P(None, None, None, "energy", "slab"),
            P(None, None, "slab", "energy"),
            P(None, "slab", "energy"),
            P("slab", "energy"),
            P("slab", "energy"),
        ),
        out_specs=P(None, None, None, "energy", "slab"),
        check_vma=False,
    )
```

```python
import functools

import jax
import jax.numpy as jnp
from jax import lax
from jax.experimental import pallas as pl
from jax.experimental.pallas import tpu as pltpu
from jax.sharding import PartitionSpec as P

ORB = 12
NBR = 16
BAND = 9
SHIFT = 32
HALO = 4
BLOCK = 2 * ORB * ORB
PAIR = ORB * ORB
REACH = SHIFT + BAND // 2
SPAN = 64
WINDOW = 128

MESH = pl.DeviceIdType.MESH
NT = (((1,), (1,)), ((), ()))


def order(groups, per_dev):
    count = groups * per_dev
    row = lax.broadcasted_iota(jnp.int32, (count, count), 0)
    atom = lax.broadcasted_iota(jnp.int32, (count, count), 1)
    return (atom == (row % groups) * per_dev + row // groups).astype(jnp.bfloat16)


def eye(count):
    row = lax.broadcasted_iota(jnp.int32, (count, count), 0)
    column = lax.broadcasted_iota(jnp.int32, (count, count), 1)
    return (row == column).astype(jnp.bfloat16)


def partner_of(i, step):
    out, bit = 0, 1
    while bit <= step:
        out = out + bit * lax.rem(lax.div(i, bit) + step // bit, 2)
        bit *= 2
    return lax.div(i, bit) * bit + out if step else i


def pack_kernel(groups, per_dev, x_ref, sent, wide, packed):
    local_e = sent.shape[1]
    tiles = wide.shape[0]
    count = x_ref.shape[1]
    lanes = min(count, 128)
    if lanes < 128:
        wide[...] = jnp.zeros_like(wide)
    for j in range(tiles):
        wide[j, :x_ref.shape[0], :lanes] = x_ref[:, j * 128:j * 128 + lanes].astype(jnp.float32)
    pick = order(groups, per_dev)
    for e in range(local_e):
        rows = jnp.concatenate([wide[j, pl.ds(e, BLOCK, stride=local_e), :] for j in range(tiles)], axis=1)
        rows = rows[:, :count].astype(jnp.bfloat16)
        turned = lax.dot_general(pick, rows, NT, preferred_element_type=jnp.float32)
        flat = jnp.concatenate([turned[i * groups:(i + 1) * groups] for i in range(per_dev)], axis=1)
        for j in range(packed.shape[0]):
            packed[j, pl.ds(e, groups, stride=local_e), :] = flat[:, j * 128:(j + 1) * 128]
    for g in range(groups):
        for j in range(packed.shape[0]):
            sent[g, :, j * 128:(j + 1) * 128] = packed[j, g * local_e:(g + 1) * local_e, :].astype(jnp.bfloat16)


def unpack_kernel(groups, per_dev, landed, out_ref, wide, tall):
    local_e = landed.shape[1]
    lanes = min(out_ref.shape[1], 128)
    for g in range(groups):
        for j in range(wide.shape[0]):
            wide[j, g * local_e:(g + 1) * local_e, :] = landed[g, :, j * 128:(j + 1) * 128].astype(jnp.float32)
    pick = order(groups, per_dev)
    for e in range(local_e):
        rows = jnp.concatenate(
            [wide[j, pl.ds(e, groups, stride=local_e), :] for j in range(wide.shape[0])], axis=1)
        stack = jnp.concatenate([rows[:, i * BLOCK:(i + 1) * BLOCK] for i in range(per_dev)], axis=0)
        turned = jnp.dot(stack.T.astype(jnp.bfloat16), pick, preferred_element_type=jnp.float32)
        if lanes < 128:
            turned = jnp.concatenate([turned, jnp.zeros((BLOCK, 128 - lanes), jnp.float32)], axis=1)
        for j in range(tall.shape[0]):
            tall[j, pl.ds(e, BLOCK, stride=local_e), :] = turned[:, j * 128:(j + 1) * 128]
    for j in range(tall.shape[0]):
        out_ref[:, j * 128:j * 128 + lanes] = tall[j, :out_ref.shape[0], :lanes].astype(jnp.bfloat16)


def table_tall(padded, weight_rows, mats_in):
    pairs = padded.shape[2]
    atoms, lanes = pairs // NBR, mats_in.shape[1]
    wide = atoms * lanes
    tall = padded[...].reshape(ORB * 16, pairs).astype(jnp.bfloat16)
    lane = lax.broadcasted_iota(jnp.int32, (8, wide), 1)[:1]
    inside = lane % lanes
    pair_of = jnp.where(inside < NBR * ORB, lane // lanes * NBR + inside // ORB, -1)
    row = lax.broadcasted_iota(jnp.int32, (pairs, wide), 0)
    spread = jnp.dot(tall, (row == pair_of).astype(jnp.bfloat16), preferred_element_type=jnp.float32)
    row = lax.broadcasted_iota(jnp.int32, (ORB * 16, wide), 0) % 16
    spread = jnp.where(row == inside % ORB, spread, 0.0).astype(jnp.bfloat16)
    p = lax.broadcasted_iota(jnp.int32, (16, ORB * 16), 0)
    of = lax.broadcasted_iota(jnp.int32, (16, ORB * 16), 1) // 16
    flat = jnp.dot((p == of).astype(jnp.bfloat16), spread, preferred_element_type=jnp.float32)
    at = lax.broadcasted_iota(jnp.int32, (pairs, lanes), 1) - NBR * ORB
    pair = lax.broadcasted_iota(jnp.int32, (pairs, lanes), 0)
    behind = jnp.dot(
        weight_rows[...].astype(jnp.bfloat16), (at == pair).astype(jnp.bfloat16), preferred_element_type=jnp.float32)
    for atom in range(atoms):
        block = flat[:, atom * lanes:(atom + 1) * lanes]
        mats_in[atom * 16:(atom + 1) * 16, :] = (block + behind if atom == 0 else block).astype(jnp.bfloat16)


def wire_kernel(inner, layers, side, x_ref, coupling_ref, weight_ref, near_ref, shift_ref, back_ref,
                packed_wide, packed, sent, padded, weight_rows, mats_in,
                landed, mats, weights, near, shifts, near_at, shift_at,
                out_ref, green, spread_q, spread_r, both, toeplitz, bands, stage,
                slot_send, slot_recv, relay_send, relay_recv, table_send, table_recv, back_send, back_recv, local_sem):
    slots, pieces, local_e, width = landed.shape
    mine = slots - 2
    chunks = sent.shape[0]
    rows_e = pieces * local_e
    late = rows_e - WINDOW
    me, slab = lax.axis_index("energy"), lax.axis_index("slab")
    slabs = lax.axis_size("slab")
    layer, i = lax.div(me, inner), lax.rem(me, inner)
    first_of_layer = layer * inner
    first_atom = slab * (chunks * HALO) + i * (mine * HALO) - HALO
    first, last = i == 0, i == inner - 1
    below, above = layer > 0, layer < layers - 1
    slab_below, slab_above = slab > 0, slab < slabs - 1
    owner, spot = lax.div(me, layers), lax.rem(me, layers)
    barrier = pltpu.get_barrier_semaphore()
    one = lambda flag: jnp.where(flag, 1, 0)

    def hail(device, row):
        pl.semaphore_signal(barrier, inc=1, device_id=(device, row), device_id_type=MESH)

    for step in range(1, inner):
        hail(first_of_layer + partner_of(i, step), slab)

    @pl.when(first & slab_below)
    def _():
        for j in range(inner):
            hail(first_of_layer + j, slab - 1)

    @pl.when(last & slab_above)
    def _():
        for j in range(inner):
            hail(first_of_layer + j, slab + 1)

    pl.when(below)(lambda: hail(me - inner, slab))
    pl.when(above)(lambda: hail(me + inner, slab))
    for j in range(layers):
        pl.when(i * layers + j != me)(lambda: hail(i * layers + j, slab))
    pack_kernel(chunks, HALO, x_ref, sent, packed_wide, packed)
    padded[...] = jnp.zeros_like(padded)
    weight_rows[...] = jnp.zeros_like(weight_rows)
    for p in range(ORB):
        padded[p, :ORB, :] = coupling_ref[p].astype(jnp.float32)
    weight_rows[:BAND, :] = weight_ref[:, 0, :]
    table_tall(padded, weight_rows, mats_in)

    landed[pl.ds(1, mine), side + i] = sent[pl.ds(i * mine, mine)]

    @pl.when(i > 0)
    def _():
        landed[0, side + i] = sent[lax.rem(i * mine - 1 + chunks, chunks)]

    @pl.when(i < inner - 1)
    def _():
        landed[slots - 1, side + i] = sent[lax.rem(i * mine + mine, chunks)]

    @pl.when(first & jnp.logical_not(slab_below))
    def _():
        landed[0, side:side + inner] = jnp.zeros((inner, local_e, width), landed.dtype)

    @pl.when(last & jnp.logical_not(slab_above))
    def _():
        landed[slots - 1, side:side + inner] = jnp.zeros((inner, local_e, width), landed.dtype)

    def clear(start):
        landed[:, start:start + side] = jnp.zeros((slots, side, local_e, width), landed.dtype)

    pl.when(jnp.logical_not(below))(lambda: clear(0))
    pl.when(jnp.logical_not(above))(lambda: clear(side + inner))

    tables = ((mats_in, mats), (near_ref, near), (shift_ref, shifts))

    @pl.when(owner == i)
    def _():
        for src, dst in tables:
            dst[spot] = src[...]

    pl.semaphore_wait(
        barrier, inner - 1 + one(slab_above) + one(slab_below) + one(above) + one(below) + layers - one(owner == i))

    def table(number, j, at, to):
        src, dst = tables[number]
        return pltpu.make_async_remote_copy(
            src_ref=src, dst_ref=dst.at[at], send_sem=table_send.at[number, j], recv_sem=table_recv.at[number, at],
            device_id=(to, slab), device_id_type=MESH)

    def outgoing(slot, step):
        to = partner_of(i, step)
        row = slab + one((slot == 0) & (to == 0)) - one((slot == slots - 1) & (to == inner - 1))
        return pltpu.make_async_remote_copy(
            src_ref=sent.at[lax.rem(to * mine + slot - 1 + chunks, chunks)], dst_ref=landed.at[slot, side + i],
            send_sem=slot_send.at[slot, step], recv_sem=slot_recv.at[slot, step],
            device_id=(first_of_layer + to, row), device_id_type=MESH)

    def incoming(slot, step):
        source = partner_of(i, step)
        return pltpu.make_async_remote_copy(
            src_ref=sent.at[0], dst_ref=landed.at[slot, side + source],
            send_sem=slot_send.at[slot, step], recv_sem=slot_recv.at[slot, step],
            device_id=(first_of_layer + source, slab), device_id_type=MESH)

    def leaves(slot, step):
        to = partner_of(i, step)
        real = ((slot > 0) | (to > 0) | slab_above) & ((slot < slots - 1) | (to < inner - 1) | slab_below)
        if step:
            return real
        return real & (((slot == 0) & first) | ((slot == slots - 1) & last))

    def comes(slot, step):
        real = ((slot > 0) | (i > 0) | slab_below) & ((slot < slots - 1) | (i < inner - 1) | slab_above)
        if step:
            return real
        return real & (((slot == 0) & first) | ((slot == slots - 1) & last))

    def send_slot(slot, carry):
        for step in range(inner):
            pl.when(leaves(slot, step))(lambda: outgoing(slot, step).start())
        return carry

    lax.fori_loop(0, 3, send_slot, 0)
    for j in range(layers):
        to = j * inner + owner

        @pl.when(to != me)
        def _():
            for number in range(3):
                table(number, j, spot, to).start()

    lax.fori_loop(3, slots, send_slot, 0)

    def relay(way, slot):
        start, into = (inner, 0) if way == 0 else (side, side + inner)
        return pltpu.make_async_remote_copy(
            src_ref=landed.at[slot, start:start + side], dst_ref=landed.at[slot, into:into + side],
            send_sem=relay_send.at[way, slot], recv_sem=relay_recv.at[way, slot],
            device_id=(me + inner if way == 0 else me - inner, slab), device_id_type=MESH)

    def relayed(way, slot):
        into = 0 if way == 0 else side + inner
        return pltpu.make_async_remote_copy(
            src_ref=landed.at[slot, into:into + side], dst_ref=landed.at[slot, into:into + side],
            send_sem=relay_send.at[way, slot], recv_sem=relay_recv.at[way, slot],
            device_id=(me - inner if way == 0 else me + inner, slab), device_id_type=MESH)

    def pass_on(slot):
        for step in range(inner):
            pl.when(comes(slot, step))(lambda: incoming(slot, step).wait_recv())
        pl.when(above)(lambda: relay(0, slot).start())
        pl.when(below)(lambda: relay(1, slot).start())

    pass_on(0)
    for j in range(layers):
        @pl.when(i * layers + j != me)
        def _():
            for number in range(3):
                table(number, j, j, me).wait_recv()
    to_scalars = (pltpu.make_async_copy(near, near_at, local_sem.at[0]),
                  pltpu.make_async_copy(shifts, shift_at, local_sem.at[1]))
    for copy in to_scalars:
        copy.start()
    lane_of = lax.broadcasted_iota(jnp.int32, (16, WINDOW), 1)
    row_of = lax.broadcasted_iota(jnp.int32, (16, WINDOW), 0)
    place = ((lane_of + row_of == BAND - 1) & (row_of < BAND)).astype(jnp.bfloat16)
    count_pairs = mats.shape[2] - NBR * ORB
    for j in range(layers):
        column = lax.dot_general(
            eye(count_pairs), mats[j, :16, NBR * ORB:], NT, preferred_element_type=jnp.float32).astype(jnp.bfloat16)
        weights[j] = jnp.dot(column, place, preferred_element_type=jnp.float32)

    wide = NBR * PAIR
    lane = lax.broadcasted_iota(jnp.int32, (8, wide), 1)
    key_q = (lane // ORB)[:1]
    key_r = (lane // PAIR * ORB + lane % ORB)[:1]
    row = lax.broadcasted_iota(jnp.int32, (NBR * ORB, wide), 0)
    count = mats.shape[0] * mats.shape[1]
    matrices = mats[...].reshape(count, mats.shape[2])[:, :NBR * ORB]
    spread_q[...] = jnp.dot(matrices, (row == key_q).astype(jnp.bfloat16), preferred_element_type=jnp.float32)
    pass_on(1)
    spread_r[...] = jnp.dot(matrices, (row == key_r).astype(jnp.bfloat16), preferred_element_type=jnp.float32)
    for copy in to_scalars:
        copy.wait()
    pass_on(2)

    sub = lax.broadcasted_iota(jnp.int32, (8, WINDOW), 0)
    left_half = lax.broadcasted_iota(jnp.int32, (WINDOW, WINDOW), 1) < SPAN
    low_rows = lax.broadcasted_iota(jnp.int32, (8, wide), 0) < 4
    pair_of_atoms = 2
    zero = jnp.zeros((16, WINDOW), jnp.bfloat16)

    def window_of(m, index):
        shift = shift_at[m, 0, index]
        return shift, jnp.where(shift >= 0, 1, 0)

    def prepare(h, carry):
        m = lax.div(h, HALO // pair_of_atoms)
        for a in range(pair_of_atoms):
            atom = h * pair_of_atoms + a
            tiles = []
            for k in range(NBR):
                index = lax.rem(atom, HALO) * NBR + k
                shift, later = window_of(m, index)
                base = shift + side * local_e - BAND // 2 - later * late
                weight = weights[m, pl.ds(index, 1), :]
                tiles.append(pltpu.roll(jnp.broadcast_to(weight, (8, WINDOW)), WINDOW - BAND + 1 - base, 1))
            for step in (1, 2, 4):
                tiles = [jnp.where((sub & step) != 0, pltpu.roll(tile, step, 1), tile) for tile in tiles]
            tiles = [jnp.concatenate([tile, pltpu.roll(tile, 8, 1)], axis=0).astype(jnp.bfloat16) for tile in tiles]
            for b in range(WINDOW // 16):
                for k in range(NBR):
                    tile = pltpu.roll(tiles[k], 16 * b, 1) if b else tiles[k]
                    toeplitz[atom * NBR + k, 16 * b:16 * b + 16] = jnp.where(left_half[:16], tile, zero)
                    low = WINDOW + (16 * b - SPAN) % WINDOW
                    toeplitz[atom * NBR + k, low:low + 16] = jnp.where(left_half[:16], zero, tile)
            right = spread_r[pl.ds(pl.multiple_of(atom * 16, 16), 16), :]
            rights = (right[:8], jnp.concatenate([right[8:12], right[:4]], axis=0), right[4:12])
            for four in range(ORB // 4):
                rows = []
                for half in range(2):
                    p = four * 4 + half * 2
                    q0 = spread_q[pl.ds(atom * 16 + p, 1), :]
                    q1 = spread_q[pl.ds(atom * 16 + p + 1, 1), :]
                    rows += [q0 * rights[0], jnp.where(low_rows, q0, q1) * rights[1], q1 * rights[2]]
                both[atom, four * 48:(four + 1) * 48, :] = jnp.concatenate(rows, axis=0).astype(jnp.bfloat16)

        pl.when(h < slots - 3)(lambda: pass_on(h + 3))
        return carry

    steps = mine * HALO // pair_of_atoms
    assert steps >= slots
    lax.fori_loop(0, steps, prepare, 0)

    unit = eye(128)

    def turn(slot, carry):
        pl.when(below)(lambda: relayed(0, slot).wait_recv())
        pl.when(above)(lambda: relayed(1, slot).wait_recv())
        if local_e % 16:
            for piece in range(pieces):
                stage[piece * local_e:(piece + 1) * local_e, :] = landed[slot, piece].astype(jnp.float32)
            tall = stage[...].astype(jnp.bfloat16)
        else:
            tall = landed[slot].reshape(rows_e, width)
        two = jnp.concatenate([tall[:WINDOW], tall[late:]], axis=0)
        turned = jnp.concatenate([
            lax.dot_general(unit, two[:, j * 128:(j + 1) * 128], NT, preferred_element_type=jnp.float32).astype(
                jnp.bfloat16) for j in range(width // 128)], axis=0)
        for atom in range(HALO):
            for c in range(2):
                start = (2 * atom + c) * PAIR
                for window in range(2):
                    green[window, slot * HALO + atom, :, c * WINDOW:(c + 1) * WINDOW] = (
                        turned[start:start + PAIR, window * WINDOW:(window + 1) * WINDOW])
        return carry

    lax.fori_loop(0, 2, turn, 0)

    def share(step, m, at):
        to = partner_of(i, step)
        return pltpu.make_async_remote_copy(
            src_ref=out_ref.at[to, m], dst_ref=back_ref.at[at * mine + m],
            send_sem=back_send.at[step, m], recv_sem=back_recv.at[step, m],
            device_id=(first_of_layer + to, slab), device_id_type=MESH)

    def chunk(m, carry):
        turn(m + 2, 0)
        for a in range(HALO):
            for k in range(NBR):
                index = a * NBR + k
                later = window_of(m, index)[1]
                partner = jnp.clip(near_at[m, 0, index] - first_atom, 0, slots * HALO - 1)
                banded = jnp.dot(
                    green[later, partner], toeplitz[m * HALO * NBR + index], preferred_element_type=jnp.float32)
                bands[a, k * PAIR:(k + 1) * PAIR, :] = banded.astype(jnp.bfloat16)
        parts = []
        for a in range(HALO):
            total = jnp.dot(both[m * HALO + a], bands[a], preferred_element_type=jnp.float32)
            turned = lax.dot_general(unit, total.astype(jnp.bfloat16), NT, preferred_element_type=jnp.float32)
            parts += [turned[:SPAN], turned[SPAN:]]
        whole = jnp.concatenate(parts, axis=1)
        for d in range(inner):
            out_ref[d, m] = whole[d * local_e:(d + 1) * local_e].astype(jnp.bfloat16)
        for step in range(1, inner):
            share(step, m, i).start()
        back_ref[i * mine + m] = out_ref[i, m]
        return carry

    lax.fori_loop(0, mine, chunk, 0)

    for j in range(layers):
        @pl.when(j * inner + owner != me)
        def _():
            for number in range(3):
                table(number, j, j, me).wait_send()

    def sent_slot(slot, carry):
        for step in range(inner):
            pl.when(leaves(slot, step))(lambda: outgoing(slot, step).wait_send())
        pl.when(above)(lambda: relay(0, slot).wait_send())
        pl.when(below)(lambda: relay(1, slot).wait_send())
        return carry

    lax.fori_loop(0, slots, sent_slot, 0)

    def finish(m, carry):
        for step in range(1, inner):
            share(step, m, partner_of(i, step)).wait_recv()
            share(step, m, i).wait_send()
        return carry

    lax.fori_loop(0, mine, finish, 0)


def on_device(green_blocks, couplings, band_weights, neighbours, shifts):
    groups = lax.axis_size("energy")
    local_e, slab_count = green_blocks.shape[3:]
    per_dev = slab_count // groups
    width = per_dev * BLOCK
    pairs = per_dev * NBR
    lanes = NBR * ORB + pairs
    inner = SPAN // local_e
    layers = groups // inner
    side = pl.cdiv(REACH, local_e)
    pieces = inner + 2 * side
    mine = groups // inner
    slots = mine + 2
    assert per_dev == HALO and side <= inner and pieces * local_e >= WINDOW
    vmem = pl.BlockSpec(memory_space=pltpu.VMEM)
    smem = pl.BlockSpec(memory_space=pltpu.SMEM)
    blocks = jax.ShapeDtypeStruct((groups, local_e, width), jnp.bfloat16)
    wide = pltpu.VMEM((pl.cdiv(slab_count, 128), BLOCK * local_e, 128), jnp.float32)
    packed = pltpu.VMEM((width // 128, local_e * groups, 128), jnp.float32)
    room = pltpu.CompilerParams(vmem_limit_bytes=32 * 1024 * 1024)

    back = pl.pallas_call(
        functools.partial(wire_kernel, inner, layers, side),
        out_shape=blocks,
        in_specs=[vmem] * 5,
        out_specs=vmem,
        scratch_shapes=[
            wide, packed, pltpu.VMEM(blocks.shape, jnp.bfloat16),
            pltpu.VMEM((ORB, 16, pairs), jnp.float32), pltpu.VMEM((16, pairs), jnp.float32),
            pltpu.VMEM((per_dev * 16, lanes), jnp.bfloat16),
            pltpu.VMEM((slots, pieces, local_e, width), jnp.bfloat16),
            pltpu.VMEM((layers, per_dev * 16, lanes), jnp.bfloat16),
            pltpu.VMEM((layers, pairs, WINDOW), jnp.float32),
            pltpu.VMEM((layers, 1, pairs), jnp.int32),
            pltpu.VMEM((layers, 1, pairs), jnp.int32),
            pltpu.SMEM((layers, 1, pairs), jnp.int32),
            pltpu.SMEM((layers, 1, pairs), jnp.int32),
            pltpu.VMEM((inner, mine, local_e, width), jnp.bfloat16),
            pltpu.VMEM((2, slots * HALO, PAIR, 2 * WINDOW), jnp.bfloat16),
            pltpu.VMEM((mine * HALO * 16, NBR * PAIR), jnp.float32),
            pltpu.VMEM((mine * HALO * 16, NBR * PAIR), jnp.float32),
            pltpu.VMEM((mine * HALO, PAIR, NBR * PAIR), jnp.bfloat16),
            pltpu.VMEM((mine * HALO * NBR, 2 * WINDOW, WINDOW), jnp.bfloat16),
            pltpu.VMEM((HALO, NBR * PAIR, WINDOW), jnp.bfloat16),
            pltpu.VMEM((pieces * local_e if local_e % 16 else 8, width), jnp.float32),
            pltpu.SemaphoreType.DMA((slots, inner)), pltpu.SemaphoreType.DMA((slots, inner)),
            pltpu.SemaphoreType.DMA((2, slots)), pltpu.SemaphoreType.DMA((2, slots)),
            pltpu.SemaphoreType.DMA((3, layers)), pltpu.SemaphoreType.DMA((3, layers)),
            pltpu.SemaphoreType.DMA((inner, mine)), pltpu.SemaphoreType.DMA((inner, mine)),
            pltpu.SemaphoreType.DMA((2,)),
        ],
        compiler_params=pltpu.CompilerParams(
            collective_id=0, has_side_effects=True, vmem_limit_bytes=48 * 1024 * 1024),
    )(green_blocks.reshape(BLOCK * local_e, slab_count), couplings.reshape(ORB, ORB, pairs), band_weights, neighbours, shifts)
    result = pl.pallas_call(
        functools.partial(unpack_kernel, groups, per_dev),
        out_shape=jax.ShapeDtypeStruct((BLOCK * local_e, slab_count), jnp.bfloat16),
        in_specs=[vmem], out_specs=vmem,
        scratch_shapes=[packed, wide], compiler_params=room,
    )(back)
    return result.reshape(2, ORB, ORB, local_e, slab_count)


def solution(mesh):
    return jax.shard_map(
        on_device,
        mesh=mesh,
        in_specs=(
            P(None, None, None, "energy", "slab"),
            P(None, None, "slab", "energy"),
            P(None, "slab", "energy"),
            P("slab", "energy"),
            P("slab", "energy"),
        ),
        out_specs=P(None, None, None, "energy", "slab"),
        check_vma=False,
    )
```

```python
import functools

import jax
import jax.numpy as jnp
from jax import lax
from jax.experimental import pallas as pl
from jax.experimental.pallas import tpu as pltpu
from jax.sharding import PartitionSpec as P

ORB = 12
NBR = 16
BAND = 9
SHIFT = 32
HALO = 4
BLOCK = 2 * ORB * ORB
PAIR = ORB * ORB
REACH = SHIFT + BAND // 2
SPAN = 64
WINDOW = 128

MESH = pl.DeviceIdType.MESH
NT = (((1,), (1,)), ((), ()))


def order(groups, per_dev):
    count = groups * per_dev
    row = lax.broadcasted_iota(jnp.int32, (count, count), 0)
    atom = lax.broadcasted_iota(jnp.int32, (count, count), 1)
    return (atom == (row % groups) * per_dev + row // groups).astype(jnp.bfloat16)


def eye(count):
    row = lax.broadcasted_iota(jnp.int32, (count, count), 0)
    column = lax.broadcasted_iota(jnp.int32, (count, count), 1)
    return (row == column).astype(jnp.bfloat16)


def partner_of(i, step):
    out, bit = 0, 1
    while bit <= step:
        out = out + bit * lax.rem(lax.div(i, bit) + step // bit, 2)
        bit *= 2
    return lax.div(i, bit) * bit + out if step else i


def pack_kernel(groups, per_dev, x_ref, sent, wide, packed):
    local_e = sent.shape[1]
    tiles = wide.shape[0]
    count = x_ref.shape[1]
    lanes = min(count, 128)
    if lanes < 128:
        wide[...] = jnp.zeros_like(wide)
    for j in range(tiles):
        wide[j, :x_ref.shape[0], :lanes] = x_ref[:, j * 128:j * 128 + lanes].astype(jnp.float32)
    pick = order(groups, per_dev)
    for e in range(local_e):
        rows = jnp.concatenate([wide[j, pl.ds(e, BLOCK, stride=local_e), :] for j in range(tiles)], axis=1)
        rows = rows[:, :count].astype(jnp.bfloat16)
        turned = lax.dot_general(pick, rows, NT, preferred_element_type=jnp.float32)
        flat = jnp.concatenate([turned[i * groups:(i + 1) * groups] for i in range(per_dev)], axis=1)
        for j in range(packed.shape[0]):
            packed[j, pl.ds(e, groups, stride=local_e), :] = flat[:, j * 128:(j + 1) * 128]
    for g in range(groups):
        for j in range(packed.shape[0]):
            sent[g, :, j * 128:(j + 1) * 128] = packed[j, g * local_e:(g + 1) * local_e, :].astype(jnp.bfloat16)


def unpack_kernel(groups, per_dev, landed, out_ref, wide, tall):
    local_e = landed.shape[1]
    lanes = min(out_ref.shape[1], 128)
    for g in range(groups):
        for j in range(wide.shape[0]):
            wide[j, g * local_e:(g + 1) * local_e, :] = landed[g, :, j * 128:(j + 1) * 128].astype(jnp.float32)
    pick = order(groups, per_dev)
    for e in range(local_e):
        rows = jnp.concatenate(
            [wide[j, pl.ds(e, groups, stride=local_e), :] for j in range(wide.shape[0])], axis=1)
        stack = jnp.concatenate([rows[:, i * BLOCK:(i + 1) * BLOCK] for i in range(per_dev)], axis=0)
        turned = jnp.dot(stack.T.astype(jnp.bfloat16), pick, preferred_element_type=jnp.float32)
        if lanes < 128:
            turned = jnp.concatenate([turned, jnp.zeros((BLOCK, 128 - lanes), jnp.float32)], axis=1)
        for j in range(tall.shape[0]):
            tall[j, pl.ds(e, BLOCK, stride=local_e), :] = turned[:, j * 128:(j + 1) * 128]
    for j in range(tall.shape[0]):
        out_ref[:, j * 128:j * 128 + lanes] = tall[j, :out_ref.shape[0], :lanes].astype(jnp.bfloat16)


def table_tall(padded, weight_rows, mats_in):
    pairs = padded.shape[2]
    atoms, lanes = pairs // NBR, mats_in.shape[1]
    wide = atoms * lanes
    tall = padded[...].reshape(ORB * 16, pairs).astype(jnp.bfloat16)
    lane = lax.broadcasted_iota(jnp.int32, (8, wide), 1)[:1]
    inside = lane % lanes
    pair_of = jnp.where(inside < NBR * ORB, lane // lanes * NBR + inside // ORB, -1)
    row = lax.broadcasted_iota(jnp.int32, (pairs, wide), 0)
    spread = jnp.dot(tall, (row == pair_of).astype(jnp.bfloat16), preferred_element_type=jnp.float32)
    row = lax.broadcasted_iota(jnp.int32, (ORB * 16, wide), 0) % 16
    spread = jnp.where(row == inside % ORB, spread, 0.0).astype(jnp.bfloat16)
    p = lax.broadcasted_iota(jnp.int32, (16, ORB * 16), 0)
    of = lax.broadcasted_iota(jnp.int32, (16, ORB * 16), 1) // 16
    flat = jnp.dot((p == of).astype(jnp.bfloat16), spread, preferred_element_type=jnp.float32)
    at = lax.broadcasted_iota(jnp.int32, (pairs, lanes), 1) - NBR * ORB
    pair = lax.broadcasted_iota(jnp.int32, (pairs, lanes), 0)
    behind = jnp.dot(
        weight_rows[...].astype(jnp.bfloat16), (at == pair).astype(jnp.bfloat16), preferred_element_type=jnp.float32)
    for atom in range(atoms):
        block = flat[:, atom * lanes:(atom + 1) * lanes]
        mats_in[atom * 16:(atom + 1) * 16, :] = (block + behind if atom == 0 else block).astype(jnp.bfloat16)


def wire_kernel(inner, layers, side, sent, coupling_ref, weight_ref, near_ref, shift_ref, back_ref,
                padded, weight_rows, mats_in,
                landed, mats, weights, near, shifts, near_at, shift_at, pick_q, pick_r,
                out_ref, green, spread_q, spread_r, both, toeplitz, bands, stage,
                slot_send, slot_recv, relay_send, relay_recv, table_send, table_recv, back_send, back_recv, local_sem):
    slots, pieces, local_e, width = landed.shape
    mine = slots - 2
    chunks = sent.shape[0]
    rows_e = pieces * local_e
    late = rows_e - WINDOW
    me, slab = lax.axis_index("energy"), lax.axis_index("slab")
    slabs = lax.axis_size("slab")
    layer, i = lax.div(me, inner), lax.rem(me, inner)
    first_of_layer = layer * inner
    first_atom = slab * (chunks * HALO) + i * (mine * HALO) - HALO
    first, last = i == 0, i == inner - 1
    below, above = layer > 0, layer < layers - 1
    slab_below, slab_above = slab > 0, slab < slabs - 1
    owner, spot = lax.div(me, layers), lax.rem(me, layers)
    barrier = pltpu.get_barrier_semaphore()
    one = lambda flag: jnp.where(flag, 1, 0)

    def hail(device, row):
        pl.semaphore_signal(barrier, inc=1, device_id=(device, row), device_id_type=MESH)

    for step in range(1, inner):
        hail(first_of_layer + partner_of(i, step), slab)

    @pl.when(first & slab_below)
    def _():
        for j in range(inner):
            hail(first_of_layer + j, slab - 1)

    @pl.when(last & slab_above)
    def _():
        for j in range(inner):
            hail(first_of_layer + j, slab + 1)

    pl.when(below)(lambda: hail(me - inner, slab))
    pl.when(above)(lambda: hail(me + inner, slab))
    for j in range(layers):
        pl.when(i * layers + j != me)(lambda: hail(i * layers + j, slab))
    padded[...] = jnp.zeros_like(padded)
    weight_rows[...] = jnp.zeros_like(weight_rows)
    for p in range(ORB):
        padded[p, :ORB, :] = coupling_ref[p].astype(jnp.float32)
    weight_rows[:BAND, :] = weight_ref[:, 0, :]
    table_tall(padded, weight_rows, mats_in)

    landed[pl.ds(1, mine), side + i] = sent[pl.ds(i * mine, mine)]

    @pl.when(i > 0)
    def _():
        landed[0, side + i] = sent[lax.rem(i * mine - 1 + chunks, chunks)]

    @pl.when(i < inner - 1)
    def _():
        landed[slots - 1, side + i] = sent[lax.rem(i * mine + mine, chunks)]

    @pl.when(first & jnp.logical_not(slab_below))
    def _():
        landed[0, side:side + inner] = jnp.zeros((inner, local_e, width), landed.dtype)

    @pl.when(last & jnp.logical_not(slab_above))
    def _():
        landed[slots - 1, side:side + inner] = jnp.zeros((inner, local_e, width), landed.dtype)

    def clear(start):
        landed[:, start:start + side] = jnp.zeros((slots, side, local_e, width), landed.dtype)

    pl.when(jnp.logical_not(below))(lambda: clear(0))
    pl.when(jnp.logical_not(above))(lambda: clear(side + inner))

    tables = ((mats_in, mats), (near_ref, near), (shift_ref, shifts))

    @pl.when(owner == i)
    def _():
        for src, dst in tables:
            dst[spot] = src[...]

    pl.semaphore_wait(
        barrier, inner - 1 + one(slab_above) + one(slab_below) + one(above) + one(below) + layers - one(owner == i))

    def table(number, j, at, to):
        src, dst = tables[number]
        return pltpu.make_async_remote_copy(
            src_ref=src, dst_ref=dst.at[at], send_sem=table_send.at[number, j], recv_sem=table_recv.at[number, at],
            device_id=(to, slab), device_id_type=MESH)

    def outgoing(slot, step):
        to = partner_of(i, step)
        row = slab + one((slot == 0) & (to == 0)) - one((slot == slots - 1) & (to == inner - 1))
        return pltpu.make_async_remote_copy(
            src_ref=sent.at[lax.rem(to * mine + slot - 1 + chunks, chunks)], dst_ref=landed.at[slot, side + i],
            send_sem=slot_send.at[slot, step], recv_sem=slot_recv.at[slot, step],
            device_id=(first_of_layer + to, row), device_id_type=MESH)

    def incoming(slot, step):
        source = partner_of(i, step)
        return pltpu.make_async_remote_copy(
            src_ref=sent.at[0], dst_ref=landed.at[slot, side + source],
            send_sem=slot_send.at[slot, step], recv_sem=slot_recv.at[slot, step],
            device_id=(first_of_layer + source, slab), device_id_type=MESH)

    def leaves(slot, step):
        to = partner_of(i, step)
        real = ((slot > 0) | (to > 0) | slab_above) & ((slot < slots - 1) | (to < inner - 1) | slab_below)
        if step:
            return real
        return real & (((slot == 0) & first) | ((slot == slots - 1) & last))

    def comes(slot, step):
        real = ((slot > 0) | (i > 0) | slab_below) & ((slot < slots - 1) | (i < inner - 1) | slab_above)
        if step:
            return real
        return real & (((slot == 0) & first) | ((slot == slots - 1) & last))

    def send_slot(slot, carry):
        for step in range(inner):
            pl.when(leaves(slot, step))(lambda: outgoing(slot, step).start())
        return carry

    lax.fori_loop(0, 3, send_slot, 0)
    for j in range(layers):
        to = j * inner + owner

        @pl.when(to != me)
        def _():
            for number in range(3):
                table(number, j, spot, to).start()

    wide = NBR * PAIR
    lane = lax.broadcasted_iota(jnp.int32, (8, wide), 1)
    key_q = (lane // ORB)[:1]
    key_r = (lane // PAIR * ORB + lane % ORB)[:1]
    row = lax.broadcasted_iota(jnp.int32, (NBR * ORB, wide), 0)
    pick_q[...] = (row == key_q).astype(jnp.bfloat16)
    pick_r[...] = (row == key_r).astype(jnp.bfloat16)

    def relay(way, slot):
        start, into = (inner, 0) if way == 0 else (side, side + inner)
        return pltpu.make_async_remote_copy(
            src_ref=landed.at[slot, start:start + side], dst_ref=landed.at[slot, into:into + side],
            send_sem=relay_send.at[way, slot], recv_sem=relay_recv.at[way, slot],
            device_id=(me + inner if way == 0 else me - inner, slab), device_id_type=MESH)

    def relayed(way, slot):
        into = 0 if way == 0 else side + inner
        return pltpu.make_async_remote_copy(
            src_ref=landed.at[slot, into:into + side], dst_ref=landed.at[slot, into:into + side],
            send_sem=relay_send.at[way, slot], recv_sem=relay_recv.at[way, slot],
            device_id=(me - inner if way == 0 else me + inner, slab), device_id_type=MESH)

    def pass_on(slot):
        for step in range(inner):
            pl.when(comes(slot, step))(lambda: incoming(slot, step).wait_recv())
        pl.when(above)(lambda: relay(0, slot).start())
        pl.when(below)(lambda: relay(1, slot).start())

    pass_on(0)
    send_slot(3, 0)
    for j in range(layers):
        @pl.when(i * layers + j != me)
        def _():
            for number in range(3):
                table(number, j, j, me).wait_recv()
    to_scalars = (pltpu.make_async_copy(near, near_at, local_sem.at[0]),
                  pltpu.make_async_copy(shifts, shift_at, local_sem.at[1]))
    for copy in to_scalars:
        copy.start()
    lane_of = lax.broadcasted_iota(jnp.int32, (16, WINDOW), 1)
    row_of = lax.broadcasted_iota(jnp.int32, (16, WINDOW), 0)
    place = ((lane_of + row_of == BAND - 1) & (row_of < BAND)).astype(jnp.bfloat16)
    count_pairs = mats.shape[2] - NBR * ORB
    for j in range(layers):
        column = lax.dot_general(
            eye(count_pairs), mats[j, :16, NBR * ORB:], NT, preferred_element_type=jnp.float32).astype(jnp.bfloat16)
        weights[j] = jnp.dot(column, place, preferred_element_type=jnp.float32)

    count = mats.shape[0] * mats.shape[1]
    matrices = mats[...].reshape(count, mats.shape[2])[:, :NBR * ORB]
    spread_q[...] = jnp.dot(matrices, pick_q[...], preferred_element_type=jnp.float32)
    pass_on(1)
    send_slot(4, 0)
    spread_r[...] = jnp.dot(matrices, pick_r[...], preferred_element_type=jnp.float32)
    for copy in to_scalars:
        copy.wait()
    pass_on(2)
    send_slot(5, 0)

    sub = lax.broadcasted_iota(jnp.int32, (8, WINDOW), 0)
    left_half = lax.broadcasted_iota(jnp.int32, (WINDOW, WINDOW), 1) < SPAN
    low_rows = lax.broadcasted_iota(jnp.int32, (8, wide), 0) < 4
    pair_of_atoms = 2
    zero = jnp.zeros((16, WINDOW), jnp.bfloat16)

    def window_of(m, index):
        shift = shift_at[m, 0, index]
        return shift, jnp.where(shift >= 0, 1, 0)

    def prepare(h, carry):
        m = lax.div(h, HALO // pair_of_atoms)
        for a in range(pair_of_atoms):
            atom = h * pair_of_atoms + a
            tiles = []
            for k in range(NBR):
                index = lax.rem(atom, HALO) * NBR + k
                shift, later = window_of(m, index)
                base = shift + side * local_e - BAND // 2 - later * late
                weight = weights[m, pl.ds(index, 1), :]
                tiles.append(pltpu.roll(jnp.broadcast_to(weight, (8, WINDOW)), WINDOW - BAND + 1 - base, 1))
            for step in (1, 2, 4):
                tiles = [jnp.where((sub & step) != 0, pltpu.roll(tile, step, 1), tile) for tile in tiles]
            tiles = [jnp.concatenate([tile, pltpu.roll(tile, 8, 1)], axis=0).astype(jnp.bfloat16) for tile in tiles]
            for b in range(WINDOW // 16):
                for k in range(NBR):
                    tile = pltpu.roll(tiles[k], 16 * b, 1) if b else tiles[k]
                    toeplitz[atom * NBR + k, 16 * b:16 * b + 16] = jnp.where(left_half[:16], tile, zero)
                    low = WINDOW + (16 * b - SPAN) % WINDOW
                    toeplitz[atom * NBR + k, low:low + 16] = jnp.where(left_half[:16], zero, tile)
            right = spread_r[pl.ds(pl.multiple_of(atom * 16, 16), 16), :]
            rights = (right[:8], jnp.concatenate([right[8:12], right[:4]], axis=0), right[4:12])
            for four in range(ORB // 4):
                rows = []
                for half in range(2):
                    p = four * 4 + half * 2
                    q0 = spread_q[pl.ds(atom * 16 + p, 1), :]
                    q1 = spread_q[pl.ds(atom * 16 + p + 1, 1), :]
                    rows += [q0 * rights[0], jnp.where(low_rows, q0, q1) * rights[1], q1 * rights[2]]
                both[atom, four * 48:(four + 1) * 48, :] = jnp.concatenate(rows, axis=0).astype(jnp.bfloat16)

        pl.when((h % 2 == 1) & (h < 6))(lambda: pass_on(lax.div(h, 2) + 3))
        return carry

    steps = mine * HALO // pair_of_atoms
    assert slots == 6 and steps >= slots
    lax.fori_loop(0, steps, prepare, 0)

    unit = eye(128)

    def turn(slot, carry):
        pl.when(below)(lambda: relayed(0, slot).wait_recv())
        pl.when(above)(lambda: relayed(1, slot).wait_recv())
        if local_e % 16:
            for piece in range(pieces):
                stage[piece * local_e:(piece + 1) * local_e, :] = landed[slot, piece].astype(jnp.float32)
            tall = stage[...].astype(jnp.bfloat16)
        else:
            tall = landed[slot].reshape(rows_e, width)
        two = jnp.concatenate([tall[:WINDOW], tall[late:]], axis=0)
        turned = jnp.concatenate([
            lax.dot_general(unit, two[:, j * 128:(j + 1) * 128], NT, preferred_element_type=jnp.float32).astype(
                jnp.bfloat16) for j in range(width // 128)], axis=0)
        for atom in range(HALO):
            for c in range(2):
                start = (2 * atom + c) * PAIR
                for window in range(2):
                    green[window, slot * HALO + atom, :, c * WINDOW:(c + 1) * WINDOW] = (
                        turned[start:start + PAIR, window * WINDOW:(window + 1) * WINDOW])
        return carry

    lax.fori_loop(0, 2, turn, 0)

    def share(step, m, at):
        to = partner_of(i, step)
        return pltpu.make_async_remote_copy(
            src_ref=out_ref.at[to, m], dst_ref=back_ref.at[at * mine + m],
            send_sem=back_send.at[step, m], recv_sem=back_recv.at[step, m],
            device_id=(first_of_layer + to, slab), device_id_type=MESH)

    def chunk(m, carry):
        turn(m + 2, 0)
        for a in range(HALO):
            for k in range(NBR):
                index = a * NBR + k
                later = window_of(m, index)[1]
                partner = jnp.clip(near_at[m, 0, index] - first_atom, 0, slots * HALO - 1)
                banded = jnp.dot(
                    green[later, partner], toeplitz[m * HALO * NBR + index], preferred_element_type=jnp.float32)
                bands[a, k * PAIR:(k + 1) * PAIR, :] = banded.astype(jnp.bfloat16)
        parts = []
        for a in range(HALO):
            total = jnp.dot(both[m * HALO + a], bands[a], preferred_element_type=jnp.float32)
            turned = lax.dot_general(unit, total.astype(jnp.bfloat16), NT, preferred_element_type=jnp.float32)
            parts += [turned[:SPAN], turned[SPAN:]]
        whole = jnp.concatenate(parts, axis=1)
        for d in range(inner):
            out_ref[d, m] = whole[d * local_e:(d + 1) * local_e].astype(jnp.bfloat16)
        for step in range(1, inner):
            share(step, m, i).start()
        back_ref[i * mine + m] = out_ref[i, m]
        return carry

    lax.fori_loop(0, mine, chunk, 0)

    for j in range(layers):
        @pl.when(j * inner + owner != me)
        def _():
            for number in range(3):
                table(number, j, j, me).wait_send()

    def sent_slot(slot, carry):
        for step in range(inner):
            pl.when(leaves(slot, step))(lambda: outgoing(slot, step).wait_send())
        pl.when(above)(lambda: relay(0, slot).wait_send())
        pl.when(below)(lambda: relay(1, slot).wait_send())
        return carry

    lax.fori_loop(0, slots, sent_slot, 0)

    def finish(m, carry):
        for step in range(1, inner):
            share(step, m, partner_of(i, step)).wait_recv()
            share(step, m, i).wait_send()
        return carry

    lax.fori_loop(0, mine, finish, 0)


def on_device(green_blocks, couplings, band_weights, neighbours, shifts):
    groups = lax.axis_size("energy")
    local_e, slab_count = green_blocks.shape[3:]
    per_dev = slab_count // groups
    width = per_dev * BLOCK
    pairs = per_dev * NBR
    lanes = NBR * ORB + pairs
    inner = SPAN // local_e
    layers = groups // inner
    side = pl.cdiv(REACH, local_e)
    pieces = inner + 2 * side
    mine = groups // inner
    slots = mine + 2
    assert per_dev == HALO and side <= inner and pieces * local_e >= WINDOW
    vmem = pl.BlockSpec(memory_space=pltpu.VMEM)
    smem = pl.BlockSpec(memory_space=pltpu.SMEM)
    blocks = jax.ShapeDtypeStruct((groups, local_e, width), jnp.bfloat16)
    wide = pltpu.VMEM((pl.cdiv(slab_count, 128), BLOCK * local_e, 128), jnp.float32)
    packed = pltpu.VMEM((width // 128, local_e * groups, 128), jnp.float32)
    room = pltpu.CompilerParams(vmem_limit_bytes=32 * 1024 * 1024)

    sent = pl.pallas_call(
        functools.partial(pack_kernel, groups, per_dev),
        out_shape=blocks, in_specs=[vmem], out_specs=vmem,
        scratch_shapes=[wide, packed], compiler_params=room,
    )(green_blocks.reshape(BLOCK * local_e, slab_count))
    back = pl.pallas_call(
        functools.partial(wire_kernel, inner, layers, side),
        out_shape=blocks,
        in_specs=[vmem] * 5,
        out_specs=vmem,
        scratch_shapes=[
            pltpu.VMEM((ORB, 16, pairs), jnp.float32), pltpu.VMEM((16, pairs), jnp.float32),
            pltpu.VMEM((per_dev * 16, lanes), jnp.bfloat16),
            pltpu.VMEM((slots, pieces, local_e, width), jnp.bfloat16),
            pltpu.VMEM((layers, per_dev * 16, lanes), jnp.bfloat16),
            pltpu.VMEM((layers, pairs, WINDOW), jnp.float32),
            pltpu.VMEM((layers, 1, pairs), jnp.int32),
            pltpu.VMEM((layers, 1, pairs), jnp.int32),
            pltpu.SMEM((layers, 1, pairs), jnp.int32),
            pltpu.SMEM((layers, 1, pairs), jnp.int32),
            pltpu.VMEM((NBR * ORB, NBR * PAIR), jnp.bfloat16), pltpu.VMEM((NBR * ORB, NBR * PAIR), jnp.bfloat16),
            pltpu.VMEM((inner, mine, local_e, width), jnp.bfloat16),
            pltpu.VMEM((2, slots * HALO, PAIR, 2 * WINDOW), jnp.bfloat16),
            pltpu.VMEM((mine * HALO * 16, NBR * PAIR), jnp.float32),
            pltpu.VMEM((mine * HALO * 16, NBR * PAIR), jnp.float32),
            pltpu.VMEM((mine * HALO, PAIR, NBR * PAIR), jnp.bfloat16),
            pltpu.VMEM((mine * HALO * NBR, 2 * WINDOW, WINDOW), jnp.bfloat16),
            pltpu.VMEM((HALO, NBR * PAIR, WINDOW), jnp.bfloat16),
            pltpu.VMEM((pieces * local_e if local_e % 16 else 8, width), jnp.float32),
            pltpu.SemaphoreType.DMA((slots, inner)), pltpu.SemaphoreType.DMA((slots, inner)),
            pltpu.SemaphoreType.DMA((2, slots)), pltpu.SemaphoreType.DMA((2, slots)),
            pltpu.SemaphoreType.DMA((3, layers)), pltpu.SemaphoreType.DMA((3, layers)),
            pltpu.SemaphoreType.DMA((inner, mine)), pltpu.SemaphoreType.DMA((inner, mine)),
            pltpu.SemaphoreType.DMA((2,)),
        ],
        compiler_params=pltpu.CompilerParams(
            collective_id=0, has_side_effects=True, vmem_limit_bytes=48 * 1024 * 1024),
    )(sent, couplings.reshape(ORB, ORB, pairs), band_weights, neighbours, shifts)
    result = pl.pallas_call(
        functools.partial(unpack_kernel, groups, per_dev),
        out_shape=jax.ShapeDtypeStruct((BLOCK * local_e, slab_count), jnp.bfloat16),
        in_specs=[vmem], out_specs=vmem,
        scratch_shapes=[packed, wide], compiler_params=room,
    )(back)
    return result.reshape(2, ORB, ORB, local_e, slab_count)


def solution(mesh):
    return jax.shard_map(
        on_device,
        mesh=mesh,
        in_specs=(
            P(None, None, None, "energy", "slab"),
            P(None, None, "slab", "energy"),
            P(None, "slab", "energy"),
            P("slab", "energy"),
            P("slab", "energy"),
        ),
        out_specs=P(None, None, None, "energy", "slab"),
        check_vma=False,
    )
```

```python
import functools

import jax
import jax.numpy as jnp
from jax import lax
from jax.experimental import pallas as pl
from jax.experimental.pallas import tpu as pltpu
from jax.sharding import PartitionSpec as P

ORB = 12
NBR = 16
BAND = 9
SHIFT = 32
HALO = 4
BLOCK = 2 * ORB * ORB
PAIR = ORB * ORB
REACH = SHIFT + BAND // 2
SPAN = 64
WINDOW = 128

MESH = pl.DeviceIdType.MESH
NT = (((1,), (1,)), ((), ()))


def order(groups, per_dev):
    count = groups * per_dev
    row = lax.broadcasted_iota(jnp.int32, (count, count), 0)
    atom = lax.broadcasted_iota(jnp.int32, (count, count), 1)
    return (atom == (row % groups) * per_dev + row // groups).astype(jnp.bfloat16)


def eye(count):
    row = lax.broadcasted_iota(jnp.int32, (count, count), 0)
    column = lax.broadcasted_iota(jnp.int32, (count, count), 1)
    return (row == column).astype(jnp.bfloat16)


def partner_of(i, step):
    out, bit = 0, 1
    while bit <= step:
        out = out + bit * lax.rem(lax.div(i, bit) + step // bit, 2)
        bit *= 2
    return lax.div(i, bit) * bit + out if step else i


def pack_kernel(groups, per_dev, x_ref, sent, wide, packed):
    local_e = sent.shape[1]
    tiles = wide.shape[0]
    count = x_ref.shape[1]
    lanes = min(count, 128)
    if lanes < 128:
        wide[...] = jnp.zeros_like(wide)
    for j in range(tiles):
        wide[j, :x_ref.shape[0], :lanes] = x_ref[:, j * 128:j * 128 + lanes].astype(jnp.float32)
    pick = order(groups, per_dev)
    for e in range(local_e):
        rows = jnp.concatenate([wide[j, pl.ds(e, BLOCK, stride=local_e), :] for j in range(tiles)], axis=1)
        rows = rows[:, :count].astype(jnp.bfloat16)
        turned = lax.dot_general(pick, rows, NT, preferred_element_type=jnp.float32)
        flat = jnp.concatenate([turned[i * groups:(i + 1) * groups] for i in range(per_dev)], axis=1)
        for j in range(packed.shape[0]):
            packed[j, pl.ds(e, groups, stride=local_e), :] = flat[:, j * 128:(j + 1) * 128]
    for g in range(groups):
        for j in range(packed.shape[0]):
            sent[g, :, j * 128:(j + 1) * 128] = packed[j, g * local_e:(g + 1) * local_e, :].astype(jnp.bfloat16)


def unpack_kernel(groups, per_dev, landed, out_ref, wide, tall):
    local_e = landed.shape[1]
    lanes = min(out_ref.shape[1], 128)
    for g in range(groups):
        for j in range(wide.shape[0]):
            wide[j, g * local_e:(g + 1) * local_e, :] = landed[g, :, j * 128:(j + 1) * 128].astype(jnp.float32)
    pick = order(groups, per_dev)
    for e in range(local_e):
        rows = jnp.concatenate(
            [wide[j, pl.ds(e, groups, stride=local_e), :] for j in range(wide.shape[0])], axis=1)
        stack = jnp.concatenate([rows[:, i * BLOCK:(i + 1) * BLOCK] for i in range(per_dev)], axis=0)
        turned = jnp.dot(stack.T.astype(jnp.bfloat16), pick, preferred_element_type=jnp.float32)
        if lanes < 128:
            turned = jnp.concatenate([turned, jnp.zeros((BLOCK, 128 - lanes), jnp.float32)], axis=1)
        for j in range(tall.shape[0]):
            tall[j, pl.ds(e, BLOCK, stride=local_e), :] = turned[:, j * 128:(j + 1) * 128]
    for j in range(tall.shape[0]):
        out_ref[:, j * 128:j * 128 + lanes] = tall[j, :out_ref.shape[0], :lanes].astype(jnp.bfloat16)


def table_tall(padded, weight_rows, mats_in):
    pairs = padded.shape[2]
    atoms, lanes = pairs // NBR, mats_in.shape[1]
    wide = atoms * lanes
    tall = padded[...].reshape(ORB * 16, pairs).astype(jnp.bfloat16)
    lane = lax.broadcasted_iota(jnp.int32, (8, wide), 1)[:1]
    inside = lane % lanes
    pair_of = jnp.where(inside < NBR * ORB, lane // lanes * NBR + inside // ORB, -1)
    row = lax.broadcasted_iota(jnp.int32, (pairs, wide), 0)
    spread = jnp.dot(tall, (row == pair_of).astype(jnp.bfloat16), preferred_element_type=jnp.float32)
    row = lax.broadcasted_iota(jnp.int32, (ORB * 16, wide), 0) % 16
    spread = jnp.where(row == inside % ORB, spread, 0.0).astype(jnp.bfloat16)
    p = lax.broadcasted_iota(jnp.int32, (16, ORB * 16), 0)
    of = lax.broadcasted_iota(jnp.int32, (16, ORB * 16), 1) // 16
    flat = jnp.dot((p == of).astype(jnp.bfloat16), spread, preferred_element_type=jnp.float32)
    at = lax.broadcasted_iota(jnp.int32, (pairs, lanes), 1) - NBR * ORB
    pair = lax.broadcasted_iota(jnp.int32, (pairs, lanes), 0)
    behind = jnp.dot(
        weight_rows[...].astype(jnp.bfloat16), (at == pair).astype(jnp.bfloat16), preferred_element_type=jnp.float32)
    for atom in range(atoms):
        block = flat[:, atom * lanes:(atom + 1) * lanes]
        mats_in[atom * 16:(atom + 1) * 16, :] = (block + behind if atom == 0 else block).astype(jnp.bfloat16)


def wire_kernel(inner, layers, side, sent, coupling_ref, weight_ref, near_ref, shift_ref, back_ref,
                padded, weight_rows, mats_in,
                landed, mats, weights, near, shifts, near_at, shift_at, pick_q, pick_r,
                out_ref, green, spread_q, spread_r, both, toeplitz, bands, stage,
                slot_send, slot_recv, relay_send, relay_recv, table_send, table_recv, back_send, back_recv, local_sem):
    slots, pieces, local_e, width = landed.shape
    mine = slots - 2
    chunks = sent.shape[0]
    rows_e = pieces * local_e
    late = rows_e - WINDOW
    me, slab = lax.axis_index("energy"), lax.axis_index("slab")
    slabs = lax.axis_size("slab")
    layer, i = lax.div(me, inner), lax.rem(me, inner)
    first_of_layer = layer * inner
    first_atom = slab * (chunks * HALO) + i * (mine * HALO) - HALO
    first, last = i == 0, i == inner - 1
    below, above = layer > 0, layer < layers - 1
    slab_below, slab_above = slab > 0, slab < slabs - 1
    owner, spot = lax.div(me, layers), lax.rem(me, layers)
    barrier = pltpu.get_barrier_semaphore()
    one = lambda flag: jnp.where(flag, 1, 0)

    def hail(device, row):
        pl.semaphore_signal(barrier, inc=1, device_id=(device, row), device_id_type=MESH)

    for step in range(1, inner):
        hail(first_of_layer + partner_of(i, step), slab)

    @pl.when(first & slab_below)
    def _():
        for j in range(inner):
            hail(first_of_layer + j, slab - 1)

    @pl.when(last & slab_above)
    def _():
        for j in range(inner):
            hail(first_of_layer + j, slab + 1)

    pl.when(below)(lambda: hail(me - inner, slab))
    pl.when(above)(lambda: hail(me + inner, slab))
    for j in range(layers):
        pl.when(i * layers + j != me)(lambda: hail(i * layers + j, slab))
    padded[...] = jnp.zeros_like(padded)
    weight_rows[...] = jnp.zeros_like(weight_rows)
    for p in range(ORB):
        padded[p, :ORB, :] = coupling_ref[p].astype(jnp.float32)
    weight_rows[:BAND, :] = weight_ref[:, 0, :]
    table_tall(padded, weight_rows, mats_in)

    landed[pl.ds(1, mine), side + i] = sent[pl.ds(i * mine, mine)]

    @pl.when(i > 0)
    def _():
        landed[0, side + i] = sent[lax.rem(i * mine - 1 + chunks, chunks)]

    @pl.when(i < inner - 1)
    def _():
        landed[slots - 1, side + i] = sent[lax.rem(i * mine + mine, chunks)]

    @pl.when(first & jnp.logical_not(slab_below))
    def _():
        landed[0, side:side + inner] = jnp.zeros((inner, local_e, width), landed.dtype)

    @pl.when(last & jnp.logical_not(slab_above))
    def _():
        landed[slots - 1, side:side + inner] = jnp.zeros((inner, local_e, width), landed.dtype)

    def clear(start):
        landed[:, start:start + side] = jnp.zeros((slots, side, local_e, width), landed.dtype)

    pl.when(jnp.logical_not(below))(lambda: clear(0))
    pl.when(jnp.logical_not(above))(lambda: clear(side + inner))

    tables = ((mats_in, mats), (near_ref, near), (shift_ref, shifts))

    @pl.when(owner == i)
    def _():
        for src, dst in tables:
            dst[spot] = src[...]

    pl.semaphore_wait(
        barrier, inner - 1 + one(slab_above) + one(slab_below) + one(above) + one(below) + layers - one(owner == i))

    def table(number, j, at, to):
        src, dst = tables[number]
        return pltpu.make_async_remote_copy(
            src_ref=src, dst_ref=dst.at[at], send_sem=table_send.at[number, j], recv_sem=table_recv.at[number, at],
            device_id=(to, slab), device_id_type=MESH)

    def outgoing(slot, step):
        to = partner_of(i, step)
        row = slab + one((slot == 0) & (to == 0)) - one((slot == slots - 1) & (to == inner - 1))
        return pltpu.make_async_remote_copy(
            src_ref=sent.at[lax.rem(to * mine + slot - 1 + chunks, chunks)], dst_ref=landed.at[slot, side + i],
            send_sem=slot_send.at[slot, step], recv_sem=slot_recv.at[slot, step],
            device_id=(first_of_layer + to, row), device_id_type=MESH)

    def incoming(slot, step):
        source = partner_of(i, step)
        return pltpu.make_async_remote_copy(
            src_ref=sent.at[0], dst_ref=landed.at[slot, side + source],
            send_sem=slot_send.at[slot, step], recv_sem=slot_recv.at[slot, step],
            device_id=(first_of_layer + source, slab), device_id_type=MESH)

    def leaves(slot, step):
        to = partner_of(i, step)
        real = ((slot > 0) | (to > 0) | slab_above) & ((slot < slots - 1) | (to < inner - 1) | slab_below)
        if step:
            return real
        return real & (((slot == 0) & first) | ((slot == slots - 1) & last))

    def comes(slot, step):
        real = ((slot > 0) | (i > 0) | slab_below) & ((slot < slots - 1) | (i < inner - 1) | slab_above)
        if step:
            return real
        return real & (((slot == 0) & first) | ((slot == slots - 1) & last))

    def send_slot(slot, carry):
        for step in range(inner):
            pl.when(leaves(slot, step))(lambda: outgoing(slot, step).start())
        return carry

    for j in range(layers):
        to = j * inner + owner

        @pl.when(to != me)
        def _():
            for number in range(3):
                table(number, j, spot, to).start()

    lax.fori_loop(0, 3, send_slot, 0)

    wide = NBR * PAIR
    lane = lax.broadcasted_iota(jnp.int32, (8, wide), 1)
    key_q = (lane // ORB)[:1]
    key_r = (lane // PAIR * ORB + lane % ORB)[:1]
    row = lax.broadcasted_iota(jnp.int32, (NBR * ORB, wide), 0)
    pick_q[...] = (row == key_q).astype(jnp.bfloat16)
    pick_r[...] = (row == key_r).astype(jnp.bfloat16)

    def relay(way, slot):
        start, into = (inner, 0) if way == 0 else (side, side + inner)
        return pltpu.make_async_remote_copy(
            src_ref=landed.at[slot, start:start + side], dst_ref=landed.at[slot, into:into + side],
            send_sem=relay_send.at[way, slot], recv_sem=relay_recv.at[way, slot],
            device_id=(me + inner if way == 0 else me - inner, slab), device_id_type=MESH)

    def relayed(way, slot):
        into = 0 if way == 0 else side + inner
        return pltpu.make_async_remote_copy(
            src_ref=landed.at[slot, into:into + side], dst_ref=landed.at[slot, into:into + side],
            send_sem=relay_send.at[way, slot], recv_sem=relay_recv.at[way, slot],
            device_id=(me - inner if way == 0 else me + inner, slab), device_id_type=MESH)

    def pass_on(slot):
        for step in range(inner):
            pl.when(comes(slot, step))(lambda: incoming(slot, step).wait_recv())
        pl.when(above)(lambda: relay(0, slot).start())
        pl.when(below)(lambda: relay(1, slot).start())

    for j in range(layers):
        @pl.when(i * layers + j != me)
        def _():
            for number in range(3):
                table(number, j, j, me).wait_recv()
    to_scalars = (pltpu.make_async_copy(near, near_at, local_sem.at[0]),
                  pltpu.make_async_copy(shifts, shift_at, local_sem.at[1]))
    for copy in to_scalars:
        copy.start()
    lane_of = lax.broadcasted_iota(jnp.int32, (16, WINDOW), 1)
    row_of = lax.broadcasted_iota(jnp.int32, (16, WINDOW), 0)
    place = ((lane_of + row_of == BAND - 1) & (row_of < BAND)).astype(jnp.bfloat16)
    count_pairs = mats.shape[2] - NBR * ORB
    for j in range(layers):
        column = lax.dot_general(
            eye(count_pairs), mats[j, :16, NBR * ORB:], NT, preferred_element_type=jnp.float32).astype(jnp.bfloat16)
        weights[j] = jnp.dot(column, place, preferred_element_type=jnp.float32)

    count = mats.shape[0] * mats.shape[1]
    matrices = mats[...].reshape(count, mats.shape[2])[:, :NBR * ORB]
    spread_q[...] = jnp.dot(matrices, pick_q[...], preferred_element_type=jnp.float32)
    pass_on(0)
    send_slot(3, 0)
    spread_r[...] = jnp.dot(matrices, pick_r[...], preferred_element_type=jnp.float32)
    for copy in to_scalars:
        copy.wait()
    pass_on(1)
    send_slot(4, 0)

    sub = lax.broadcasted_iota(jnp.int32, (8, WINDOW), 0)
    left_half = lax.broadcasted_iota(jnp.int32, (WINDOW, WINDOW), 1) < SPAN
    low_rows = lax.broadcasted_iota(jnp.int32, (8, wide), 0) < 4
    pair_of_atoms = 2
    zero = jnp.zeros((16, WINDOW), jnp.bfloat16)

    def window_of(m, index):
        shift = shift_at[m, 0, index]
        return shift, jnp.where(shift >= 0, 1, 0)

    def prepare(h, carry):
        m = lax.div(h, HALO // pair_of_atoms)
        for a in range(pair_of_atoms):
            atom = h * pair_of_atoms + a
            tiles = []
            for k in range(NBR):
                index = lax.rem(atom, HALO) * NBR + k
                shift, later = window_of(m, index)
                base = shift + side * local_e - BAND // 2 - later * late
                weight = weights[m, pl.ds(index, 1), :]
                tiles.append(pltpu.roll(jnp.broadcast_to(weight, (8, WINDOW)), WINDOW - BAND + 1 - base, 1))
            for step in (1, 2, 4):
                tiles = [jnp.where((sub & step) != 0, pltpu.roll(tile, step, 1), tile) for tile in tiles]
            tiles = [jnp.concatenate([tile, pltpu.roll(tile, 8, 1)], axis=0).astype(jnp.bfloat16) for tile in tiles]
            for b in range(WINDOW // 16):
                for k in range(NBR):
                    tile = pltpu.roll(tiles[k], 16 * b, 1) if b else tiles[k]
                    toeplitz[atom * NBR + k, 16 * b:16 * b + 16] = jnp.where(left_half[:16], tile, zero)
                    low = WINDOW + (16 * b - SPAN) % WINDOW
                    toeplitz[atom * NBR + k, low:low + 16] = jnp.where(left_half[:16], zero, tile)
            right = spread_r[pl.ds(pl.multiple_of(atom * 16, 16), 16), :]
            rights = (right[:8], jnp.concatenate([right[8:12], right[:4]], axis=0), right[4:12])
            for four in range(ORB // 4):
                rows = []
                for half in range(2):
                    p = four * 4 + half * 2
                    q0 = spread_q[pl.ds(atom * 16 + p, 1), :]
                    q1 = spread_q[pl.ds(atom * 16 + p + 1, 1), :]
                    rows += [q0 * rights[0], jnp.where(low_rows, q0, q1) * rights[1], q1 * rights[2]]
                both[atom, four * 48:(four + 1) * 48, :] = jnp.concatenate(rows, axis=0).astype(jnp.bfloat16)


        pl.when(lax.rem(h, 2) == 0)(lambda: pass_on(lax.div(h, 2) + 2))
        pl.when(h == 0)(lambda: [send_slot(5, 0), None][1])
        return carry

    steps = mine * HALO // pair_of_atoms
    assert slots == 6 and steps >= slots
    lax.fori_loop(0, steps, prepare, 0)

    unit = eye(128)

    def turn(slot, carry):
        pl.when(below)(lambda: relayed(0, slot).wait_recv())
        pl.when(above)(lambda: relayed(1, slot).wait_recv())
        if local_e % 16:
            for piece in range(pieces):
                stage[piece * local_e:(piece + 1) * local_e, :] = landed[slot, piece].astype(jnp.float32)
            tall = stage[...].astype(jnp.bfloat16)
        else:
            tall = landed[slot].reshape(rows_e, width)
        two = jnp.concatenate([tall[:WINDOW], tall[late:]], axis=0)
        turned = jnp.concatenate([
            lax.dot_general(unit, two[:, j * 128:(j + 1) * 128], NT, preferred_element_type=jnp.float32).astype(
                jnp.bfloat16) for j in range(width // 128)], axis=0)
        for atom in range(HALO):
            for c in range(2):
                start = (2 * atom + c) * PAIR
                for window in range(2):
                    green[window, slot * HALO + atom, :, c * WINDOW:(c + 1) * WINDOW] = (
                        turned[start:start + PAIR, window * WINDOW:(window + 1) * WINDOW])
        return carry

    lax.fori_loop(0, 2, turn, 0)

    def share(step, m, at):
        to = partner_of(i, step)
        return pltpu.make_async_remote_copy(
            src_ref=out_ref.at[to, m], dst_ref=back_ref.at[at * mine + m],
            send_sem=back_send.at[step, m], recv_sem=back_recv.at[step, m],
            device_id=(first_of_layer + to, slab), device_id_type=MESH)

    def chunk(m, carry):
        turn(m + 2, 0)
        for a in range(HALO):
            for k in range(NBR):
                index = a * NBR + k
                later = window_of(m, index)[1]
                partner = jnp.clip(near_at[m, 0, index] - first_atom, 0, slots * HALO - 1)
                banded = jnp.dot(
                    green[later, partner], toeplitz[m * HALO * NBR + index], preferred_element_type=jnp.float32)
                bands[a, k * PAIR:(k + 1) * PAIR, :] = banded.astype(jnp.bfloat16)
        parts = []
        for a in range(HALO):
            total = jnp.dot(both[m * HALO + a], bands[a], preferred_element_type=jnp.float32)
            turned = lax.dot_general(unit, total.astype(jnp.bfloat16), NT, preferred_element_type=jnp.float32)
            parts += [turned[:SPAN], turned[SPAN:]]
        whole = jnp.concatenate(parts, axis=1)
        for d in range(inner):
            out_ref[d, m] = whole[d * local_e:(d + 1) * local_e].astype(jnp.bfloat16)
        for step in range(1, inner):
            share(step, m, i).start()
        back_ref[i * mine + m] = out_ref[i, m]
        return carry

    lax.fori_loop(0, mine, chunk, 0)

    for j in range(layers):
        @pl.when(j * inner + owner != me)
        def _():
            for number in range(3):
                table(number, j, j, me).wait_send()

    def sent_slot(slot, carry):
        for step in range(inner):
            pl.when(leaves(slot, step))(lambda: outgoing(slot, step).wait_send())
        pl.when(above)(lambda: relay(0, slot).wait_send())
        pl.when(below)(lambda: relay(1, slot).wait_send())
        return carry

    lax.fori_loop(0, slots, sent_slot, 0)

    def finish(m, carry):
        for step in range(1, inner):
            share(step, m, partner_of(i, step)).wait_recv()
            share(step, m, i).wait_send()
        return carry

    lax.fori_loop(0, mine, finish, 0)


def on_device(green_blocks, couplings, band_weights, neighbours, shifts):
    groups = lax.axis_size("energy")
    local_e, slab_count = green_blocks.shape[3:]
    per_dev = slab_count // groups
    width = per_dev * BLOCK
    pairs = per_dev * NBR
    lanes = NBR * ORB + pairs
    inner = SPAN // local_e
    layers = groups // inner
    side = pl.cdiv(REACH, local_e)
    pieces = inner + 2 * side
    mine = groups // inner
    slots = mine + 2
    assert per_dev == HALO and side <= inner and pieces * local_e >= WINDOW
    vmem = pl.BlockSpec(memory_space=pltpu.VMEM)
    smem = pl.BlockSpec(memory_space=pltpu.SMEM)
    blocks = jax.ShapeDtypeStruct((groups, local_e, width), jnp.bfloat16)
    wide = pltpu.VMEM((pl.cdiv(slab_count, 128), BLOCK * local_e, 128), jnp.float32)
    packed = pltpu.VMEM((width // 128, local_e * groups, 128), jnp.float32)
    room = pltpu.CompilerParams(vmem_limit_bytes=32 * 1024 * 1024)

    sent = pl.pallas_call(
        functools.partial(pack_kernel, groups, per_dev),
        out_shape=blocks, in_specs=[vmem], out_specs=vmem,
        scratch_shapes=[wide, packed], compiler_params=room,
    )(green_blocks.reshape(BLOCK * local_e, slab_count))
    back = pl.pallas_call(
        functools.partial(wire_kernel, inner, layers, side),
        out_shape=blocks,
        in_specs=[vmem] * 5,
        out_specs=vmem,
        scratch_shapes=[
            pltpu.VMEM((ORB, 16, pairs), jnp.float32), pltpu.VMEM((16, pairs), jnp.float32),
            pltpu.VMEM((per_dev * 16, lanes), jnp.bfloat16),
            pltpu.VMEM((slots, pieces, local_e, width), jnp.bfloat16),
            pltpu.VMEM((layers, per_dev * 16, lanes), jnp.bfloat16),
            pltpu.VMEM((layers, pairs, WINDOW), jnp.float32),
            pltpu.VMEM((layers, 1, pairs), jnp.int32),
            pltpu.VMEM((layers, 1, pairs), jnp.int32),
            pltpu.SMEM((layers, 1, pairs), jnp.int32),
            pltpu.SMEM((layers, 1, pairs), jnp.int32),
            pltpu.VMEM((NBR * ORB, NBR * PAIR), jnp.bfloat16), pltpu.VMEM((NBR * ORB, NBR * PAIR), jnp.bfloat16),
            pltpu.VMEM((inner, mine, local_e, width), jnp.bfloat16),
            pltpu.VMEM((2, slots * HALO, PAIR, 2 * WINDOW), jnp.bfloat16),
            pltpu.VMEM((mine * HALO * 16, NBR * PAIR), jnp.float32),
            pltpu.VMEM((mine * HALO * 16, NBR * PAIR), jnp.float32),
            pltpu.VMEM((mine * HALO, PAIR, NBR * PAIR), jnp.bfloat16),
            pltpu.VMEM((mine * HALO * NBR, 2 * WINDOW, WINDOW), jnp.bfloat16),
            pltpu.VMEM((HALO, NBR * PAIR, WINDOW), jnp.bfloat16),
            pltpu.VMEM((pieces * local_e if local_e % 16 else 8, width), jnp.float32),
            pltpu.SemaphoreType.DMA((slots, inner)), pltpu.SemaphoreType.DMA((slots, inner)),
            pltpu.SemaphoreType.DMA((2, slots)), pltpu.SemaphoreType.DMA((2, slots)),
            pltpu.SemaphoreType.DMA((3, layers)), pltpu.SemaphoreType.DMA((3, layers)),
            pltpu.SemaphoreType.DMA((inner, mine)), pltpu.SemaphoreType.DMA((inner, mine)),
            pltpu.SemaphoreType.DMA((2,)),
        ],
        compiler_params=pltpu.CompilerParams(
            collective_id=0, has_side_effects=True, vmem_limit_bytes=48 * 1024 * 1024),
    )(sent, couplings.reshape(ORB, ORB, pairs), band_weights, neighbours, shifts)
    result = pl.pallas_call(
        functools.partial(unpack_kernel, groups, per_dev),
        out_shape=jax.ShapeDtypeStruct((BLOCK * local_e, slab_count), jnp.bfloat16),
        in_specs=[vmem], out_specs=vmem,
        scratch_shapes=[packed, wide], compiler_params=room,
    )(back)
    return result.reshape(2, ORB, ORB, local_e, slab_count)


def solution(mesh):
    return jax.shard_map(
        on_device,
        mesh=mesh,
        in_specs=(
            P(None, None, None, "energy", "slab"),
            P(None, None, "slab", "energy"),
            P(None, "slab", "energy"),
            P("slab", "energy"),
            P("slab", "energy"),
        ),
        out_specs=P(None, None, None, "energy", "slab"),
        check_vma=False,
    )
```

```python
import functools

import jax
import jax.numpy as jnp
from jax import lax
from jax.experimental import pallas as pl
from jax.experimental.pallas import tpu as pltpu
from jax.sharding import PartitionSpec as P

ORB = 12
NBR = 16
BAND = 9
SHIFT = 32
HALO = 4
BLOCK = 2 * ORB * ORB
PAIR = ORB * ORB
REACH = SHIFT + BAND // 2
SPAN = 64
WINDOW = 128

MESH = pl.DeviceIdType.MESH
NT = (((1,), (1,)), ((), ()))


def order(groups, per_dev):
    count = groups * per_dev
    row = lax.broadcasted_iota(jnp.int32, (count, count), 0)
    atom = lax.broadcasted_iota(jnp.int32, (count, count), 1)
    return (atom == (row % groups) * per_dev + row // groups).astype(jnp.bfloat16)


def eye(count):
    row = lax.broadcasted_iota(jnp.int32, (count, count), 0)
    column = lax.broadcasted_iota(jnp.int32, (count, count), 1)
    return (row == column).astype(jnp.bfloat16)


def partner_of(i, step):
    out, bit = 0, 1
    while bit <= step:
        out = out + bit * lax.rem(lax.div(i, bit) + step // bit, 2)
        bit *= 2
    return lax.div(i, bit) * bit + out if step else i


def pack_kernel(groups, per_dev, x_ref, sent, wide, packed):
    local_e = sent.shape[1]
    tiles = wide.shape[0]
    count = x_ref.shape[1]
    lanes = min(count, 128)
    if lanes < 128:
        wide[...] = jnp.zeros_like(wide)
    for j in range(tiles):
        wide[j, :x_ref.shape[0], :lanes] = x_ref[:, j * 128:j * 128 + lanes].astype(jnp.float32)
    pick = order(groups, per_dev)
    for e in range(local_e):
        rows = jnp.concatenate([wide[j, pl.ds(e, BLOCK, stride=local_e), :] for j in range(tiles)], axis=1)
        rows = rows[:, :count].astype(jnp.bfloat16)
        turned = lax.dot_general(pick, rows, NT, preferred_element_type=jnp.float32)
        flat = jnp.concatenate([turned[i * groups:(i + 1) * groups] for i in range(per_dev)], axis=1)
        for j in range(packed.shape[0]):
            packed[j, pl.ds(e, groups, stride=local_e), :] = flat[:, j * 128:(j + 1) * 128]
    for g in range(groups):
        for j in range(packed.shape[0]):
            sent[g, :, j * 128:(j + 1) * 128] = packed[j, g * local_e:(g + 1) * local_e, :].astype(jnp.bfloat16)


def unpack_kernel(groups, per_dev, landed, out_ref, wide, tall):
    local_e = landed.shape[1]
    lanes = min(out_ref.shape[1], 128)
    for g in range(groups):
        for j in range(wide.shape[0]):
            wide[j, g * local_e:(g + 1) * local_e, :] = landed[g, :, j * 128:(j + 1) * 128].astype(jnp.float32)
    pick = order(per_dev, groups)
    unit = eye(128)
    for e in range(local_e):
        rows = jnp.concatenate(
            [wide[j, pl.ds(e, groups, stride=local_e), :] for j in range(wide.shape[0])], axis=1)
        stack = jnp.concatenate([rows[:, i * BLOCK:(i + 1) * BLOCK] for i in range(per_dev)], axis=0)
        atoms = lax.dot_general(
            pick, stack.astype(jnp.bfloat16), (((1,), (0,)), ((), ())), preferred_element_type=jnp.float32)
        atoms = atoms.astype(jnp.bfloat16)
        turned = jnp.concatenate([
            lax.dot_general(
                unit[:min(128, BLOCK - b), :min(128, BLOCK - b)], atoms[:, b:b + 128], NT,
                preferred_element_type=jnp.float32) for b in range(0, BLOCK, 128)], axis=0)
        if lanes < 128:
            turned = jnp.concatenate([turned, jnp.zeros((BLOCK, 128 - lanes), jnp.float32)], axis=1)
        for j in range(tall.shape[0]):
            tall[j, pl.ds(e, BLOCK, stride=local_e), :] = turned[:, j * 128:(j + 1) * 128]
    for j in range(tall.shape[0]):
        out_ref[:, j * 128:j * 128 + lanes] = tall[j, :out_ref.shape[0], :lanes].astype(jnp.bfloat16)


def table_tall(padded, weight_rows, mats_in):
    pairs = padded.shape[2]
    atoms, lanes = pairs // NBR, mats_in.shape[1]
    wide = atoms * lanes
    tall = padded[...].reshape(ORB * 16, pairs).astype(jnp.bfloat16)
    lane = lax.broadcasted_iota(jnp.int32, (8, wide), 1)[:1]
    inside = lane % lanes
    pair_of = jnp.where(inside < NBR * ORB, lane // lanes * NBR + inside // ORB, -1)
    row = lax.broadcasted_iota(jnp.int32, (pairs, wide), 0)
    spread = jnp.dot(tall, (row == pair_of).astype(jnp.bfloat16), preferred_element_type=jnp.float32)
    row = lax.broadcasted_iota(jnp.int32, (ORB * 16, wide), 0) % 16
    spread = jnp.where(row == inside % ORB, spread, 0.0).astype(jnp.bfloat16)
    p = lax.broadcasted_iota(jnp.int32, (16, ORB * 16), 0)
    of = lax.broadcasted_iota(jnp.int32, (16, ORB * 16), 1) // 16
    flat = jnp.dot((p == of).astype(jnp.bfloat16), spread, preferred_element_type=jnp.float32)
    at = lax.broadcasted_iota(jnp.int32, (pairs, lanes), 1) - NBR * ORB
    pair = lax.broadcasted_iota(jnp.int32, (pairs, lanes), 0)
    behind = jnp.dot(
        weight_rows[...].astype(jnp.bfloat16), (at == pair).astype(jnp.bfloat16), preferred_element_type=jnp.float32)
    for atom in range(atoms):
        block = flat[:, atom * lanes:(atom + 1) * lanes]
        mats_in[atom * 16:(atom + 1) * 16, :] = (block + behind if atom == 0 else block).astype(jnp.bfloat16)


def wire_kernel(inner, layers, side, sent, coupling_ref, weight_ref, near_ref, shift_ref, back_ref,
                padded, weight_rows, mats_in,
                landed, mats, weights, near, shifts, near_at, shift_at, pick_q, pick_r,
                out_ref, green, spread_q, spread_r, both, toeplitz, bands, stage,
                slot_send, slot_recv, relay_send, relay_recv, table_send, table_recv, back_send, back_recv, local_sem):
    slots, pieces, local_e, width = landed.shape
    mine = slots - 2
    chunks = sent.shape[0]
    rows_e = pieces * local_e
    late = rows_e - WINDOW
    me, slab = lax.axis_index("energy"), lax.axis_index("slab")
    slabs = lax.axis_size("slab")
    layer, i = lax.div(me, inner), lax.rem(me, inner)
    first_of_layer = layer * inner
    first_atom = slab * (chunks * HALO) + i * (mine * HALO) - HALO
    first, last = i == 0, i == inner - 1
    below, above = layer > 0, layer < layers - 1
    slab_below, slab_above = slab > 0, slab < slabs - 1
    owner, spot = lax.div(me, layers), lax.rem(me, layers)
    barrier = pltpu.get_barrier_semaphore()
    one = lambda flag: jnp.where(flag, 1, 0)

    def hail(device, row):
        pl.semaphore_signal(barrier, inc=1, device_id=(device, row), device_id_type=MESH)

    for step in range(1, inner):
        hail(first_of_layer + partner_of(i, step), slab)

    @pl.when(first & slab_below)
    def _():
        for j in range(inner):
            hail(first_of_layer + j, slab - 1)

    @pl.when(last & slab_above)
    def _():
        for j in range(inner):
            hail(first_of_layer + j, slab + 1)

    pl.when(below)(lambda: hail(me - inner, slab))
    pl.when(above)(lambda: hail(me + inner, slab))
    for j in range(layers):
        pl.when(i * layers + j != me)(lambda: hail(i * layers + j, slab))
    padded[...] = jnp.zeros_like(padded)
    weight_rows[...] = jnp.zeros_like(weight_rows)
    for p in range(ORB):
        padded[p, :ORB, :] = coupling_ref[p].astype(jnp.float32)
    weight_rows[:BAND, :] = weight_ref[:, 0, :]
    table_tall(padded, weight_rows, mats_in)

    landed[pl.ds(1, mine), side + i] = sent[pl.ds(i * mine, mine)]

    @pl.when(i > 0)
    def _():
        landed[0, side + i] = sent[lax.rem(i * mine - 1 + chunks, chunks)]

    @pl.when(i < inner - 1)
    def _():
        landed[slots - 1, side + i] = sent[lax.rem(i * mine + mine, chunks)]

    @pl.when(first & jnp.logical_not(slab_below))
    def _():
        landed[0, side:side + inner] = jnp.zeros((inner, local_e, width), landed.dtype)

    @pl.when(last & jnp.logical_not(slab_above))
    def _():
        landed[slots - 1, side:side + inner] = jnp.zeros((inner, local_e, width), landed.dtype)

    def clear(start):
        landed[:, start:start + side] = jnp.zeros((slots, side, local_e, width), landed.dtype)

    pl.when(jnp.logical_not(below))(lambda: clear(0))
    pl.when(jnp.logical_not(above))(lambda: clear(side + inner))

    tables = ((mats_in, mats), (near_ref, near), (shift_ref, shifts))

    @pl.when(owner == i)
    def _():
        for src, dst in tables:
            dst[spot] = src[...]

    pl.semaphore_wait(
        barrier, inner - 1 + one(slab_above) + one(slab_below) + one(above) + one(below) + layers - one(owner == i))

    def table(number, j, at, to):
        src, dst = tables[number]
        return pltpu.make_async_remote_copy(
            src_ref=src, dst_ref=dst.at[at], send_sem=table_send.at[number, j], recv_sem=table_recv.at[number, at],
            device_id=(to, slab), device_id_type=MESH)

    def outgoing(slot, step):
        to = partner_of(i, step)
        row = slab + one((slot == 0) & (to == 0)) - one((slot == slots - 1) & (to == inner - 1))
        return pltpu.make_async_remote_copy(
            src_ref=sent.at[lax.rem(to * mine + slot - 1 + chunks, chunks)], dst_ref=landed.at[slot, side + i],
            send_sem=slot_send.at[slot, step], recv_sem=slot_recv.at[slot, step],
            device_id=(first_of_layer + to, row), device_id_type=MESH)

    def incoming(slot, step):
        source = partner_of(i, step)
        return pltpu.make_async_remote_copy(
            src_ref=sent.at[0], dst_ref=landed.at[slot, side + source],
            send_sem=slot_send.at[slot, step], recv_sem=slot_recv.at[slot, step],
            device_id=(first_of_layer + source, slab), device_id_type=MESH)

    def leaves(slot, step):
        to = partner_of(i, step)
        real = ((slot > 0) | (to > 0) | slab_above) & ((slot < slots - 1) | (to < inner - 1) | slab_below)
        if step:
            return real
        return real & (((slot == 0) & first) | ((slot == slots - 1) & last))

    def comes(slot, step):
        real = ((slot > 0) | (i > 0) | slab_below) & ((slot < slots - 1) | (i < inner - 1) | slab_above)
        if step:
            return real
        return real & (((slot == 0) & first) | ((slot == slots - 1) & last))

    def send_slot(slot, carry):
        for step in range(inner):
            pl.when(leaves(slot, step))(lambda: outgoing(slot, step).start())
        return carry

    for j in range(layers):
        to = j * inner + owner

        @pl.when(to != me)
        def _():
            for number in range(3):
                table(number, j, spot, to).start()

    lax.fori_loop(0, 3, send_slot, 0)

    wide = NBR * PAIR
    lane = lax.broadcasted_iota(jnp.int32, (8, wide), 1)
    key_q = (lane // ORB)[:1]
    key_r = (lane // PAIR * ORB + lane % ORB)[:1]
    row = lax.broadcasted_iota(jnp.int32, (NBR * ORB, wide), 0)
    pick_q[...] = (row == key_q).astype(jnp.bfloat16)
    pick_r[...] = (row == key_r).astype(jnp.bfloat16)

    def relay(way, slot):
        start, into = (inner, 0) if way == 0 else (side, side + inner)
        return pltpu.make_async_remote_copy(
            src_ref=landed.at[slot, start:start + side], dst_ref=landed.at[slot, into:into + side],
            send_sem=relay_send.at[way, slot], recv_sem=relay_recv.at[way, slot],
            device_id=(me + inner if way == 0 else me - inner, slab), device_id_type=MESH)

    def relayed(way, slot):
        into = 0 if way == 0 else side + inner
        return pltpu.make_async_remote_copy(
            src_ref=landed.at[slot, into:into + side], dst_ref=landed.at[slot, into:into + side],
            send_sem=relay_send.at[way, slot], recv_sem=relay_recv.at[way, slot],
            device_id=(me - inner if way == 0 else me + inner, slab), device_id_type=MESH)

    def pass_on(slot):
        for step in range(inner):
            pl.when(comes(slot, step))(lambda: incoming(slot, step).wait_recv())
        pl.when(above)(lambda: relay(0, slot).start())
        pl.when(below)(lambda: relay(1, slot).start())

    for j in range(layers):
        @pl.when(i * layers + j != me)
        def _():
            for number in range(3):
                table(number, j, j, me).wait_recv()
    to_scalars = (pltpu.make_async_copy(near, near_at, local_sem.at[0]),
                  pltpu.make_async_copy(shifts, shift_at, local_sem.at[1]))
    for copy in to_scalars:
        copy.start()
    lane_of = lax.broadcasted_iota(jnp.int32, (16, WINDOW), 1)
    row_of = lax.broadcasted_iota(jnp.int32, (16, WINDOW), 0)
    place = ((lane_of + row_of == BAND - 1) & (row_of < BAND)).astype(jnp.bfloat16)
    count_pairs = mats.shape[2] - NBR * ORB
    for j in range(layers):
        column = lax.dot_general(
            eye(count_pairs), mats[j, :16, NBR * ORB:], NT, preferred_element_type=jnp.float32).astype(jnp.bfloat16)
        weights[j] = jnp.dot(column, place, preferred_element_type=jnp.float32)

    count = mats.shape[0] * mats.shape[1]
    matrices = mats[...].reshape(count, mats.shape[2])[:, :NBR * ORB]
    spread_q[...] = jnp.dot(matrices, pick_q[...], preferred_element_type=jnp.float32)
    pass_on(0)
    send_slot(3, 0)
    spread_r[...] = jnp.dot(matrices, pick_r[...], preferred_element_type=jnp.float32)
    for copy in to_scalars:
        copy.wait()
    pass_on(1)
    send_slot(4, 0)

    sub = lax.broadcasted_iota(jnp.int32, (8, WINDOW), 0)
    left_half = lax.broadcasted_iota(jnp.int32, (WINDOW, WINDOW), 1) < SPAN
    low_rows = lax.broadcasted_iota(jnp.int32, (8, wide), 0) < 4
    pair_of_atoms = 2
    zero = jnp.zeros((16, WINDOW), jnp.bfloat16)

    def window_of(m, index):
        shift = shift_at[m, 0, index]
        return shift, jnp.where(shift >= 0, 1, 0)

    def prepare(h, carry):
        m = lax.div(h, HALO // pair_of_atoms)
        for a in range(pair_of_atoms):
            atom = h * pair_of_atoms + a
            tiles = []
            for k in range(NBR):
                index = lax.rem(atom, HALO) * NBR + k
                shift, later = window_of(m, index)
                base = shift + side * local_e - BAND // 2 - later * late
                weight = weights[m, pl.ds(index, 1), :]
                tiles.append(pltpu.roll(jnp.broadcast_to(weight, (8, WINDOW)), WINDOW - BAND + 1 - base, 1))
            for step in (1, 2, 4):
                tiles = [jnp.where((sub & step) != 0, pltpu.roll(tile, step, 1), tile) for tile in tiles]
            tiles = [jnp.concatenate([tile, pltpu.roll(tile, 8, 1)], axis=0).astype(jnp.bfloat16) for tile in tiles]
            for b in range(WINDOW // 16):
                for k in range(NBR):
                    tile = pltpu.roll(tiles[k], 16 * b, 1) if b else tiles[k]
                    toeplitz[atom * NBR + k, 16 * b:16 * b + 16] = jnp.where(left_half[:16], tile, zero)
                    low = WINDOW + (16 * b - SPAN) % WINDOW
                    toeplitz[atom * NBR + k, low:low + 16] = jnp.where(left_half[:16], zero, tile)
            right = spread_r[pl.ds(pl.multiple_of(atom * 16, 16), 16), :]
            rights = (right[:8], jnp.concatenate([right[8:12], right[:4]], axis=0), right[4:12])
            for four in range(ORB // 4):
                rows = []
                for half in range(2):
                    p = four * 4 + half * 2
                    q0 = spread_q[pl.ds(atom * 16 + p, 1), :]
                    q1 = spread_q[pl.ds(atom * 16 + p + 1, 1), :]
                    rows += [q0 * rights[0], jnp.where(low_rows, q0, q1) * rights[1], q1 * rights[2]]
                both[atom, four * 48:(four + 1) * 48, :] = jnp.concatenate(rows, axis=0).astype(jnp.bfloat16)


        pl.when(lax.rem(h, 2) == 0)(lambda: pass_on(lax.div(h, 2) + 2))
        pl.when(h == 0)(lambda: [send_slot(5, 0), None][1])
        return carry

    steps = mine * HALO // pair_of_atoms
    assert slots == 6 and steps >= slots
    lax.fori_loop(0, steps, prepare, 0)

    unit = eye(128)

    def turn(slot, carry):
        pl.when(below)(lambda: relayed(0, slot).wait_recv())
        pl.when(above)(lambda: relayed(1, slot).wait_recv())
        if local_e % 16:
            for piece in range(pieces):
                stage[piece * local_e:(piece + 1) * local_e, :] = landed[slot, piece].astype(jnp.float32)
            tall = stage[...].astype(jnp.bfloat16)
        else:
            tall = landed[slot].reshape(rows_e, width)
        two = jnp.concatenate([tall[:WINDOW], tall[late:]], axis=0)
        turned = jnp.concatenate([
            lax.dot_general(unit, two[:, j * 128:(j + 1) * 128], NT, preferred_element_type=jnp.float32).astype(
                jnp.bfloat16) for j in range(width // 128)], axis=0)
        for atom in range(HALO):
            for c in range(2):
                start = (2 * atom + c) * PAIR
                for window in range(2):
                    green[window, slot * HALO + atom, :, c * WINDOW:(c + 1) * WINDOW] = (
                        turned[start:start + PAIR, window * WINDOW:(window + 1) * WINDOW])
        return carry

    lax.fori_loop(0, 2, turn, 0)

    def share(step, m, at):
        to = partner_of(i, step)
        return pltpu.make_async_remote_copy(
            src_ref=out_ref.at[to, m], dst_ref=back_ref.at[at * mine + m],
            send_sem=back_send.at[step, m], recv_sem=back_recv.at[step, m],
            device_id=(first_of_layer + to, slab), device_id_type=MESH)

    def chunk(m, carry):
        turn(m + 2, 0)
        for a in range(HALO):
            for k in range(NBR):
                index = a * NBR + k
                later = window_of(m, index)[1]
                partner = jnp.clip(near_at[m, 0, index] - first_atom, 0, slots * HALO - 1)
                banded = jnp.dot(
                    green[later, partner], toeplitz[m * HALO * NBR + index], preferred_element_type=jnp.float32)
                bands[a, k * PAIR:(k + 1) * PAIR, :] = banded.astype(jnp.bfloat16)
        parts = []
        totals = [jnp.dot(both[m * HALO + a], bands[a], preferred_element_type=jnp.float32) for a in range(HALO)]
        for total in totals:
            turned = lax.dot_general(unit, total.astype(jnp.bfloat16), NT, preferred_element_type=jnp.float32)
            parts += [turned[:SPAN], turned[SPAN:]]
        whole = jnp.concatenate(parts, axis=1)
        for d in range(inner):
            out_ref[d, m] = whole[d * local_e:(d + 1) * local_e].astype(jnp.bfloat16)
        for step in range(1, inner):
            share(step, m, i).start()
        back_ref[i * mine + m] = out_ref[i, m]
        return carry

    lax.fori_loop(0, mine, chunk, 0)

    for j in range(layers):
        @pl.when(j * inner + owner != me)
        def _():
            for number in range(3):
                table(number, j, j, me).wait_send()

    def sent_slot(slot, carry):
        for step in range(inner):
            pl.when(leaves(slot, step))(lambda: outgoing(slot, step).wait_send())
        pl.when(above)(lambda: relay(0, slot).wait_send())
        pl.when(below)(lambda: relay(1, slot).wait_send())
        return carry

    lax.fori_loop(0, slots, sent_slot, 0)

    def finish(m, carry):
        for step in range(1, inner):
            share(step, m, partner_of(i, step)).wait_recv()
            share(step, m, i).wait_send()
        return carry

    lax.fori_loop(0, mine, finish, 0)


def on_device(green_blocks, couplings, band_weights, neighbours, shifts):
    groups = lax.axis_size("energy")
    local_e, slab_count = green_blocks.shape[3:]
    per_dev = slab_count // groups
    width = per_dev * BLOCK
    pairs = per_dev * NBR
    lanes = NBR * ORB + pairs
    inner = SPAN // local_e
    layers = groups // inner
    side = pl.cdiv(REACH, local_e)
    pieces = inner + 2 * side
    mine = groups // inner
    slots = mine + 2
    assert per_dev == HALO and side <= inner and pieces * local_e >= WINDOW
    vmem = pl.BlockSpec(memory_space=pltpu.VMEM)
    smem = pl.BlockSpec(memory_space=pltpu.SMEM)
    blocks = jax.ShapeDtypeStruct((groups, local_e, width), jnp.bfloat16)
    wide = pltpu.VMEM((pl.cdiv(slab_count, 128), BLOCK * local_e, 128), jnp.float32)
    packed = pltpu.VMEM((width // 128, local_e * groups, 128), jnp.float32)
    room = pltpu.CompilerParams(vmem_limit_bytes=32 * 1024 * 1024)

    sent = pl.pallas_call(
        functools.partial(pack_kernel, groups, per_dev),
        out_shape=blocks, in_specs=[vmem], out_specs=vmem,
        scratch_shapes=[wide, packed], compiler_params=room,
    )(green_blocks.reshape(BLOCK * local_e, slab_count))
    back = pl.pallas_call(
        functools.partial(wire_kernel, inner, layers, side),
        out_shape=blocks,
        in_specs=[vmem] * 5,
        out_specs=vmem,
        scratch_shapes=[
            pltpu.VMEM((ORB, 16, pairs), jnp.float32), pltpu.VMEM((16, pairs), jnp.float32),
            pltpu.VMEM((per_dev * 16, lanes), jnp.bfloat16),
            pltpu.VMEM((slots, pieces, local_e, width), jnp.bfloat16),
            pltpu.VMEM((layers, per_dev * 16, lanes), jnp.bfloat16),
            pltpu.VMEM((layers, pairs, WINDOW), jnp.float32),
            pltpu.VMEM((layers, 1, pairs), jnp.int32),
            pltpu.VMEM((layers, 1, pairs), jnp.int32),
            pltpu.SMEM((layers, 1, pairs), jnp.int32),
            pltpu.SMEM((layers, 1, pairs), jnp.int32),
            pltpu.VMEM((NBR * ORB, NBR * PAIR), jnp.bfloat16), pltpu.VMEM((NBR * ORB, NBR * PAIR), jnp.bfloat16),
            pltpu.VMEM((inner, mine, local_e, width), jnp.bfloat16),
            pltpu.VMEM((2, slots * HALO, PAIR, 2 * WINDOW), jnp.bfloat16),
            pltpu.VMEM((mine * HALO * 16, NBR * PAIR), jnp.float32),
            pltpu.VMEM((mine * HALO * 16, NBR * PAIR), jnp.float32),
            pltpu.VMEM((mine * HALO, PAIR, NBR * PAIR), jnp.bfloat16),
            pltpu.VMEM((mine * HALO * NBR, 2 * WINDOW, WINDOW), jnp.bfloat16),
            pltpu.VMEM((HALO, NBR * PAIR, WINDOW), jnp.bfloat16),
            pltpu.VMEM((pieces * local_e if local_e % 16 else 8, width), jnp.float32),
            pltpu.SemaphoreType.DMA((slots, inner)), pltpu.SemaphoreType.DMA((slots, inner)),
            pltpu.SemaphoreType.DMA((2, slots)), pltpu.SemaphoreType.DMA((2, slots)),
            pltpu.SemaphoreType.DMA((3, layers)), pltpu.SemaphoreType.DMA((3, layers)),
            pltpu.SemaphoreType.DMA((inner, mine)), pltpu.SemaphoreType.DMA((inner, mine)),
            pltpu.SemaphoreType.DMA((2,)),
        ],
        compiler_params=pltpu.CompilerParams(
            collective_id=0, has_side_effects=True, vmem_limit_bytes=48 * 1024 * 1024),
    )(sent, couplings.reshape(ORB, ORB, pairs), band_weights, neighbours, shifts)
    result = pl.pallas_call(
        functools.partial(unpack_kernel, groups, per_dev),
        out_shape=jax.ShapeDtypeStruct((BLOCK * local_e, slab_count), jnp.bfloat16),
        in_specs=[vmem], out_specs=vmem,
        scratch_shapes=[packed, wide], compiler_params=room,
    )(back)
    return result.reshape(2, ORB, ORB, local_e, slab_count)


def solution(mesh):
    return jax.shard_map(
        on_device,
        mesh=mesh,
        in_specs=(
            P(None, None, None, "energy", "slab"),
            P(None, None, "slab", "energy"),
            P(None, "slab", "energy"),
            P("slab", "energy"),
            P("slab", "energy"),
        ),
        out_specs=P(None, None, None, "energy", "slab"),
        check_vma=False,
    )
```

```python
import functools

import jax
import jax.numpy as jnp
from jax import lax
from jax.experimental import pallas as pl
from jax.experimental.pallas import tpu as pltpu
from jax.sharding import PartitionSpec as P

ORB = 12
NBR = 16
BAND = 9
SHIFT = 32
HALO = 4
BLOCK = 2 * ORB * ORB
PAIR = ORB * ORB
REACH = SHIFT + BAND // 2
SPAN = 64
WINDOW = 128

MESH = pl.DeviceIdType.MESH
NT = (((1,), (1,)), ((), ()))


def order(groups, per_dev):
    count = groups * per_dev
    row = lax.broadcasted_iota(jnp.int32, (count, count), 0)
    atom = lax.broadcasted_iota(jnp.int32, (count, count), 1)
    return (atom == (row % groups) * per_dev + row // groups).astype(jnp.bfloat16)


def eye(count):
    row = lax.broadcasted_iota(jnp.int32, (count, count), 0)
    column = lax.broadcasted_iota(jnp.int32, (count, count), 1)
    return (row == column).astype(jnp.bfloat16)


def partner_of(i, step):
    out, bit = 0, 1
    while bit <= step:
        out = out + bit * lax.rem(lax.div(i, bit) + step // bit, 2)
        bit *= 2
    return lax.div(i, bit) * bit + out if step else i


def pack_kernel(groups, per_dev, x_ref, sent, wide, packed):
    local_e = sent.shape[1]
    tiles = wide.shape[0]
    count = x_ref.shape[1]
    lanes = min(count, 128)
    if lanes < 128:
        wide[...] = jnp.zeros_like(wide)
    for j in range(tiles):
        wide[j, :x_ref.shape[0], :lanes] = x_ref[:, j * 128:j * 128 + lanes].astype(jnp.float32)
    pick = order(groups, per_dev)
    for e in range(local_e):
        rows = jnp.concatenate([wide[j, pl.ds(e, BLOCK, stride=local_e), :] for j in range(tiles)], axis=1)
        rows = rows[:, :count].astype(jnp.bfloat16)
        turned = lax.dot_general(pick, rows, NT, preferred_element_type=jnp.float32)
        flat = jnp.concatenate([turned[i * groups:(i + 1) * groups] for i in range(per_dev)], axis=1)
        for j in range(packed.shape[0]):
            packed[j, pl.ds(e, groups, stride=local_e), :] = flat[:, j * 128:(j + 1) * 128]
    for g in range(groups):
        for j in range(packed.shape[0]):
            sent[g, :, j * 128:(j + 1) * 128] = packed[j, g * local_e:(g + 1) * local_e, :].astype(jnp.bfloat16)


def unpack_kernel(groups, per_dev, landed, out_ref, wide, tall):
    local_e = landed.shape[1]
    lanes = min(out_ref.shape[1], 128)
    for g in range(groups):
        for j in range(wide.shape[0]):
            wide[j, g * local_e:(g + 1) * local_e, :] = landed[g, :, j * 128:(j + 1) * 128].astype(jnp.float32)
    pick = order(groups, per_dev)
    for e in range(local_e):
        rows = jnp.concatenate(
            [wide[j, pl.ds(e, groups, stride=local_e), :] for j in range(wide.shape[0])], axis=1)
        stack = jnp.concatenate([rows[:, i * BLOCK:(i + 1) * BLOCK] for i in range(per_dev)], axis=0)
        turned = jnp.dot(stack.astype(jnp.bfloat16).T, pick, preferred_element_type=jnp.float32)
        if lanes < 128:
            turned = jnp.concatenate([turned, jnp.zeros((BLOCK, 128 - lanes), jnp.float32)], axis=1)
        for j in range(tall.shape[0]):
            tall[j, pl.ds(e, BLOCK, stride=local_e), :] = turned[:, j * 128:(j + 1) * 128]
    for j in range(tall.shape[0]):
        out_ref[:, j * 128:j * 128 + lanes] = tall[j, :out_ref.shape[0], :lanes].astype(jnp.bfloat16)


def table_tall(padded, weight_rows, mats_in):
    pairs = padded.shape[2]
    atoms, lanes = pairs // NBR, mats_in.shape[1]
    wide = atoms * lanes
    tall = padded[...].reshape(ORB * 16, pairs).astype(jnp.bfloat16)
    lane = lax.broadcasted_iota(jnp.int32, (8, wide), 1)[:1]
    inside = lane % lanes
    pair_of = jnp.where(inside < NBR * ORB, lane // lanes * NBR + inside // ORB, -1)
    row = lax.broadcasted_iota(jnp.int32, (pairs, wide), 0)
    spread = jnp.dot(tall, (row == pair_of).astype(jnp.bfloat16), preferred_element_type=jnp.float32)
    row = lax.broadcasted_iota(jnp.int32, (ORB * 16, wide), 0) % 16
    spread = jnp.where(row == inside % ORB, spread, 0.0).astype(jnp.bfloat16)
    p = lax.broadcasted_iota(jnp.int32, (16, ORB * 16), 0)
    of = lax.broadcasted_iota(jnp.int32, (16, ORB * 16), 1) // 16
    flat = jnp.dot((p == of).astype(jnp.bfloat16), spread, preferred_element_type=jnp.float32)
    at = lax.broadcasted_iota(jnp.int32, (pairs, lanes), 1) - NBR * ORB
    pair = lax.broadcasted_iota(jnp.int32, (pairs, lanes), 0)
    behind = jnp.dot(
        weight_rows[...].astype(jnp.bfloat16), (at == pair).astype(jnp.bfloat16), preferred_element_type=jnp.float32)
    for atom in range(atoms):
        block = flat[:, atom * lanes:(atom + 1) * lanes]
        mats_in[atom * 16:(atom + 1) * 16, :] = (block + behind if atom == 0 else block).astype(jnp.bfloat16)


def wire_kernel(inner, layers, side, sent, coupling_ref, weight_ref, near_ref, shift_ref, back_ref,
                padded, weight_rows, mats_in,
                landed, mats, weights, near, shifts, near_at, shift_at, pick_q, pick_r,
                out_ref, green, spread_q, spread_r, both, toeplitz, bands, stage,
                slot_send, slot_recv, relay_send, relay_recv, table_send, table_recv, back_send, back_recv, local_sem):
    slots, pieces, local_e, width = landed.shape
    mine = slots - 2
    chunks = sent.shape[0]
    rows_e = pieces * local_e
    late = rows_e - WINDOW
    me, slab = lax.axis_index("energy"), lax.axis_index("slab")
    slabs = lax.axis_size("slab")
    layer, i = lax.div(me, inner), lax.rem(me, inner)
    first_of_layer = layer * inner
    first_atom = slab * (chunks * HALO) + i * (mine * HALO) - HALO
    first, last = i == 0, i == inner - 1
    below, above = layer > 0, layer < layers - 1
    slab_below, slab_above = slab > 0, slab < slabs - 1
    owner, spot = lax.div(me, layers), lax.rem(me, layers)
    barrier = pltpu.get_barrier_semaphore()
    one = lambda flag: jnp.where(flag, 1, 0)

    def hail(device, row):
        pl.semaphore_signal(barrier, inc=1, device_id=(device, row), device_id_type=MESH)

    for step in range(1, inner):
        hail(first_of_layer + partner_of(i, step), slab)

    @pl.when(first & slab_below)
    def _():
        for j in range(inner):
            hail(first_of_layer + j, slab - 1)

    @pl.when(last & slab_above)
    def _():
        for j in range(inner):
            hail(first_of_layer + j, slab + 1)

    pl.when(below)(lambda: hail(me - inner, slab))
    pl.when(above)(lambda: hail(me + inner, slab))
    for j in range(layers):
        pl.when(i * layers + j != me)(lambda: hail(i * layers + j, slab))
    padded[...] = jnp.zeros_like(padded)
    weight_rows[...] = jnp.zeros_like(weight_rows)
    for p in range(ORB):
        padded[p, :ORB, :] = coupling_ref[p].astype(jnp.float32)
    weight_rows[:BAND, :] = weight_ref[:, 0, :]
    table_tall(padded, weight_rows, mats_in)

    tables = ((mats_in, mats), (near_ref, near), (shift_ref, shifts))

    @pl.when(owner == i)
    def _():
        for src, dst in tables:
            dst[spot] = src[...]

    pl.semaphore_wait(
        barrier, inner - 1 + one(slab_above) + one(slab_below) + one(above) + one(below) + layers - one(owner == i))

    def table(number, j, at, to):
        src, dst = tables[number]
        return pltpu.make_async_remote_copy(
            src_ref=src, dst_ref=dst.at[at], send_sem=table_send.at[number, j], recv_sem=table_recv.at[number, at],
            device_id=(to, slab), device_id_type=MESH)

    def outgoing(slot, step):
        to = partner_of(i, step)
        row = slab + one((slot == 0) & (to == 0)) - one((slot == slots - 1) & (to == inner - 1))
        return pltpu.make_async_remote_copy(
            src_ref=sent.at[lax.rem(to * mine + slot - 1 + chunks, chunks)], dst_ref=landed.at[slot, side + i],
            send_sem=slot_send.at[slot, step], recv_sem=slot_recv.at[slot, step],
            device_id=(first_of_layer + to, row), device_id_type=MESH)

    def incoming(slot, step):
        source = partner_of(i, step)
        return pltpu.make_async_remote_copy(
            src_ref=sent.at[0], dst_ref=landed.at[slot, side + source],
            send_sem=slot_send.at[slot, step], recv_sem=slot_recv.at[slot, step],
            device_id=(first_of_layer + source, slab), device_id_type=MESH)

    def leaves(slot, step):
        to = partner_of(i, step)
        real = ((slot > 0) | (to > 0) | slab_above) & ((slot < slots - 1) | (to < inner - 1) | slab_below)
        if step:
            return real
        return real & (((slot == 0) & first) | ((slot == slots - 1) & last))

    def comes(slot, step):
        real = ((slot > 0) | (i > 0) | slab_below) & ((slot < slots - 1) | (i < inner - 1) | slab_above)
        if step:
            return real
        return real & (((slot == 0) & first) | ((slot == slots - 1) & last))

    def send_slot(slot, carry):
        for step in range(inner):
            pl.when(leaves(slot, step))(lambda: outgoing(slot, step).start())
        return carry

    for j in range(layers):
        to = j * inner + owner

        @pl.when(to != me)
        def _():
            for number in range(3):
                table(number, j, spot, to).start()

    lax.fori_loop(0, 3, send_slot, 0)

    landed[pl.ds(1, mine), side + i] = sent[pl.ds(i * mine, mine)]

    @pl.when(i > 0)
    def _():
        landed[0, side + i] = sent[lax.rem(i * mine - 1 + chunks, chunks)]

    @pl.when(i < inner - 1)
    def _():
        landed[slots - 1, side + i] = sent[lax.rem(i * mine + mine, chunks)]

    @pl.when(first & jnp.logical_not(slab_below))
    def _():
        landed[0, side:side + inner] = jnp.zeros((inner, local_e, width), landed.dtype)

    @pl.when(last & jnp.logical_not(slab_above))
    def _():
        landed[slots - 1, side:side + inner] = jnp.zeros((inner, local_e, width), landed.dtype)

    def clear(start):
        landed[:, start:start + side] = jnp.zeros((slots, side, local_e, width), landed.dtype)

    pl.when(jnp.logical_not(below))(lambda: clear(0))
    pl.when(jnp.logical_not(above))(lambda: clear(side + inner))

    wide = NBR * PAIR
    lane = lax.broadcasted_iota(jnp.int32, (8, wide), 1)
    key_q = (lane // ORB)[:1]
    key_r = (lane // PAIR * ORB + lane % ORB)[:1]
    row = lax.broadcasted_iota(jnp.int32, (NBR * ORB, wide), 0)
    pick_q[...] = (row == key_q).astype(jnp.bfloat16)
    pick_r[...] = (row == key_r).astype(jnp.bfloat16)

    def relay(way, slot):
        start, into = (inner, 0) if way == 0 else (side, side + inner)
        return pltpu.make_async_remote_copy(
            src_ref=landed.at[slot, start:start + side], dst_ref=landed.at[slot, into:into + side],
            send_sem=relay_send.at[way, slot], recv_sem=relay_recv.at[way, slot],
            device_id=(me + inner if way == 0 else me - inner, slab), device_id_type=MESH)

    def relayed(way, slot):
        into = 0 if way == 0 else side + inner
        return pltpu.make_async_remote_copy(
            src_ref=landed.at[slot, into:into + side], dst_ref=landed.at[slot, into:into + side],
            send_sem=relay_send.at[way, slot], recv_sem=relay_recv.at[way, slot],
            device_id=(me - inner if way == 0 else me + inner, slab), device_id_type=MESH)

    def pass_on(slot):
        for step in range(inner):
            pl.when(comes(slot, step))(lambda: incoming(slot, step).wait_recv())
        pl.when(above)(lambda: relay(0, slot).start())
        pl.when(below)(lambda: relay(1, slot).start())

    for j in range(layers):
        @pl.when(i * layers + j != me)
        def _():
            for number in range(3):
                table(number, j, j, me).wait_recv()
    to_scalars = (pltpu.make_async_copy(near, near_at, local_sem.at[0]),
                  pltpu.make_async_copy(shifts, shift_at, local_sem.at[1]))
    for copy in to_scalars:
        copy.start()
    lane_of = lax.broadcasted_iota(jnp.int32, (16, WINDOW), 1)
    row_of = lax.broadcasted_iota(jnp.int32, (16, WINDOW), 0)
    place = ((lane_of + row_of == BAND - 1) & (row_of < BAND)).astype(jnp.bfloat16)
    count_pairs = mats.shape[2] - NBR * ORB
    for j in range(layers):
        column = lax.dot_general(
            eye(count_pairs), mats[j, :16, NBR * ORB:], NT, preferred_element_type=jnp.float32).astype(jnp.bfloat16)
        weights[j] = jnp.dot(column, place, preferred_element_type=jnp.float32)

    count = mats.shape[0] * mats.shape[1]
    matrices = mats[...].reshape(count, mats.shape[2])[:, :NBR * ORB]
    spread_q[...] = jnp.dot(matrices, pick_q[...], preferred_element_type=jnp.float32)
    pass_on(0)
    send_slot(3, 0)
    spread_r[...] = jnp.dot(matrices, pick_r[...], preferred_element_type=jnp.float32)
    for copy in to_scalars:
        copy.wait()
    pass_on(1)
    send_slot(4, 0)

    sub = lax.broadcasted_iota(jnp.int32, (8, WINDOW), 0)
    left_half = lax.broadcasted_iota(jnp.int32, (WINDOW, WINDOW), 1) < SPAN
    low_rows = lax.broadcasted_iota(jnp.int32, (8, wide), 0) < 4
    pair_of_atoms = 2
    zero = jnp.zeros((16, WINDOW), jnp.bfloat16)

    def window_of(m, index):
        shift = shift_at[m, 0, index]
        return shift, jnp.where(shift >= 0, 1, 0)

    def prepare(h, carry):
        m = lax.div(h, HALO // pair_of_atoms)
        for a in range(pair_of_atoms):
            atom = h * pair_of_atoms + a
            tiles = []
            for k in range(NBR):
                index = lax.rem(atom, HALO) * NBR + k
                shift, later = window_of(m, index)
                base = shift + side * local_e - BAND // 2 - later * late
                weight = weights[m, pl.ds(index, 1), :]
                tiles.append(pltpu.roll(jnp.broadcast_to(weight, (8, WINDOW)), WINDOW - BAND + 1 - base, 1))
            for step in (1, 2, 4):
                tiles = [jnp.where((sub & step) != 0, pltpu.roll(tile, step, 1), tile) for tile in tiles]
            tiles = [jnp.concatenate([tile, pltpu.roll(tile, 8, 1)], axis=0).astype(jnp.bfloat16) for tile in tiles]
            for b in range(WINDOW // 16):
                for k in range(NBR):
                    tile = pltpu.roll(tiles[k], 16 * b, 1) if b else tiles[k]
                    toeplitz[atom * NBR + k, 16 * b:16 * b + 16] = jnp.where(left_half[:16], tile, zero)
                    low = WINDOW + (16 * b - SPAN) % WINDOW
                    toeplitz[atom * NBR + k, low:low + 16] = jnp.where(left_half[:16], zero, tile)
            right = spread_r[pl.ds(pl.multiple_of(atom * 16, 16), 16), :]
            rights = (right[:8], jnp.concatenate([right[8:12], right[:4]], axis=0), right[4:12])
            for four in range(ORB // 4):
                rows = []
                for half in range(2):
                    p = four * 4 + half * 2
                    q0 = spread_q[pl.ds(atom * 16 + p, 1), :]
                    q1 = spread_q[pl.ds(atom * 16 + p + 1, 1), :]
                    rows += [q0 * rights[0], jnp.where(low_rows, q0, q1) * rights[1], q1 * rights[2]]
                both[atom, four * 48:(four + 1) * 48, :] = jnp.concatenate(rows, axis=0).astype(jnp.bfloat16)


        pl.when(lax.rem(h, 2) == 0)(lambda: pass_on(lax.div(h, 2) + 2))
        pl.when(h == 0)(lambda: [send_slot(5, 0), None][1])
        return carry

    steps = mine * HALO // pair_of_atoms
    assert slots == 6 and steps >= slots
    lax.fori_loop(0, steps, prepare, 0)

    unit = eye(128)

    def turn(slot, carry):
        pl.when(below)(lambda: relayed(0, slot).wait_recv())
        pl.when(above)(lambda: relayed(1, slot).wait_recv())
        if local_e % 16:
            for piece in range(pieces):
                stage[piece * local_e:(piece + 1) * local_e, :] = landed[slot, piece].astype(jnp.float32)
            tall = stage[...].astype(jnp.bfloat16)
        else:
            tall = landed[slot].reshape(rows_e, width)
        two = jnp.concatenate([tall[:WINDOW], tall[late:]], axis=0)
        turned = jnp.concatenate([
            lax.dot_general(unit, two[:, j * 128:(j + 1) * 128], NT, preferred_element_type=jnp.float32).astype(
                jnp.bfloat16) for j in range(width // 128)], axis=0)
        for atom in range(HALO):
            for c in range(2):
                start = (2 * atom + c) * PAIR
                for window in range(2):
                    green[window, slot * HALO + atom, :, c * WINDOW:(c + 1) * WINDOW] = (
                        turned[start:start + PAIR, window * WINDOW:(window + 1) * WINDOW])
        return carry

    lax.fori_loop(0, 2, turn, 0)

    def share(step, m, at):
        to = partner_of(i, step)
        return pltpu.make_async_remote_copy(
            src_ref=out_ref.at[to, m], dst_ref=back_ref.at[at * mine + m],
            send_sem=back_send.at[step, m], recv_sem=back_recv.at[step, m],
            device_id=(first_of_layer + to, slab), device_id_type=MESH)

    def chunk(m, carry):
        turn(m + 2, 0)
        for a in range(HALO):
            for k in range(NBR):
                index = a * NBR + k
                later = window_of(m, index)[1]
                partner = jnp.clip(near_at[m, 0, index] - first_atom, 0, slots * HALO - 1)
                banded = jnp.dot(
                    green[later, partner], toeplitz[m * HALO * NBR + index], preferred_element_type=jnp.float32)
                bands[a, k * PAIR:(k + 1) * PAIR, :] = banded.astype(jnp.bfloat16)
        parts = []
        totals = [jnp.dot(both[m * HALO + a], bands[a], preferred_element_type=jnp.float32) for a in range(HALO)]
        for total in totals:
            turned = lax.dot_general(unit, total.astype(jnp.bfloat16), NT, preferred_element_type=jnp.float32)
            parts += [turned[:SPAN], turned[SPAN:]]
        whole = jnp.concatenate(parts, axis=1)
        for d in range(inner):
            out_ref[d, m] = whole[d * local_e:(d + 1) * local_e].astype(jnp.bfloat16)
        for step in range(1, inner):
            share(step, m, i).start()
        back_ref[i * mine + m] = out_ref[i, m]
        return carry

    lax.fori_loop(0, mine, chunk, 0)

    for j in range(layers):
        @pl.when(j * inner + owner != me)
        def _():
            for number in range(3):
                table(number, j, j, me).wait_send()

    def sent_slot(slot, carry):
        for step in range(inner):
            pl.when(leaves(slot, step))(lambda: outgoing(slot, step).wait_send())
        pl.when(above)(lambda: relay(0, slot).wait_send())
        pl.when(below)(lambda: relay(1, slot).wait_send())
        return carry

    lax.fori_loop(0, slots, sent_slot, 0)

    def finish(m, carry):
        for step in range(1, inner):
            share(step, m, partner_of(i, step)).wait_recv()
            share(step, m, i).wait_send()
        return carry

    lax.fori_loop(0, mine, finish, 0)


def on_device(green_blocks, couplings, band_weights, neighbours, shifts):
    groups = lax.axis_size("energy")
    local_e, slab_count = green_blocks.shape[3:]
    per_dev = slab_count // groups
    width = per_dev * BLOCK
    pairs = per_dev * NBR
    lanes = NBR * ORB + pairs
    inner = SPAN // local_e
    layers = groups // inner
    side = pl.cdiv(REACH, local_e)
    pieces = inner + 2 * side
    mine = groups // inner
    slots = mine + 2
    assert per_dev == HALO and side <= inner and pieces * local_e >= WINDOW
    vmem = pl.BlockSpec(memory_space=pltpu.VMEM)
    smem = pl.BlockSpec(memory_space=pltpu.SMEM)
    blocks = jax.ShapeDtypeStruct((groups, local_e, width), jnp.bfloat16)
    wide = pltpu.VMEM((pl.cdiv(slab_count, 128), BLOCK * local_e, 128), jnp.float32)
    packed = pltpu.VMEM((width // 128, local_e * groups, 128), jnp.float32)
    room = pltpu.CompilerParams(vmem_limit_bytes=32 * 1024 * 1024)

    sent = pl.pallas_call(
        functools.partial(pack_kernel, groups, per_dev),
        out_shape=blocks, in_specs=[vmem], out_specs=vmem,
        scratch_shapes=[wide, packed], compiler_params=room,
    )(green_blocks.reshape(BLOCK * local_e, slab_count))
    back = pl.pallas_call(
        functools.partial(wire_kernel, inner, layers, side),
        out_shape=blocks,
        in_specs=[vmem] * 5,
        out_specs=vmem,
        scratch_shapes=[
            pltpu.VMEM((ORB, 16, pairs), jnp.float32), pltpu.VMEM((16, pairs), jnp.float32),
            pltpu.VMEM((per_dev * 16, lanes), jnp.bfloat16),
            pltpu.VMEM((slots, pieces, local_e, width), jnp.bfloat16),
            pltpu.VMEM((layers, per_dev * 16, lanes), jnp.bfloat16),
            pltpu.VMEM((layers, pairs, WINDOW), jnp.float32),
            pltpu.VMEM((layers, 1, pairs), jnp.int32),
            pltpu.VMEM((layers, 1, pairs), jnp.int32),
            pltpu.SMEM((layers, 1, pairs), jnp.int32),
            pltpu.SMEM((layers, 1, pairs), jnp.int32),
            pltpu.VMEM((NBR * ORB, NBR * PAIR), jnp.bfloat16), pltpu.VMEM((NBR * ORB, NBR * PAIR), jnp.bfloat16),
            pltpu.VMEM((inner, mine, local_e, width), jnp.bfloat16),
            pltpu.VMEM((2, slots * HALO, PAIR, 2 * WINDOW), jnp.bfloat16),
            pltpu.VMEM((mine * HALO * 16, NBR * PAIR), jnp.float32),
            pltpu.VMEM((mine * HALO * 16, NBR * PAIR), jnp.float32),
            pltpu.VMEM((mine * HALO, PAIR, NBR * PAIR), jnp.bfloat16),
            pltpu.VMEM((mine * HALO * NBR, 2 * WINDOW, WINDOW), jnp.bfloat16),
            pltpu.VMEM((HALO, NBR * PAIR, WINDOW), jnp.bfloat16),
            pltpu.VMEM((pieces * local_e if local_e % 16 else 8, width), jnp.float32),
            pltpu.SemaphoreType.DMA((slots, inner)), pltpu.SemaphoreType.DMA((slots, inner)),
            pltpu.SemaphoreType.DMA((2, slots)), pltpu.SemaphoreType.DMA((2, slots)),
            pltpu.SemaphoreType.DMA((3, layers)), pltpu.SemaphoreType.DMA((3, layers)),
            pltpu.SemaphoreType.DMA((inner, mine)), pltpu.SemaphoreType.DMA((inner, mine)),
            pltpu.SemaphoreType.DMA((2,)),
        ],
        compiler_params=pltpu.CompilerParams(
            collective_id=0, has_side_effects=True, vmem_limit_bytes=48 * 1024 * 1024),
    )(sent, couplings.reshape(ORB, ORB, pairs), band_weights, neighbours, shifts)
    result = pl.pallas_call(
        functools.partial(unpack_kernel, groups, per_dev),
        out_shape=jax.ShapeDtypeStruct((BLOCK * local_e, slab_count), jnp.bfloat16),
        in_specs=[vmem], out_specs=vmem,
        scratch_shapes=[packed, wide], compiler_params=room,
    )(back)
    return result.reshape(2, ORB, ORB, local_e, slab_count)


def solution(mesh):
    return jax.shard_map(
        on_device,
        mesh=mesh,
        in_specs=(
            P(None, None, None, "energy", "slab"),
            P(None, None, "slab", "energy"),
            P(None, "slab", "energy"),
            P("slab", "energy"),
            P("slab", "energy"),
        ),
        out_specs=P(None, None, None, "energy", "slab"),
        check_vma=False,
    )
```

```python
import functools

import jax
import jax.numpy as jnp
from jax import lax
from jax.experimental import pallas as pl
from jax.experimental.pallas import tpu as pltpu
from jax.sharding import PartitionSpec as P

ORB = 12
NBR = 16
BAND = 9
SHIFT = 32
HALO = 4
BLOCK = 2 * ORB * ORB
PAIR = ORB * ORB
REACH = SHIFT + BAND // 2
SPAN = 64
WINDOW = 128

MESH = pl.DeviceIdType.MESH
NT = (((1,), (1,)), ((), ()))


def order(groups, per_dev):
    count = groups * per_dev
    row = lax.broadcasted_iota(jnp.int32, (count, count), 0)
    atom = lax.broadcasted_iota(jnp.int32, (count, count), 1)
    return (atom == (row % groups) * per_dev + row // groups).astype(jnp.bfloat16)


def eye(count):
    row = lax.broadcasted_iota(jnp.int32, (count, count), 0)
    column = lax.broadcasted_iota(jnp.int32, (count, count), 1)
    return (row == column).astype(jnp.bfloat16)


def partner_of(i, step):
    out, bit = 0, 1
    while bit <= step:
        out = out + bit * lax.rem(lax.div(i, bit) + step // bit, 2)
        bit *= 2
    return lax.div(i, bit) * bit + out if step else i


def pack_kernel(groups, per_dev, x_ref, sent, wide, packed):
    local_e = sent.shape[1]
    tiles = wide.shape[0]
    count = x_ref.shape[1]
    lanes = min(count, 128)
    if lanes < 128:
        wide[...] = jnp.zeros_like(wide)
    for j in range(tiles):
        wide[j, :x_ref.shape[0], :lanes] = x_ref[:, j * 128:j * 128 + lanes].astype(jnp.float32)
    pick = order(groups, per_dev)
    for e in range(local_e):
        rows = jnp.concatenate([wide[j, pl.ds(e, BLOCK, stride=local_e), :] for j in range(tiles)], axis=1)
        rows = rows[:, :count].astype(jnp.bfloat16)
        turned = lax.dot_general(pick, rows, NT, preferred_element_type=jnp.float32)
        flat = jnp.concatenate([turned[i * groups:(i + 1) * groups] for i in range(per_dev)], axis=1)
        for j in range(packed.shape[0]):
            packed[j, pl.ds(e, groups, stride=local_e), :] = flat[:, j * 128:(j + 1) * 128]
    for g in range(groups):
        for j in range(packed.shape[0]):
            sent[g, :, j * 128:(j + 1) * 128] = packed[j, g * local_e:(g + 1) * local_e, :].astype(jnp.bfloat16)


def unpack_kernel(groups, per_dev, landed, out_ref, wide, tall):
    local_e = landed.shape[1]
    lanes = min(out_ref.shape[1], 128)
    for g in range(groups):
        for j in range(wide.shape[0]):
            wide[j, g * local_e:(g + 1) * local_e, :] = landed[g, :, j * 128:(j + 1) * 128].astype(jnp.float32)
    pick = order(groups, per_dev)
    for e in range(local_e):
        rows = jnp.concatenate(
            [wide[j, pl.ds(e, groups, stride=local_e), :] for j in range(wide.shape[0])], axis=1)
        stack = jnp.concatenate([rows[:, i * BLOCK:(i + 1) * BLOCK] for i in range(per_dev)], axis=0)
        turned = jnp.dot(stack.astype(jnp.bfloat16).T, pick, preferred_element_type=jnp.float32)
        if lanes < 128:
            turned = jnp.concatenate([turned, jnp.zeros((BLOCK, 128 - lanes), jnp.float32)], axis=1)
        for j in range(tall.shape[0]):
            tall[j, pl.ds(e, BLOCK, stride=local_e), :] = turned[:, j * 128:(j + 1) * 128]
    for j in range(tall.shape[0]):
        out_ref[:, j * 128:j * 128 + lanes] = tall[j, :out_ref.shape[0], :lanes].astype(jnp.bfloat16)


def table_tall(padded, weight_rows, mats_in):
    pairs = padded.shape[2]
    atoms, lanes = pairs // NBR, mats_in.shape[1]
    wide = atoms * lanes
    tall = padded[...].reshape(ORB * 16, pairs).astype(jnp.bfloat16)
    lane = lax.broadcasted_iota(jnp.int32, (8, wide), 1)[:1]
    inside = lane % lanes
    pair_of = jnp.where(inside < NBR * ORB, lane // lanes * NBR + inside // ORB, -1)
    row = lax.broadcasted_iota(jnp.int32, (pairs, wide), 0)
    spread = jnp.dot(tall, (row == pair_of).astype(jnp.bfloat16), preferred_element_type=jnp.float32)
    row = lax.broadcasted_iota(jnp.int32, (ORB * 16, wide), 0) % 16
    spread = jnp.where(row == inside % ORB, spread, 0.0).astype(jnp.bfloat16)
    p = lax.broadcasted_iota(jnp.int32, (16, ORB * 16), 0)
    of = lax.broadcasted_iota(jnp.int32, (16, ORB * 16), 1) // 16
    flat = jnp.dot((p == of).astype(jnp.bfloat16), spread, preferred_element_type=jnp.float32)
    at = lax.broadcasted_iota(jnp.int32, (pairs, lanes), 1) - NBR * ORB
    pair = lax.broadcasted_iota(jnp.int32, (pairs, lanes), 0)
    behind = jnp.dot(
        weight_rows[...].astype(jnp.bfloat16), (at == pair).astype(jnp.bfloat16), preferred_element_type=jnp.float32)
    for atom in range(atoms):
        block = flat[:, atom * lanes:(atom + 1) * lanes]
        mats_in[atom * 16:(atom + 1) * 16, :] = (block + behind if atom == 0 else block).astype(jnp.bfloat16)


def wire_kernel(inner, layers, side, sent, coupling_ref, weight_ref, near_ref, shift_ref, back_ref,
                padded, weight_rows, mats_in,
                landed, mats, weights, near, shifts, near_at, shift_at, pick_q, pick_r,
                out_ref, green, spread_q, spread_r, both, toeplitz, bands, stage,
                slot_send, slot_recv, relay_send, relay_recv, table_send, table_recv, back_send, back_recv, local_sem):
    slots, pieces, local_e, width = landed.shape
    mine = slots - 2
    chunks = sent.shape[0]
    rows_e = pieces * local_e
    late = rows_e - WINDOW
    me, slab = lax.axis_index("energy"), lax.axis_index("slab")
    slabs = lax.axis_size("slab")
    layer, i = lax.div(me, inner), lax.rem(me, inner)
    first_of_layer = layer * inner
    first_atom = slab * (chunks * HALO) + i * (mine * HALO) - HALO
    first, last = i == 0, i == inner - 1
    below, above = layer > 0, layer < layers - 1
    slab_below, slab_above = slab > 0, slab < slabs - 1
    owner, spot = lax.div(me, layers), lax.rem(me, layers)
    barrier = pltpu.get_barrier_semaphore()
    one = lambda flag: jnp.where(flag, 1, 0)

    def hail(device, row):
        pl.semaphore_signal(barrier, inc=1, device_id=(device, row), device_id_type=MESH)

    for step in range(1, inner):
        hail(first_of_layer + partner_of(i, step), slab)

    @pl.when(first & slab_below)
    def _():
        for j in range(inner):
            hail(first_of_layer + j, slab - 1)

    @pl.when(last & slab_above)
    def _():
        for j in range(inner):
            hail(first_of_layer + j, slab + 1)

    pl.when(below)(lambda: hail(me - inner, slab))
    pl.when(above)(lambda: hail(me + inner, slab))
    for j in range(layers):
        pl.when(i * layers + j != me)(lambda: hail(i * layers + j, slab))
    padded[...] = jnp.zeros_like(padded)
    weight_rows[...] = jnp.zeros_like(weight_rows)
    for p in range(ORB):
        padded[p, :ORB, :] = coupling_ref[p].astype(jnp.float32)
    weight_rows[:BAND, :] = weight_ref[:, 0, :]
    table_tall(padded, weight_rows, mats_in)

    tables = ((mats_in, mats), (near_ref, near), (shift_ref, shifts))

    @pl.when(owner == i)
    def _():
        for src, dst in tables:
            dst[spot] = src[...]

    pl.semaphore_wait(
        barrier, inner - 1 + one(slab_above) + one(slab_below) + one(above) + one(below) + layers - one(owner == i))

    def table(number, j, at, to):
        src, dst = tables[number]
        return pltpu.make_async_remote_copy(
            src_ref=src, dst_ref=dst.at[at], send_sem=table_send.at[number, j], recv_sem=table_recv.at[number, at],
            device_id=(to, slab), device_id_type=MESH)

    def outgoing(slot, step):
        to = partner_of(i, step)
        row = slab + one((slot == 0) & (to == 0)) - one((slot == slots - 1) & (to == inner - 1))
        return pltpu.make_async_remote_copy(
            src_ref=sent.at[lax.rem(to * mine + slot - 1 + chunks, chunks)], dst_ref=landed.at[slot, side + i],
            send_sem=slot_send.at[slot, step], recv_sem=slot_recv.at[slot, step],
            device_id=(first_of_layer + to, row), device_id_type=MESH)

    def incoming(slot, step):
        source = partner_of(i, step)
        return pltpu.make_async_remote_copy(
            src_ref=sent.at[0], dst_ref=landed.at[slot, side + source],
            send_sem=slot_send.at[slot, step], recv_sem=slot_recv.at[slot, step],
            device_id=(first_of_layer + source, slab), device_id_type=MESH)

    def leaves(slot, step):
        to = partner_of(i, step)
        real = ((slot > 0) | (to > 0) | slab_above) & ((slot < slots - 1) | (to < inner - 1) | slab_below)
        if step:
            return real
        return real & (((slot == 0) & first) | ((slot == slots - 1) & last))

    def comes(slot, step):
        real = ((slot > 0) | (i > 0) | slab_below) & ((slot < slots - 1) | (i < inner - 1) | slab_above)
        if step:
            return real
        return real & (((slot == 0) & first) | ((slot == slots - 1) & last))

    def send_slot(slot, carry):
        for step in range(inner):
            pl.when(leaves(slot, step))(lambda: outgoing(slot, step).start())
        return carry

    for j in range(layers):
        to = j * inner + owner

        @pl.when(to != me)
        def _():
            for number in range(3):
                table(number, j, spot, to).start()

    lax.fori_loop(0, 3, send_slot, 0)

    landed[pl.ds(1, mine), side + i] = sent[pl.ds(i * mine, mine)]

    @pl.when(i > 0)
    def _():
        landed[0, side + i] = sent[lax.rem(i * mine - 1 + chunks, chunks)]

    @pl.when(i < inner - 1)
    def _():
        landed[slots - 1, side + i] = sent[lax.rem(i * mine + mine, chunks)]

    @pl.when(first & jnp.logical_not(slab_below))
    def _():
        landed[0, side:side + inner] = jnp.zeros((inner, local_e, width), landed.dtype)

    @pl.when(last & jnp.logical_not(slab_above))
    def _():
        landed[slots - 1, side:side + inner] = jnp.zeros((inner, local_e, width), landed.dtype)

    def clear(start):
        landed[:, start:start + side] = jnp.zeros((slots, side, local_e, width), landed.dtype)

    pl.when(jnp.logical_not(below))(lambda: clear(0))
    pl.when(jnp.logical_not(above))(lambda: clear(side + inner))

    wide = NBR * PAIR
    lane = lax.broadcasted_iota(jnp.int32, (8, wide), 1)
    key_q = (lane // ORB)[:1]
    key_r = (lane // PAIR * ORB + lane % ORB)[:1]
    row = lax.broadcasted_iota(jnp.int32, (NBR * ORB, wide), 0)
    pick_q[...] = (row == key_q).astype(jnp.bfloat16)
    pick_r[...] = (row == key_r).astype(jnp.bfloat16)

    def relay(way, slot):
        start, into = (inner, 0) if way == 0 else (side, side + inner)
        return pltpu.make_async_remote_copy(
            src_ref=landed.at[slot, start:start + side], dst_ref=landed.at[slot, into:into + side],
            send_sem=relay_send.at[way, slot], recv_sem=relay_recv.at[way, slot],
            device_id=(me + inner if way == 0 else me - inner, slab), device_id_type=MESH)

    def relayed(way, slot):
        into = 0 if way == 0 else side + inner
        return pltpu.make_async_remote_copy(
            src_ref=landed.at[slot, into:into + side], dst_ref=landed.at[slot, into:into + side],
            send_sem=relay_send.at[way, slot], recv_sem=relay_recv.at[way, slot],
            device_id=(me - inner if way == 0 else me + inner, slab), device_id_type=MESH)

    def pass_on(slot):
        for step in range(inner):
            pl.when(comes(slot, step))(lambda: incoming(slot, step).wait_recv())
        pl.when(above)(lambda: relay(0, slot).start())
        pl.when(below)(lambda: relay(1, slot).start())

    for j in range(layers):
        @pl.when(i * layers + j != me)
        def _():
            for number in range(3):
                table(number, j, j, me).wait_recv()
    to_scalars = (pltpu.make_async_copy(near, near_at, local_sem.at[0]),
                  pltpu.make_async_copy(shifts, shift_at, local_sem.at[1]))
    for copy in to_scalars:
        copy.start()
    lane_of = lax.broadcasted_iota(jnp.int32, (16, WINDOW), 1)
    row_of = lax.broadcasted_iota(jnp.int32, (16, WINDOW), 0)
    place = ((lane_of + row_of == BAND - 1) & (row_of < BAND)).astype(jnp.bfloat16)
    count_pairs = mats.shape[2] - NBR * ORB
    for j in range(layers):
        column = lax.dot_general(
            eye(count_pairs), mats[j, :16, NBR * ORB:], NT, preferred_element_type=jnp.float32).astype(jnp.bfloat16)
        weights[j] = jnp.dot(column, place, preferred_element_type=jnp.float32)

    count = mats.shape[0] * mats.shape[1]
    matrices = mats[...].reshape(count, mats.shape[2])[:, :NBR * ORB]
    spread_q[...] = jnp.dot(matrices, pick_q[...], preferred_element_type=jnp.float32)
    pass_on(0)
    send_slot(3, 0)
    spread_r[...] = jnp.dot(matrices, pick_r[...], preferred_element_type=jnp.float32)
    for copy in to_scalars:
        copy.wait()
    pass_on(1)
    send_slot(4, 0)

    sub = lax.broadcasted_iota(jnp.int32, (8, WINDOW), 0)
    left_half = lax.broadcasted_iota(jnp.int32, (WINDOW, WINDOW), 1) < SPAN
    low_rows = lax.broadcasted_iota(jnp.int32, (8, wide), 0) < 4
    batch = HALO
    zero = jnp.zeros((16, WINDOW), jnp.bfloat16)

    def window_of(m, index):
        shift = shift_at[m, 0, index]
        return shift, jnp.where(shift >= 0, 1, 0)

    def prepare(h, carry):
        m = lax.div(h, HALO // batch)
        tiles = []
        first_pair = h * batch * NBR
        for k in range(batch * NBR):
            index = lax.rem(h * batch, HALO) * NBR + k
            shift, later = window_of(m, index)
            base = shift + side * local_e - BAND // 2 - later * late
            weight = weights[m, pl.ds(index, 1), :]
            tiles.append(pltpu.roll(jnp.broadcast_to(weight, (8, WINDOW)), WINDOW - BAND + 1 - base, 1))
        for step in (1, 2, 4):
            tiles = [jnp.where((sub & step) != 0, pltpu.roll(tile, step, 1), tile) for tile in tiles]
        tiles = [jnp.concatenate([tile, pltpu.roll(tile, 8, 1)], axis=0).astype(jnp.bfloat16) for tile in tiles]
        for b in range(WINDOW // 16):
            for k in range(batch * NBR):
                tile = pltpu.roll(tiles[k], 16 * b, 1) if b else tiles[k]
                toeplitz[first_pair + k, 16 * b:16 * b + 16] = jnp.where(left_half[:16], tile, zero)
                low = WINDOW + (16 * b - SPAN) % WINDOW
                toeplitz[first_pair + k, low:low + 16] = jnp.where(left_half[:16], zero, tile)
        for a in range(batch):
            atom = h * batch + a
            right = spread_r[pl.ds(pl.multiple_of(atom * 16, 16), 16), :]
            rights = (right[:8], jnp.concatenate([right[8:12], right[:4]], axis=0), right[4:12])
            for four in range(ORB // 4):
                rows = []
                for half in range(2):
                    p = four * 4 + half * 2
                    q0 = spread_q[pl.ds(atom * 16 + p, 1), :]
                    q1 = spread_q[pl.ds(atom * 16 + p + 1, 1), :]
                    rows += [q0 * rights[0], jnp.where(low_rows, q0, q1) * rights[1], q1 * rights[2]]
                both[atom, four * 48:(four + 1) * 48, :] = jnp.concatenate(rows, axis=0).astype(jnp.bfloat16)


        pass_on(h + 2)
        pl.when(h == 0)(lambda: [send_slot(5, 0), None][1])
        return carry

    steps = mine * HALO // batch
    assert steps == slots - 2
    lax.fori_loop(0, steps, prepare, 0)

    unit = eye(128)

    def turn(slot, carry):
        pl.when(below)(lambda: relayed(0, slot).wait_recv())
        pl.when(above)(lambda: relayed(1, slot).wait_recv())
        if local_e % 16:
            for piece in range(pieces):
                stage[piece * local_e:(piece + 1) * local_e, :] = landed[slot, piece].astype(jnp.float32)
            tall = stage[...].astype(jnp.bfloat16)
        else:
            tall = landed[slot].reshape(rows_e, width)
        two = jnp.concatenate([tall[:WINDOW], tall[late:]], axis=0)
        turned = jnp.concatenate([
            lax.dot_general(unit, two[:, j * 128:(j + 1) * 128], NT, preferred_element_type=jnp.float32).astype(
                jnp.bfloat16) for j in range(width // 128)], axis=0)
        for atom in range(HALO):
            for c in range(2):
                start = (2 * atom + c) * PAIR
                for window in range(2):
                    green[window, slot * HALO + atom, :, c * WINDOW:(c + 1) * WINDOW] = (
                        turned[start:start + PAIR, window * WINDOW:(window + 1) * WINDOW])
        return carry

    lax.fori_loop(0, 2, turn, 0)

    def share(step, m, at):
        to = partner_of(i, step)
        return pltpu.make_async_remote_copy(
            src_ref=out_ref.at[to, m], dst_ref=back_ref.at[at * mine + m],
            send_sem=back_send.at[step, m], recv_sem=back_recv.at[step, m],
            device_id=(first_of_layer + to, slab), device_id_type=MESH)

    def chunk(m, carry):
        turn(m + 2, 0)
        for a in range(HALO):
            for k in range(NBR):
                index = a * NBR + k
                later = window_of(m, index)[1]
                partner = jnp.clip(near_at[m, 0, index] - first_atom, 0, slots * HALO - 1)
                banded = jnp.dot(
                    green[later, partner], toeplitz[m * HALO * NBR + index], preferred_element_type=jnp.float32)
                bands[a, k * PAIR:(k + 1) * PAIR, :] = banded.astype(jnp.bfloat16)
        parts = []
        totals = [jnp.dot(both[m * HALO + a], bands[a], preferred_element_type=jnp.float32) for a in range(HALO)]
        for total in totals:
            turned = lax.dot_general(unit, total.astype(jnp.bfloat16), NT, preferred_element_type=jnp.float32)
            parts += [turned[:SPAN], turned[SPAN:]]
        whole = jnp.concatenate(parts, axis=1)
        for d in range(inner):
            out_ref[d, m] = whole[d * local_e:(d + 1) * local_e].astype(jnp.bfloat16)
        for step in range(1, inner):
            share(step, m, i).start()
        back_ref[i * mine + m] = out_ref[i, m]
        return carry

    lax.fori_loop(0, mine, chunk, 0)

    for j in range(layers):
        @pl.when(j * inner + owner != me)
        def _():
            for number in range(3):
                table(number, j, j, me).wait_send()

    def sent_slot(slot, carry):
        for step in range(inner):
            pl.when(leaves(slot, step))(lambda: outgoing(slot, step).wait_send())
        pl.when(above)(lambda: relay(0, slot).wait_send())
        pl.when(below)(lambda: relay(1, slot).wait_send())
        return carry

    lax.fori_loop(0, slots, sent_slot, 0)

    def finish(m, carry):
        for step in range(1, inner):
            share(step, m, partner_of(i, step)).wait_recv()
            share(step, m, i).wait_send()
        return carry

    lax.fori_loop(0, mine, finish, 0)


def on_device(green_blocks, couplings, band_weights, neighbours, shifts):
    groups = lax.axis_size("energy")
    local_e, slab_count = green_blocks.shape[3:]
    per_dev = slab_count // groups
    width = per_dev * BLOCK
    pairs = per_dev * NBR
    lanes = NBR * ORB + pairs
    inner = SPAN // local_e
    layers = groups // inner
    side = pl.cdiv(REACH, local_e)
    pieces = inner + 2 * side
    mine = groups // inner
    slots = mine + 2
    assert per_dev == HALO and side <= inner and pieces * local_e >= WINDOW
    vmem = pl.BlockSpec(memory_space=pltpu.VMEM)
    smem = pl.BlockSpec(memory_space=pltpu.SMEM)
    blocks = jax.ShapeDtypeStruct((groups, local_e, width), jnp.bfloat16)
    wide = pltpu.VMEM((pl.cdiv(slab_count, 128), BLOCK * local_e, 128), jnp.float32)
    packed = pltpu.VMEM((width // 128, local_e * groups, 128), jnp.float32)
    room = pltpu.CompilerParams(vmem_limit_bytes=32 * 1024 * 1024)

    sent = pl.pallas_call(
        functools.partial(pack_kernel, groups, per_dev),
        out_shape=blocks, in_specs=[vmem], out_specs=vmem,
        scratch_shapes=[wide, packed], compiler_params=room,
    )(green_blocks.reshape(BLOCK * local_e, slab_count))
    back = pl.pallas_call(
        functools.partial(wire_kernel, inner, layers, side),
        out_shape=blocks,
        in_specs=[vmem] * 5,
        out_specs=vmem,
        scratch_shapes=[
            pltpu.VMEM((ORB, 16, pairs), jnp.float32), pltpu.VMEM((16, pairs), jnp.float32),
            pltpu.VMEM((per_dev * 16, lanes), jnp.bfloat16),
            pltpu.VMEM((slots, pieces, local_e, width), jnp.bfloat16),
            pltpu.VMEM((layers, per_dev * 16, lanes), jnp.bfloat16),
            pltpu.VMEM((layers, pairs, WINDOW), jnp.float32),
            pltpu.VMEM((layers, 1, pairs), jnp.int32),
            pltpu.VMEM((layers, 1, pairs), jnp.int32),
            pltpu.SMEM((layers, 1, pairs), jnp.int32),
            pltpu.SMEM((layers, 1, pairs), jnp.int32),
            pltpu.VMEM((NBR * ORB, NBR * PAIR), jnp.bfloat16), pltpu.VMEM((NBR * ORB, NBR * PAIR), jnp.bfloat16),
            pltpu.VMEM((inner, mine, local_e, width), jnp.bfloat16),
            pltpu.VMEM((2, slots * HALO, PAIR, 2 * WINDOW), jnp.bfloat16),
            pltpu.VMEM((mine * HALO * 16, NBR * PAIR), jnp.float32),
            pltpu.VMEM((mine * HALO * 16, NBR * PAIR), jnp.float32),
            pltpu.VMEM((mine * HALO, PAIR, NBR * PAIR), jnp.bfloat16),
            pltpu.VMEM((mine * HALO * NBR, 2 * WINDOW, WINDOW), jnp.bfloat16),
            pltpu.VMEM((HALO, NBR * PAIR, WINDOW), jnp.bfloat16),
            pltpu.VMEM((pieces * local_e if local_e % 16 else 8, width), jnp.float32),
            pltpu.SemaphoreType.DMA((slots, inner)), pltpu.SemaphoreType.DMA((slots, inner)),
            pltpu.SemaphoreType.DMA((2, slots)), pltpu.SemaphoreType.DMA((2, slots)),
            pltpu.SemaphoreType.DMA((3, layers)), pltpu.SemaphoreType.DMA((3, layers)),
            pltpu.SemaphoreType.DMA((inner, mine)), pltpu.SemaphoreType.DMA((inner, mine)),
            pltpu.SemaphoreType.DMA((2,)),
        ],
        compiler_params=pltpu.CompilerParams(
            collective_id=0, has_side_effects=True, vmem_limit_bytes=48 * 1024 * 1024),
    )(sent, couplings.reshape(ORB, ORB, pairs), band_weights, neighbours, shifts)
    result = pl.pallas_call(
        functools.partial(unpack_kernel, groups, per_dev),
        out_shape=jax.ShapeDtypeStruct((BLOCK * local_e, slab_count), jnp.bfloat16),
        in_specs=[vmem], out_specs=vmem,
        scratch_shapes=[packed, wide], compiler_params=room,
    )(back)
    return result.reshape(2, ORB, ORB, local_e, slab_count)


def solution(mesh):
    return jax.shard_map(
        on_device,
        mesh=mesh,
        in_specs=(
            P(None, None, None, "energy", "slab"),
            P(None, None, "slab", "energy"),
            P(None, "slab", "energy"),
            P("slab", "energy"),
            P("slab", "energy"),
        ),
        out_specs=P(None, None, None, "energy", "slab"),
        check_vma=False,
    )
```

```python
import functools

import jax
import jax.numpy as jnp
from jax import lax
from jax.experimental import pallas as pl
from jax.experimental.pallas import tpu as pltpu
from jax.sharding import PartitionSpec as P

ORB = 12
NBR = 16
BAND = 9
SHIFT = 32
HALO = 4
BLOCK = 2 * ORB * ORB
PAIR = ORB * ORB
REACH = SHIFT + BAND // 2
SPAN = 64
WINDOW = 128

MESH = pl.DeviceIdType.MESH
NT = (((1,), (1,)), ((), ()))


def order(groups, per_dev):
    count = groups * per_dev
    row = lax.broadcasted_iota(jnp.int32, (count, count), 0)
    atom = lax.broadcasted_iota(jnp.int32, (count, count), 1)
    return (atom == (row % groups) * per_dev + row // groups).astype(jnp.bfloat16)


def eye(count):
    row = lax.broadcasted_iota(jnp.int32, (count, count), 0)
    column = lax.broadcasted_iota(jnp.int32, (count, count), 1)
    return (row == column).astype(jnp.bfloat16)


def partner_of(i, step):
    out, bit = 0, 1
    while bit <= step:
        out = out + bit * lax.rem(lax.div(i, bit) + step // bit, 2)
        bit *= 2
    return lax.div(i, bit) * bit + out if step else i


def pack_kernel(groups, per_dev, x_ref, sent, wide, packed):
    local_e = sent.shape[1]
    tiles = wide.shape[0]
    count = x_ref.shape[1]
    lanes = min(count, 128)
    if lanes < 128:
        wide[...] = jnp.zeros_like(wide)
    for j in range(tiles):
        wide[j, :x_ref.shape[0], :lanes] = x_ref[:, j * 128:j * 128 + lanes].astype(jnp.float32)
    pick = order(groups, per_dev)
    for e in range(local_e):
        rows = jnp.concatenate([wide[j, pl.ds(e, BLOCK, stride=local_e), :] for j in range(tiles)], axis=1)
        rows = rows[:, :count].astype(jnp.bfloat16)
        turned = lax.dot_general(pick, rows, NT, preferred_element_type=jnp.float32)
        flat = jnp.concatenate([turned[i * groups:(i + 1) * groups] for i in range(per_dev)], axis=1)
        for j in range(packed.shape[0]):
            packed[j, pl.ds(e, groups, stride=local_e), :] = flat[:, j * 128:(j + 1) * 128]
    for g in range(groups):
        for j in range(packed.shape[0]):
            sent[g, :, j * 128:(j + 1) * 128] = packed[j, g * local_e:(g + 1) * local_e, :].astype(jnp.bfloat16)


def unpack_kernel(groups, per_dev, landed, out_ref, wide, tall):
    local_e = landed.shape[1]
    lanes = min(out_ref.shape[1], 128)
    for g in range(groups):
        for j in range(wide.shape[0]):
            wide[j, g * local_e:(g + 1) * local_e, :] = landed[g, :, j * 128:(j + 1) * 128].astype(jnp.float32)
    pick = order(groups, per_dev)
    some = min(4, local_e)
    for start in range(0, local_e, some):
        stacks = []
        for e in range(start, start + some):
            rows = jnp.concatenate(
                [wide[j, pl.ds(e, groups, stride=local_e), :] for j in range(wide.shape[0])], axis=1)
            stacks.append(jnp.concatenate(
                [rows[:, i * BLOCK:(i + 1) * BLOCK] for i in range(per_dev)], axis=0).astype(jnp.bfloat16))
        turns = [jnp.dot(stack.T, pick, preferred_element_type=jnp.float32) for stack in stacks]
        for e, turned in zip(range(start, start + some), turns):
            if lanes < 128:
                turned = jnp.concatenate([turned, jnp.zeros((BLOCK, 128 - lanes), jnp.float32)], axis=1)
            for j in range(tall.shape[0]):
                tall[j, pl.ds(e, BLOCK, stride=local_e), :] = turned[:, j * 128:(j + 1) * 128]
    for j in range(tall.shape[0]):
        out_ref[:, j * 128:j * 128 + lanes] = tall[j, :out_ref.shape[0], :lanes].astype(jnp.bfloat16)


def table_tall(padded, weight_rows, mats_in):
    pairs = padded.shape[2]
    atoms, lanes = pairs // NBR, mats_in.shape[1]
    wide = atoms * lanes
    tall = padded[...].reshape(ORB * 16, pairs).astype(jnp.bfloat16)
    lane = lax.broadcasted_iota(jnp.int32, (8, wide), 1)[:1]
    inside = lane % lanes
    pair_of = jnp.where(inside < NBR * ORB, lane // lanes * NBR + inside // ORB, -1)
    row = lax.broadcasted_iota(jnp.int32, (pairs, wide), 0)
    spread = jnp.dot(tall, (row == pair_of).astype(jnp.bfloat16), preferred_element_type=jnp.float32)
    row = lax.broadcasted_iota(jnp.int32, (ORB * 16, wide), 0) % 16
    spread = jnp.where(row == inside % ORB, spread, 0.0).astype(jnp.bfloat16)
    p = lax.broadcasted_iota(jnp.int32, (16, ORB * 16), 0)
    of = lax.broadcasted_iota(jnp.int32, (16, ORB * 16), 1) // 16
    flat = jnp.dot((p == of).astype(jnp.bfloat16), spread, preferred_element_type=jnp.float32)
    at = lax.broadcasted_iota(jnp.int32, (pairs, lanes), 1) - NBR * ORB
    pair = lax.broadcasted_iota(jnp.int32, (pairs, lanes), 0)
    behind = jnp.dot(
        weight_rows[...].astype(jnp.bfloat16), (at == pair).astype(jnp.bfloat16), preferred_element_type=jnp.float32)
    for atom in range(atoms):
        block = flat[:, atom * lanes:(atom + 1) * lanes]
        mats_in[atom * 16:(atom + 1) * 16, :] = (block + behind if atom == 0 else block).astype(jnp.bfloat16)


def wire_kernel(inner, layers, side, sent, coupling_ref, weight_ref, near_ref, shift_ref, back_ref,
                padded, weight_rows, mats_in,
                landed, mats, weights, near, shifts, near_at, shift_at, pick_q, pick_r,
                out_ref, green, spread_q, spread_r, both, toeplitz, bands, stage,
                slot_send, slot_recv, relay_send, relay_recv, table_send, table_recv, back_send, back_recv, local_sem):
    slots, pieces, local_e, width = landed.shape
    mine = slots - 2
    chunks = sent.shape[0]
    rows_e = pieces * local_e
    late = rows_e - WINDOW
    me, slab = lax.axis_index("energy"), lax.axis_index("slab")
    slabs = lax.axis_size("slab")
    layer, i = lax.div(me, inner), lax.rem(me, inner)
    first_of_layer = layer * inner
    first_atom = slab * (chunks * HALO) + i * (mine * HALO) - HALO
    first, last = i == 0, i == inner - 1
    below, above = layer > 0, layer < layers - 1
    slab_below, slab_above = slab > 0, slab < slabs - 1
    owner, spot = lax.div(me, layers), lax.rem(me, layers)
    barrier = pltpu.get_barrier_semaphore()
    one = lambda flag: jnp.where(flag, 1, 0)

    def hail(device, row):
        pl.semaphore_signal(barrier, inc=1, device_id=(device, row), device_id_type=MESH)

    for step in range(1, inner):
        hail(first_of_layer + partner_of(i, step), slab)

    @pl.when(first & slab_below)
    def _():
        for j in range(inner):
            hail(first_of_layer + j, slab - 1)

    @pl.when(last & slab_above)
    def _():
        for j in range(inner):
            hail(first_of_layer + j, slab + 1)

    pl.when(below)(lambda: hail(me - inner, slab))
    pl.when(above)(lambda: hail(me + inner, slab))
    for j in range(layers):
        pl.when(i * layers + j != me)(lambda: hail(i * layers + j, slab))
    padded[...] = jnp.zeros_like(padded)
    weight_rows[...] = jnp.zeros_like(weight_rows)
    for p in range(ORB):
        padded[p, :ORB, :] = coupling_ref[p].astype(jnp.float32)
    weight_rows[:BAND, :] = weight_ref[:, 0, :]
    table_tall(padded, weight_rows, mats_in)

    tables = ((mats_in, mats), (near_ref, near), (shift_ref, shifts))

    @pl.when(owner == i)
    def _():
        for src, dst in tables:
            dst[spot] = src[...]

    pl.semaphore_wait(
        barrier, inner - 1 + one(slab_above) + one(slab_below) + one(above) + one(below) + layers - one(owner == i))

    def table(number, j, at, to):
        src, dst = tables[number]
        return pltpu.make_async_remote_copy(
            src_ref=src, dst_ref=dst.at[at], send_sem=table_send.at[number, j], recv_sem=table_recv.at[number, at],
            device_id=(to, slab), device_id_type=MESH)

    def outgoing(slot, step):
        to = partner_of(i, step)
        row = slab + one((slot == 0) & (to == 0)) - one((slot == slots - 1) & (to == inner - 1))
        return pltpu.make_async_remote_copy(
            src_ref=sent.at[lax.rem(to * mine + slot - 1 + chunks, chunks)], dst_ref=landed.at[slot, side + i],
            send_sem=slot_send.at[slot, step], recv_sem=slot_recv.at[slot, step],
            device_id=(first_of_layer + to, row), device_id_type=MESH)

    def incoming(slot, step):
        source = partner_of(i, step)
        return pltpu.make_async_remote_copy(
            src_ref=sent.at[0], dst_ref=landed.at[slot, side + source],
            send_sem=slot_send.at[slot, step], recv_sem=slot_recv.at[slot, step],
            device_id=(first_of_layer + source, slab), device_id_type=MESH)

    def leaves(slot, step):
        to = partner_of(i, step)
        real = ((slot > 0) | (to > 0) | slab_above) & ((slot < slots - 1) | (to < inner - 1) | slab_below)
        if step:
            return real
        return real & (((slot == 0) & first) | ((slot == slots - 1) & last))

    def comes(slot, step):
        real = ((slot > 0) | (i > 0) | slab_below) & ((slot < slots - 1) | (i < inner - 1) | slab_above)
        if step:
            return real
        return real & (((slot == 0) & first) | ((slot == slots - 1) & last))

    def send_slot(slot, carry):
        for step in range(inner):
            pl.when(leaves(slot, step))(lambda: outgoing(slot, step).start())
        return carry

    for j in range(layers):
        to = j * inner + owner

        @pl.when(to != me)
        def _():
            for number in range(3):
                table(number, j, spot, to).start()

    lax.fori_loop(0, 3, send_slot, 0)

    landed[pl.ds(1, mine), side + i] = sent[pl.ds(i * mine, mine)]

    @pl.when(i > 0)
    def _():
        landed[0, side + i] = sent[lax.rem(i * mine - 1 + chunks, chunks)]

    @pl.when(i < inner - 1)
    def _():
        landed[slots - 1, side + i] = sent[lax.rem(i * mine + mine, chunks)]

    @pl.when(first & jnp.logical_not(slab_below))
    def _():
        landed[0, side:side + inner] = jnp.zeros((inner, local_e, width), landed.dtype)

    @pl.when(last & jnp.logical_not(slab_above))
    def _():
        landed[slots - 1, side:side + inner] = jnp.zeros((inner, local_e, width), landed.dtype)

    def clear(start):
        landed[:, start:start + side] = jnp.zeros((slots, side, local_e, width), landed.dtype)

    pl.when(jnp.logical_not(below))(lambda: clear(0))
    pl.when(jnp.logical_not(above))(lambda: clear(side + inner))

    wide = NBR * PAIR
    lane = lax.broadcasted_iota(jnp.int32, (8, wide), 1)
    key_q = (lane // ORB)[:1]
    key_r = (lane // PAIR * ORB + lane % ORB)[:1]
    row = lax.broadcasted_iota(jnp.int32, (NBR * ORB, wide), 0)
    pick_q[...] = (row == key_q).astype(jnp.bfloat16)
    pick_r[...] = (row == key_r).astype(jnp.bfloat16)

    def relay(way, slot):
        start, into = (inner, 0) if way == 0 else (side, side + inner)
        return pltpu.make_async_remote_copy(
            src_ref=landed.at[slot, start:start + side], dst_ref=landed.at[slot, into:into + side],
            send_sem=relay_send.at[way, slot], recv_sem=relay_recv.at[way, slot],
            device_id=(me + inner if way == 0 else me - inner, slab), device_id_type=MESH)

    def relayed(way, slot):
        into = 0 if way == 0 else side + inner
        return pltpu.make_async_remote_copy(
            src_ref=landed.at[slot, into:into + side], dst_ref=landed.at[slot, into:into + side],
            send_sem=relay_send.at[way, slot], recv_sem=relay_recv.at[way, slot],
            device_id=(me - inner if way == 0 else me + inner, slab), device_id_type=MESH)

    def pass_on(slot):
        for step in range(inner):
            pl.when(comes(slot, step))(lambda: incoming(slot, step).wait_recv())
        pl.when(above)(lambda: relay(0, slot).start())
        pl.when(below)(lambda: relay(1, slot).start())

    for j in range(layers):
        @pl.when(i * layers + j != me)
        def _():
            for number in range(3):
                table(number, j, j, me).wait_recv()
    to_scalars = (pltpu.make_async_copy(near, near_at, local_sem.at[0]),
                  pltpu.make_async_copy(shifts, shift_at, local_sem.at[1]))
    for copy in to_scalars:
        copy.start()
    lane_of = lax.broadcasted_iota(jnp.int32, (16, WINDOW), 1)
    row_of = lax.broadcasted_iota(jnp.int32, (16, WINDOW), 0)
    place = ((lane_of + row_of == BAND - 1) & (row_of < BAND)).astype(jnp.bfloat16)
    count_pairs = mats.shape[2] - NBR * ORB
    for j in range(layers):
        column = lax.dot_general(
            eye(count_pairs), mats[j, :16, NBR * ORB:], NT, preferred_element_type=jnp.float32).astype(jnp.bfloat16)
        weights[j] = jnp.dot(column, place, preferred_element_type=jnp.float32)

    count = mats.shape[0] * mats.shape[1]
    matrices = mats[...].reshape(count, mats.shape[2])[:, :NBR * ORB]
    spread_q[...] = jnp.dot(matrices, pick_q[...], preferred_element_type=jnp.float32)
    pass_on(0)
    send_slot(3, 0)
    spread_r[...] = jnp.dot(matrices, pick_r[...], preferred_element_type=jnp.float32)
    for copy in to_scalars:
        copy.wait()
    pass_on(1)
    send_slot(4, 0)

    sub = lax.broadcasted_iota(jnp.int32, (8, WINDOW), 0)
    left_half = lax.broadcasted_iota(jnp.int32, (WINDOW, WINDOW), 1) < SPAN
    low_rows = lax.broadcasted_iota(jnp.int32, (8, wide), 0) < 4
    batch = HALO
    zero = jnp.zeros((16, WINDOW), jnp.bfloat16)

    def window_of(m, index):
        shift = shift_at[m, 0, index]
        return shift, jnp.where(shift >= 0, 1, 0)

    def prepare(h, carry):
        m = lax.div(h, HALO // batch)
        tiles = []
        first_pair = h * batch * NBR
        for k in range(batch * NBR):
            index = lax.rem(h * batch, HALO) * NBR + k
            shift, later = window_of(m, index)
            base = shift + side * local_e - BAND // 2 - later * late
            weight = weights[m, pl.ds(index, 1), :]
            tiles.append(pltpu.roll(jnp.broadcast_to(weight, (8, WINDOW)), WINDOW - BAND + 1 - base, 1))
        for step in (1, 2, 4):
            tiles = [jnp.where((sub & step) != 0, pltpu.roll(tile, step, 1), tile) for tile in tiles]
        tiles = [jnp.concatenate([tile, pltpu.roll(tile, 8, 1)], axis=0).astype(jnp.bfloat16) for tile in tiles]
        for b in range(WINDOW // 16):
            for k in range(batch * NBR):
                tile = pltpu.roll(tiles[k], 16 * b, 1) if b else tiles[k]
                toeplitz[first_pair + k, 16 * b:16 * b + 16] = jnp.where(left_half[:16], tile, zero)
                low = WINDOW + (16 * b - SPAN) % WINDOW
                toeplitz[first_pair + k, low:low + 16] = jnp.where(left_half[:16], zero, tile)
        for a in range(batch):
            atom = h * batch + a
            right = spread_r[pl.ds(pl.multiple_of(atom * 16, 16), 16), :]
            rights = (right[:8], jnp.concatenate([right[8:12], right[:4]], axis=0), right[4:12])
            for four in range(ORB // 4):
                rows = []
                for half in range(2):
                    p = four * 4 + half * 2
                    q0 = spread_q[pl.ds(atom * 16 + p, 1), :]
                    q1 = spread_q[pl.ds(atom * 16 + p + 1, 1), :]
                    rows += [q0 * rights[0], jnp.where(low_rows, q0, q1) * rights[1], q1 * rights[2]]
                both[atom, four * 48:(four + 1) * 48, :] = jnp.concatenate(rows, axis=0).astype(jnp.bfloat16)


        pass_on(h + 2)
        pl.when(h == 0)(lambda: [send_slot(5, 0), None][1])
        return carry

    steps = mine * HALO // batch
    assert steps == slots - 2
    lax.fori_loop(0, steps, prepare, 0)

    unit = eye(128)

    def turn(slot, carry):
        pl.when(below)(lambda: relayed(0, slot).wait_recv())
        pl.when(above)(lambda: relayed(1, slot).wait_recv())
        if local_e % 16:
            for piece in range(pieces):
                stage[piece * local_e:(piece + 1) * local_e, :] = landed[slot, piece].astype(jnp.float32)
            tall = stage[...].astype(jnp.bfloat16)
        else:
            tall = landed[slot].reshape(rows_e, width)
        two = jnp.concatenate([tall[:WINDOW], tall[late:]], axis=0)
        turned = jnp.concatenate([
            lax.dot_general(unit, two[:, j * 128:(j + 1) * 128], NT, preferred_element_type=jnp.float32).astype(
                jnp.bfloat16) for j in range(width // 128)], axis=0)
        for atom in range(HALO):
            for c in range(2):
                start = (2 * atom + c) * PAIR
                for window in range(2):
                    green[window, slot * HALO + atom, :, c * WINDOW:(c + 1) * WINDOW] = (
                        turned[start:start + PAIR, window * WINDOW:(window + 1) * WINDOW])
        return carry

    lax.fori_loop(0, 2, turn, 0)

    def share(step, m, at):
        to = partner_of(i, step)
        return pltpu.make_async_remote_copy(
            src_ref=out_ref.at[to, m], dst_ref=back_ref.at[at * mine + m],
            send_sem=back_send.at[step, m], recv_sem=back_recv.at[step, m],
            device_id=(first_of_layer + to, slab), device_id_type=MESH)

    def chunk(m, carry):
        turn(m + 2, 0)
        for a in range(HALO):
            for k in range(NBR):
                index = a * NBR + k
                later = window_of(m, index)[1]
                partner = jnp.clip(near_at[m, 0, index] - first_atom, 0, slots * HALO - 1)
                banded = jnp.dot(
                    green[later, partner], toeplitz[m * HALO * NBR + index], preferred_element_type=jnp.float32)
                bands[a, k * PAIR:(k + 1) * PAIR, :] = banded.astype(jnp.bfloat16)
        parts = []
        totals = [jnp.dot(both[m * HALO + a], bands[a], preferred_element_type=jnp.float32) for a in range(HALO)]
        for total in totals:
            turned = lax.dot_general(unit, total.astype(jnp.bfloat16), NT, preferred_element_type=jnp.float32)
            turned = turned.astype(jnp.bfloat16)
            parts += [turned[:SPAN], turned[SPAN:]]
        whole = jnp.concatenate(parts, axis=1)
        for d in range(inner):
            out_ref[d, m] = whole[d * local_e:(d + 1) * local_e]
        for step in range(1, inner):
            share(step, m, i).start()
        back_ref[i * mine + m] = out_ref[i, m]
        return carry

    lax.fori_loop(0, mine, chunk, 0)

    for j in range(layers):
        @pl.when(j * inner + owner != me)
        def _():
            for number in range(3):
                table(number, j, j, me).wait_send()

    def sent_slot(slot, carry):
        for step in range(inner):
            pl.when(leaves(slot, step))(lambda: outgoing(slot, step).wait_send())
        pl.when(above)(lambda: relay(0, slot).wait_send())
        pl.when(below)(lambda: relay(1, slot).wait_send())
        return carry

    lax.fori_loop(0, slots, sent_slot, 0)

    def finish(m, carry):
        for step in range(1, inner):
            share(step, m, partner_of(i, step)).wait_recv()
            share(step, m, i).wait_send()
        return carry

    lax.fori_loop(0, mine, finish, 0)


def on_device(green_blocks, couplings, band_weights, neighbours, shifts):
    groups = lax.axis_size("energy")
    local_e, slab_count = green_blocks.shape[3:]
    per_dev = slab_count // groups
    width = per_dev * BLOCK
    pairs = per_dev * NBR
    lanes = NBR * ORB + pairs
    inner = SPAN // local_e
    layers = groups // inner
    side = pl.cdiv(REACH, local_e)
    pieces = inner + 2 * side
    mine = groups // inner
    slots = mine + 2
    assert per_dev == HALO and side <= inner and pieces * local_e >= WINDOW
    vmem = pl.BlockSpec(memory_space=pltpu.VMEM)
    smem = pl.BlockSpec(memory_space=pltpu.SMEM)
    blocks = jax.ShapeDtypeStruct((groups, local_e, width), jnp.bfloat16)
    wide = pltpu.VMEM((pl.cdiv(slab_count, 128), BLOCK * local_e, 128), jnp.float32)
    packed = pltpu.VMEM((width // 128, local_e * groups, 128), jnp.float32)
    room = pltpu.CompilerParams(vmem_limit_bytes=32 * 1024 * 1024)

    sent = pl.pallas_call(
        functools.partial(pack_kernel, groups, per_dev),
        out_shape=blocks, in_specs=[vmem], out_specs=vmem,
        scratch_shapes=[wide, packed], compiler_params=room,
    )(green_blocks.reshape(BLOCK * local_e, slab_count))
    back = pl.pallas_call(
        functools.partial(wire_kernel, inner, layers, side),
        out_shape=blocks,
        in_specs=[vmem] * 5,
        out_specs=vmem,
        scratch_shapes=[
            pltpu.VMEM((ORB, 16, pairs), jnp.float32), pltpu.VMEM((16, pairs), jnp.float32),
            pltpu.VMEM((per_dev * 16, lanes), jnp.bfloat16),
            pltpu.VMEM((slots, pieces, local_e, width), jnp.bfloat16),
            pltpu.VMEM((layers, per_dev * 16, lanes), jnp.bfloat16),
            pltpu.VMEM((layers, pairs, WINDOW), jnp.float32),
            pltpu.VMEM((layers, 1, pairs), jnp.int32),
            pltpu.VMEM((layers, 1, pairs), jnp.int32),
            pltpu.SMEM((layers, 1, pairs), jnp.int32),
            pltpu.SMEM((layers, 1, pairs), jnp.int32),
            pltpu.VMEM((NBR * ORB, NBR * PAIR), jnp.bfloat16), pltpu.VMEM((NBR * ORB, NBR * PAIR), jnp.bfloat16),
            pltpu.VMEM((inner, mine, local_e, width), jnp.bfloat16),
            pltpu.VMEM((2, slots * HALO, PAIR, 2 * WINDOW), jnp.bfloat16),
            pltpu.VMEM((mine * HALO * 16, NBR * PAIR), jnp.float32),
            pltpu.VMEM((mine * HALO * 16, NBR * PAIR), jnp.float32),
            pltpu.VMEM((mine * HALO, PAIR, NBR * PAIR), jnp.bfloat16),
            pltpu.VMEM((mine * HALO * NBR, 2 * WINDOW, WINDOW), jnp.bfloat16),
            pltpu.VMEM((HALO, NBR * PAIR, WINDOW), jnp.bfloat16),
            pltpu.VMEM((pieces * local_e if local_e % 16 else 8, width), jnp.float32),
            pltpu.SemaphoreType.DMA((slots, inner)), pltpu.SemaphoreType.DMA((slots, inner)),
            pltpu.SemaphoreType.DMA((2, slots)), pltpu.SemaphoreType.DMA((2, slots)),
            pltpu.SemaphoreType.DMA((3, layers)), pltpu.SemaphoreType.DMA((3, layers)),
            pltpu.SemaphoreType.DMA((inner, mine)), pltpu.SemaphoreType.DMA((inner, mine)),
            pltpu.SemaphoreType.DMA((2,)),
        ],
        compiler_params=pltpu.CompilerParams(
            collective_id=0, has_side_effects=True, vmem_limit_bytes=48 * 1024 * 1024),
    )(sent, couplings.reshape(ORB, ORB, pairs), band_weights, neighbours, shifts)
    result = pl.pallas_call(
        functools.partial(unpack_kernel, groups, per_dev),
        out_shape=jax.ShapeDtypeStruct((BLOCK * local_e, slab_count), jnp.bfloat16),
        in_specs=[vmem], out_specs=vmem,
        scratch_shapes=[packed, wide], compiler_params=room,
    )(back)
    return result.reshape(2, ORB, ORB, local_e, slab_count)


def solution(mesh):
    return jax.shard_map(
        on_device,
        mesh=mesh,
        in_specs=(
            P(None, None, None, "energy", "slab"),
            P(None, None, "slab", "energy"),
            P(None, "slab", "energy"),
            P("slab", "energy"),
            P("slab", "energy"),
        ),
        out_specs=P(None, None, None, "energy", "slab"),
        check_vma=False,
    )
```

```python
import functools

import jax
import jax.numpy as jnp
from jax import lax
from jax.experimental import pallas as pl
from jax.experimental.pallas import tpu as pltpu
from jax.sharding import PartitionSpec as P

ORB = 12
NBR = 16
BAND = 9
SHIFT = 32
HALO = 4
BLOCK = 2 * ORB * ORB
PAIR = ORB * ORB
REACH = SHIFT + BAND // 2
SPAN = 64
WINDOW = 128

MESH = pl.DeviceIdType.MESH
NT = (((1,), (1,)), ((), ()))


def order(groups, per_dev):
    count = groups * per_dev
    row = lax.broadcasted_iota(jnp.int32, (count, count), 0)
    atom = lax.broadcasted_iota(jnp.int32, (count, count), 1)
    return (atom == (row % groups) * per_dev + row // groups).astype(jnp.bfloat16)


def eye(count):
    row = lax.broadcasted_iota(jnp.int32, (count, count), 0)
    column = lax.broadcasted_iota(jnp.int32, (count, count), 1)
    return (row == column).astype(jnp.bfloat16)


def partner_of(i, step):
    out, bit = 0, 1
    while bit <= step:
        out = out + bit * lax.rem(lax.div(i, bit) + step // bit, 2)
        bit *= 2
    return lax.div(i, bit) * bit + out if step else i


def pack_kernel(groups, per_dev, x_ref, sent, wide, packed):
    local_e = sent.shape[1]
    tiles = wide.shape[0]
    count = x_ref.shape[1]
    lanes = min(count, 128)
    if lanes < 128:
        wide[...] = jnp.zeros_like(wide)
    for j in range(tiles):
        wide[j, :x_ref.shape[0], :lanes] = x_ref[:, j * 128:j * 128 + lanes].astype(jnp.float32)
    pick = order(groups, per_dev)
    for e in range(local_e):
        rows = jnp.concatenate([wide[j, pl.ds(e, BLOCK, stride=local_e), :] for j in range(tiles)], axis=1)
        rows = rows[:, :count].astype(jnp.bfloat16)
        turned = lax.dot_general(pick, rows, NT, preferred_element_type=jnp.float32)
        flat = jnp.concatenate([turned[i * groups:(i + 1) * groups] for i in range(per_dev)], axis=1)
        for j in range(packed.shape[0]):
            packed[j, pl.ds(e, groups, stride=local_e), :] = flat[:, j * 128:(j + 1) * 128]
    for g in range(groups):
        for j in range(packed.shape[0]):
            sent[g, :, j * 128:(j + 1) * 128] = packed[j, g * local_e:(g + 1) * local_e, :].astype(jnp.bfloat16)


def unpack_kernel(groups, per_dev, landed, out_ref, wide, tall):
    local_e = landed.shape[1]
    lanes = min(out_ref.shape[1], 128)
    for g in range(groups):
        for j in range(wide.shape[0]):
            wide[j, g * local_e:(g + 1) * local_e, :] = landed[g, :, j * 128:(j + 1) * 128].astype(jnp.float32)
    pick = order(groups, per_dev)
    some = min(4, local_e)
    for start in range(0, local_e, some):
        stacks = []
        for e in range(start, start + some):
            rows = jnp.concatenate(
                [wide[j, pl.ds(e, groups, stride=local_e), :] for j in range(wide.shape[0])], axis=1)
            stacks.append(jnp.concatenate(
                [rows[:, i * BLOCK:(i + 1) * BLOCK] for i in range(per_dev)], axis=0).astype(jnp.bfloat16))
        turns = [jnp.dot(stack.T, pick, preferred_element_type=jnp.float32) for stack in stacks]
        for e, turned in zip(range(start, start + some), turns):
            if lanes < 128:
                turned = jnp.concatenate([turned, jnp.zeros((BLOCK, 128 - lanes), jnp.float32)], axis=1)
            for j in range(tall.shape[0]):
                tall[j, pl.ds(e, BLOCK, stride=local_e), :] = turned[:, j * 128:(j + 1) * 128]
    for j in range(tall.shape[0]):
        out_ref[:, j * 128:j * 128 + lanes] = tall[j, :out_ref.shape[0], :lanes].astype(jnp.bfloat16)


def table_tall(padded, weight_rows, mats_in):
    pairs = padded.shape[2]
    atoms, lanes = pairs // NBR, mats_in.shape[1]
    wide = atoms * lanes
    tall = padded[...].reshape(ORB * 16, pairs).astype(jnp.bfloat16)
    lane = lax.broadcasted_iota(jnp.int32, (8, wide), 1)[:1]
    inside = lane % lanes
    pair_of = jnp.where(inside < NBR * ORB, lane // lanes * NBR + inside // ORB, -1)
    row = lax.broadcasted_iota(jnp.int32, (pairs, wide), 0)
    spread = jnp.dot(tall, (row == pair_of).astype(jnp.bfloat16), preferred_element_type=jnp.float32)
    row = lax.broadcasted_iota(jnp.int32, (ORB * 16, wide), 0) % 16
    spread = jnp.where(row == inside % ORB, spread, 0.0).astype(jnp.bfloat16)
    p = lax.broadcasted_iota(jnp.int32, (16, ORB * 16), 0)
    of = lax.broadcasted_iota(jnp.int32, (16, ORB * 16), 1) // 16
    flat = jnp.dot((p == of).astype(jnp.bfloat16), spread, preferred_element_type=jnp.float32)
    at = lax.broadcasted_iota(jnp.int32, (pairs, lanes), 1) - NBR * ORB
    pair = lax.broadcasted_iota(jnp.int32, (pairs, lanes), 0)
    behind = jnp.dot(
        weight_rows[...].astype(jnp.bfloat16), (at == pair).astype(jnp.bfloat16), preferred_element_type=jnp.float32)
    for atom in range(atoms):
        block = flat[:, atom * lanes:(atom + 1) * lanes]
        mats_in[atom * 16:(atom + 1) * 16, :] = (block + behind if atom == 0 else block).astype(jnp.bfloat16)


def wire_kernel(inner, layers, side, sent, coupling_ref, weight_ref, near_ref, shift_ref, back_ref,
                padded, weight_rows, mats_in,
                landed, mats, weights, near, shifts, near_at, shift_at, pick_q, pick_r,
                out_ref, green, spread_q, spread_r, both, toeplitz, bands, stage,
                slot_send, slot_recv, relay_send, relay_recv, table_send, table_recv, back_send, back_recv, local_sem):
    slots, pieces, local_e, width = landed.shape
    mine = slots - 2
    chunks = sent.shape[0]
    rows_e = pieces * local_e
    late = rows_e - WINDOW
    me, slab = lax.axis_index("energy"), lax.axis_index("slab")
    slabs = lax.axis_size("slab")
    layer, i = lax.div(me, inner), lax.rem(me, inner)
    first_of_layer = layer * inner
    first_atom = slab * (chunks * HALO) + i * (mine * HALO) - HALO
    first, last = i == 0, i == inner - 1
    below, above = layer > 0, layer < layers - 1
    slab_below, slab_above = slab > 0, slab < slabs - 1
    owner, spot = lax.div(me, layers), lax.rem(me, layers)
    barrier = pltpu.get_barrier_semaphore()
    one = lambda flag: jnp.where(flag, 1, 0)

    def hail(device, row):
        pl.semaphore_signal(barrier, inc=1, device_id=(device, row), device_id_type=MESH)

    for step in range(1, inner):
        hail(first_of_layer + partner_of(i, step), slab)

    @pl.when(first & slab_below)
    def _():
        for j in range(inner):
            hail(first_of_layer + j, slab - 1)

    @pl.when(last & slab_above)
    def _():
        for j in range(inner):
            hail(first_of_layer + j, slab + 1)

    pl.when(below)(lambda: hail(me - inner, slab))
    pl.when(above)(lambda: hail(me + inner, slab))
    for j in range(layers):
        pl.when(i * layers + j != me)(lambda: hail(i * layers + j, slab))
    padded[...] = jnp.zeros_like(padded)
    weight_rows[...] = jnp.zeros_like(weight_rows)
    for p in range(ORB):
        padded[p, :ORB, :] = coupling_ref[p].astype(jnp.float32)
    weight_rows[:BAND, :] = weight_ref[:, 0, :]
    table_tall(padded, weight_rows, mats_in)

    tables = ((mats_in, mats), (near_ref, near), (shift_ref, shifts))

    @pl.when(owner == i)
    def _():
        for src, dst in tables:
            dst[spot] = src[...]

    pl.semaphore_wait(
        barrier, inner - 1 + one(slab_above) + one(slab_below) + one(above) + one(below) + layers - one(owner == i))

    def table(number, j, at, to):
        src, dst = tables[number]
        return pltpu.make_async_remote_copy(
            src_ref=src, dst_ref=dst.at[at], send_sem=table_send.at[number, j], recv_sem=table_recv.at[number, at],
            device_id=(to, slab), device_id_type=MESH)

    def outgoing(slot, step):
        to = partner_of(i, step)
        row = slab + one((slot == 0) & (to == 0)) - one((slot == slots - 1) & (to == inner - 1))
        return pltpu.make_async_remote_copy(
            src_ref=sent.at[lax.rem(to * mine + slot - 1 + chunks, chunks)], dst_ref=landed.at[slot, side + i],
            send_sem=slot_send.at[slot, step], recv_sem=slot_recv.at[slot, step],
            device_id=(first_of_layer + to, row), device_id_type=MESH)

    def incoming(slot, step):
        source = partner_of(i, step)
        return pltpu.make_async_remote_copy(
            src_ref=sent.at[0], dst_ref=landed.at[slot, side + source],
            send_sem=slot_send.at[slot, step], recv_sem=slot_recv.at[slot, step],
            device_id=(first_of_layer + source, slab), device_id_type=MESH)

    def leaves(slot, step):
        to = partner_of(i, step)
        real = ((slot > 0) | (to > 0) | slab_above) & ((slot < slots - 1) | (to < inner - 1) | slab_below)
        if step:
            return real
        return real & (((slot == 0) & first) | ((slot == slots - 1) & last))

    def comes(slot, step):
        real = ((slot > 0) | (i > 0) | slab_below) & ((slot < slots - 1) | (i < inner - 1) | slab_above)
        if step:
            return real
        return real & (((slot == 0) & first) | ((slot == slots - 1) & last))

    def send_slot(slot, carry):
        for step in range(inner):
            pl.when(leaves(slot, step))(lambda: outgoing(slot, step).start())
        return carry

    for j in range(layers):
        to = j * inner + owner

        @pl.when(to != me)
        def _():
            for number in range(3):
                table(number, j, spot, to).start()

    lax.fori_loop(0, 3, send_slot, 0)

    landed[pl.ds(1, mine), side + i] = sent[pl.ds(i * mine, mine)]

    @pl.when(i > 0)
    def _():
        landed[0, side + i] = sent[lax.rem(i * mine - 1 + chunks, chunks)]

    @pl.when(i < inner - 1)
    def _():
        landed[slots - 1, side + i] = sent[lax.rem(i * mine + mine, chunks)]

    @pl.when(first & jnp.logical_not(slab_below))
    def _():
        landed[0, side:side + inner] = jnp.zeros((inner, local_e, width), landed.dtype)

    @pl.when(last & jnp.logical_not(slab_above))
    def _():
        landed[slots - 1, side:side + inner] = jnp.zeros((inner, local_e, width), landed.dtype)

    def clear(start):
        landed[:, start:start + side] = jnp.zeros((slots, side, local_e, width), landed.dtype)

    pl.when(jnp.logical_not(below))(lambda: clear(0))
    pl.when(jnp.logical_not(above))(lambda: clear(side + inner))

    wide = NBR * PAIR
    lane = lax.broadcasted_iota(jnp.int32, (8, wide), 1)
    key_q = (lane // ORB)[:1]
    key_r = (lane // PAIR * ORB + lane % ORB)[:1]
    row = lax.broadcasted_iota(jnp.int32, (NBR * ORB, wide), 0)
    pick_q[...] = (row == key_q).astype(jnp.bfloat16)
    pick_r[...] = (row == key_r).astype(jnp.bfloat16)

    def relay(way, slot):
        start, into = (inner, 0) if way == 0 else (side, side + inner)
        return pltpu.make_async_remote_copy(
            src_ref=landed.at[slot, start:start + side], dst_ref=landed.at[slot, into:into + side],
            send_sem=relay_send.at[way, slot], recv_sem=relay_recv.at[way, slot],
            device_id=(me + inner if way == 0 else me - inner, slab), device_id_type=MESH)

    def relayed(way, slot):
        into = 0 if way == 0 else side + inner
        return pltpu.make_async_remote_copy(
            src_ref=landed.at[slot, into:into + side], dst_ref=landed.at[slot, into:into + side],
            send_sem=relay_send.at[way, slot], recv_sem=relay_recv.at[way, slot],
            device_id=(me - inner if way == 0 else me + inner, slab), device_id_type=MESH)

    def pass_on(slot):
        for step in range(inner):
            pl.when(comes(slot, step))(lambda: incoming(slot, step).wait_recv())
        pl.when(above)(lambda: relay(0, slot).start())
        pl.when(below)(lambda: relay(1, slot).start())

    for j in range(layers):
        @pl.when(i * layers + j != me)
        def _():
            for number in range(3):
                table(number, j, j, me).wait_recv()
    to_scalars = (pltpu.make_async_copy(near, near_at, local_sem.at[0]),
                  pltpu.make_async_copy(shifts, shift_at, local_sem.at[1]))
    for copy in to_scalars:
        copy.start()
    lane_of = lax.broadcasted_iota(jnp.int32, (16, WINDOW), 1)
    row_of = lax.broadcasted_iota(jnp.int32, (16, WINDOW), 0)
    place = ((lane_of + row_of == BAND - 1) & (row_of < BAND)).astype(jnp.bfloat16)
    count_pairs = mats.shape[2] - NBR * ORB
    for j in range(layers):
        column = lax.dot_general(
            eye(count_pairs), mats[j, :16, NBR * ORB:], NT, preferred_element_type=jnp.float32).astype(jnp.bfloat16)
        weights[j] = jnp.dot(column, place, preferred_element_type=jnp.float32)

    count = mats.shape[0] * mats.shape[1]
    matrices = mats[...].reshape(count, mats.shape[2])[:, :NBR * ORB]
    spread_q[...] = jnp.dot(matrices, pick_q[...], preferred_element_type=jnp.float32)
    pass_on(0)
    send_slot(3, 0)
    spread_r[...] = jnp.dot(matrices, pick_r[...], preferred_element_type=jnp.float32)
    for copy in to_scalars:
        copy.wait()
    pass_on(1)
    send_slot(4, 0)

    sub = lax.broadcasted_iota(jnp.int32, (8, WINDOW), 0)
    left_half = lax.broadcasted_iota(jnp.int32, (WINDOW, WINDOW), 1) < SPAN
    low_rows = lax.broadcasted_iota(jnp.int32, (8, wide), 0) < 4
    batch = HALO
    zero = jnp.zeros((16, WINDOW), jnp.bfloat16)

    def window_of(m, index):
        shift = shift_at[m, 0, index]
        return shift, jnp.where(shift >= 0, 1, 0)

    def prepare(h, carry):
        m = lax.div(h, HALO // batch)
        tiles = []
        first_pair = h * batch * NBR
        for k in range(batch * NBR):
            index = lax.rem(h * batch, HALO) * NBR + k
            shift, later = window_of(m, index)
            base = shift + side * local_e - BAND // 2 - later * late
            weight = weights[m, pl.ds(index, 1), :]
            tiles.append(pltpu.roll(jnp.broadcast_to(weight, (8, WINDOW)), WINDOW - BAND + 1 - base, 1))
        for step in (1, 2, 4):
            tiles = [jnp.where((sub & step) != 0, pltpu.roll(tile, step, 1), tile) for tile in tiles]
        tiles = [jnp.concatenate([tile, pltpu.roll(tile, 8, 1)], axis=0).astype(jnp.bfloat16) for tile in tiles]
        for b in range(WINDOW // 16):
            for k in range(batch * NBR):
                tile = pltpu.roll(tiles[k], 16 * b, 1) if b else tiles[k]
                toeplitz[first_pair + k, 16 * b:16 * b + 16] = jnp.where(left_half[:16], tile, zero)
                low = WINDOW + (16 * b - SPAN) % WINDOW
                toeplitz[first_pair + k, low:low + 16] = jnp.where(left_half[:16], zero, tile)
        for a in range(batch):
            atom = h * batch + a
            right = spread_r[pl.ds(pl.multiple_of(atom * 16, 16), 16), :]
            rights = (right[:8], jnp.concatenate([right[8:12], right[:4]], axis=0), right[4:12])
            for four in range(ORB // 4):
                rows = []
                for half in range(2):
                    p = four * 4 + half * 2
                    q0 = spread_q[pl.ds(atom * 16 + p, 1), :]
                    q1 = spread_q[pl.ds(atom * 16 + p + 1, 1), :]
                    rows += [q0 * rights[0], jnp.where(low_rows, q0, q1) * rights[1], q1 * rights[2]]
                both[atom, four * 48:(four + 1) * 48, :] = jnp.concatenate(rows, axis=0).astype(jnp.bfloat16)


        pass_on(h + 2)
        pl.when(h == 0)(lambda: [send_slot(5, 0), None][1])
        return carry

    steps = mine * HALO // batch
    assert steps == slots - 2
    lax.fori_loop(0, steps, prepare, 0)

    unit = eye(128)

    def turn(slot, carry):
        pl.when(below)(lambda: relayed(0, slot).wait_recv())
        pl.when(above)(lambda: relayed(1, slot).wait_recv())
        if local_e % 16:
            for piece in range(pieces):
                stage[piece * local_e:(piece + 1) * local_e, :] = landed[slot, piece].astype(jnp.float32)
            tall = stage[...].astype(jnp.bfloat16)
        else:
            tall = landed[slot].reshape(rows_e, width)
        two = jnp.concatenate([tall[:WINDOW], tall[late:]], axis=0)
        turned = jnp.concatenate([
            lax.dot_general(unit, two[:, j * 128:(j + 1) * 128], NT, preferred_element_type=jnp.float32).astype(
                jnp.bfloat16) for j in range(width // 128)], axis=0)
        for atom in range(HALO):
            for c in range(2):
                start = (2 * atom + c) * PAIR
                for window in range(2):
                    green[window, slot * HALO + atom, :, c * WINDOW:(c + 1) * WINDOW] = (
                        turned[start:start + PAIR, window * WINDOW:(window + 1) * WINDOW])
        return carry

    lax.fori_loop(0, 2, turn, 0)

    def share(step, m, at):
        to = partner_of(i, step)
        return pltpu.make_async_remote_copy(
            src_ref=out_ref.at[to, m], dst_ref=back_ref.at[at * mine + m],
            send_sem=back_send.at[step, m], recv_sem=back_recv.at[step, m],
            device_id=(first_of_layer + to, slab), device_id_type=MESH)

    def chunk(m, carry):
        turn(m + 2, 0)
        totals = []
        for a in range(HALO):
            for k in range(NBR):
                index = a * NBR + k
                later = window_of(m, index)[1]
                partner = jnp.clip(near_at[m, 0, index] - first_atom, 0, slots * HALO - 1)
                banded = jnp.dot(
                    green[later, partner], toeplitz[m * HALO * NBR + index], preferred_element_type=jnp.float32)
                bands[a, k * PAIR:(k + 1) * PAIR, :] = banded.astype(jnp.bfloat16)
            if a % 2:
                totals += [jnp.dot(both[m * HALO + b], bands[b], preferred_element_type=jnp.float32) for b in (a - 1, a)]
        parts = []
        for total in totals:
            turned = lax.dot_general(unit, total.astype(jnp.bfloat16), NT, preferred_element_type=jnp.float32)
            turned = turned.astype(jnp.bfloat16)
            parts += [turned[:SPAN], turned[SPAN:]]
        whole = jnp.concatenate(parts, axis=1)
        for d in range(inner):
            out_ref[d, m] = whole[d * local_e:(d + 1) * local_e]
        for step in range(1, inner):
            share(step, m, i).start()
        back_ref[i * mine + m] = out_ref[i, m]
        return carry

    lax.fori_loop(0, mine, chunk, 0)

    for j in range(layers):
        @pl.when(j * inner + owner != me)
        def _():
            for number in range(3):
                table(number, j, j, me).wait_send()

    def sent_slot(slot, carry):
        for step in range(inner):
            pl.when(leaves(slot, step))(lambda: outgoing(slot, step).wait_send())
        pl.when(above)(lambda: relay(0, slot).wait_send())
        pl.when(below)(lambda: relay(1, slot).wait_send())
        return carry

    lax.fori_loop(0, slots, sent_slot, 0)

    def finish(m, carry):
        for step in range(1, inner):
            share(step, m, partner_of(i, step)).wait_recv()
            share(step, m, i).wait_send()
        return carry

    lax.fori_loop(0, mine, finish, 0)


def on_device(green_blocks, couplings, band_weights, neighbours, shifts):
    groups = lax.axis_size("energy")
    local_e, slab_count = green_blocks.shape[3:]
    per_dev = slab_count // groups
    width = per_dev * BLOCK
    pairs = per_dev * NBR
    lanes = NBR * ORB + pairs
    inner = SPAN // local_e
    layers = groups // inner
    side = pl.cdiv(REACH, local_e)
    pieces = inner + 2 * side
    mine = groups // inner
    slots = mine + 2
    assert per_dev == HALO and side <= inner and pieces * local_e >= WINDOW
    vmem = pl.BlockSpec(memory_space=pltpu.VMEM)
    smem = pl.BlockSpec(memory_space=pltpu.SMEM)
    blocks = jax.ShapeDtypeStruct((groups, local_e, width), jnp.bfloat16)
    wide = pltpu.VMEM((pl.cdiv(slab_count, 128), BLOCK * local_e, 128), jnp.float32)
    packed = pltpu.VMEM((width // 128, local_e * groups, 128), jnp.float32)
    room = pltpu.CompilerParams(vmem_limit_bytes=32 * 1024 * 1024)

    sent = pl.pallas_call(
        functools.partial(pack_kernel, groups, per_dev),
        out_shape=blocks, in_specs=[vmem], out_specs=vmem,
        scratch_shapes=[wide, packed], compiler_params=room,
    )(green_blocks.reshape(BLOCK * local_e, slab_count))
    back = pl.pallas_call(
        functools.partial(wire_kernel, inner, layers, side),
        out_shape=blocks,
        in_specs=[vmem] * 5,
        out_specs=vmem,
        scratch_shapes=[
            pltpu.VMEM((ORB, 16, pairs), jnp.float32), pltpu.VMEM((16, pairs), jnp.float32),
            pltpu.VMEM((per_dev * 16, lanes), jnp.bfloat16),
            pltpu.VMEM((slots, pieces, local_e, width), jnp.bfloat16),
            pltpu.VMEM((layers, per_dev * 16, lanes), jnp.bfloat16),
            pltpu.VMEM((layers, pairs, WINDOW), jnp.float32),
            pltpu.VMEM((layers, 1, pairs), jnp.int32),
            pltpu.VMEM((layers, 1, pairs), jnp.int32),
            pltpu.SMEM((layers, 1, pairs), jnp.int32),
            pltpu.SMEM((layers, 1, pairs), jnp.int32),
            pltpu.VMEM((NBR * ORB, NBR * PAIR), jnp.bfloat16), pltpu.VMEM((NBR * ORB, NBR * PAIR), jnp.bfloat16),
            pltpu.VMEM((inner, mine, local_e, width), jnp.bfloat16),
            pltpu.VMEM((2, slots * HALO, PAIR, 2 * WINDOW), jnp.bfloat16),
            pltpu.VMEM((mine * HALO * 16, NBR * PAIR), jnp.float32),
            pltpu.VMEM((mine * HALO * 16, NBR * PAIR), jnp.float32),
            pltpu.VMEM((mine * HALO, PAIR, NBR * PAIR), jnp.bfloat16),
            pltpu.VMEM((mine * HALO * NBR, 2 * WINDOW, WINDOW), jnp.bfloat16),
            pltpu.VMEM((HALO, NBR * PAIR, WINDOW), jnp.bfloat16),
            pltpu.VMEM((pieces * local_e if local_e % 16 else 8, width), jnp.float32),
            pltpu.SemaphoreType.DMA((slots, inner)), pltpu.SemaphoreType.DMA((slots, inner)),
            pltpu.SemaphoreType.DMA((2, slots)), pltpu.SemaphoreType.DMA((2, slots)),
            pltpu.SemaphoreType.DMA((3, layers)), pltpu.SemaphoreType.DMA((3, layers)),
            pltpu.SemaphoreType.DMA((inner, mine)), pltpu.SemaphoreType.DMA((inner, mine)),
            pltpu.SemaphoreType.DMA((2,)),
        ],
        compiler_params=pltpu.CompilerParams(
            collective_id=0, has_side_effects=True, vmem_limit_bytes=48 * 1024 * 1024),
    )(sent, couplings.reshape(ORB, ORB, pairs), band_weights, neighbours, shifts)
    result = pl.pallas_call(
        functools.partial(unpack_kernel, groups, per_dev),
        out_shape=jax.ShapeDtypeStruct((BLOCK * local_e, slab_count), jnp.bfloat16),
        in_specs=[vmem], out_specs=vmem,
        scratch_shapes=[packed, wide], compiler_params=room,
    )(back)
    return result.reshape(2, ORB, ORB, local_e, slab_count)


def solution(mesh):
    return jax.shard_map(
        on_device,
        mesh=mesh,
        in_specs=(
            P(None, None, None, "energy", "slab"),
            P(None, None, "slab", "energy"),
            P(None, "slab", "energy"),
            P("slab", "energy"),
            P("slab", "energy"),
        ),
        out_specs=P(None, None, None, "energy", "slab"),
        check_vma=False,
    )
```
